32 devices in a mesh: groups: 2 (over y), tile: 4 (over z), pass: 2 (over x), row: 2 (over core).
Axes of the slice: x: 2, y: 2, z: 4, core: 2. Of those that a mesh axis runs over, the one named last changes fastest.
Arguments:
- revisits: bfloat16 [32, 8, 64, 1024], P(('groups', 'pass'), ('tile', 'row')), parts along dimension 0, may hold values from -6 to 6
- shifts: int32 [32, 2], P(('groups', 'pass')), parts along dimension 0, may hold values from -32 to 32, as said below
- flags: int32 [32, 8], P('groups', ('tile', 'row')), parts along dimension 0, may hold values from 0 to 1, as said below
- norm1_gain: float32 [64], replicated, may hold values from 0.1 to 1.9
- w_query: bfloat16 [64, 64], replicated, may hold values from -0.75 to 0.75
- w_key: bfloat16 [64, 64], replicated, may hold values from -0.75 to 0.75
- w_value: bfloat16 [64, 64], replicated, may hold values from -0.75 to 0.75
- query_gain: float32 [64], replicated, may hold values from 0.1 to 1.9
- key_gain: float32 [64], replicated, may hold values from 0.1 to 1.9
- w_out: bfloat16 [64, 64], replicated, may hold values from -0.75 to 0.75
- norm2_gain: float32 [64], replicated, may hold values from 0.1 to 1.9
- w_in: bfloat16 [64, 128], replicated, may hold values from -0.75 to 0.75
- w_back: bfloat16 [128, 64], replicated, may hold values from -0.5 to 0.5
- conv_first: bfloat16 [3, 3, 64, 64], replicated, may hold values from -0.75 to 0.75
- conv_second: bfloat16 [3, 3, 64, 9], replicated, may hold values from -0.25 to 0.25
Outputs:
- output: float32 [16, 9, 1024], P(('groups', 'pass'), None, ('tile', 'row')), parts along dimension 0
The draws below stay inside these ranges and needn't reach their ends.
There are 2 independent parts, one for each index of `groups`. The reference program is written for one: setup_inputs(seed, part) draws one part's arguments, and reference() takes and returns one part's arrays. A program takes and returns all parts, laid end to end along the dimension named above; an argument that names none is the same for every part. Nothing has to cross between parts.
Inputs may be any that keep to these rules, and one draw needn't show every extreme that they name: `shifts`: some revisit has row shift 32, some -32, some column shift 32 and some -32. `flags`: every row band has at least one cloud-free revisit.
All inputs are finite; a program needn't handle non-finite values.
Results may differ from the reference program's by a relative error of at most 0.007.
Values may be sent and summed in bfloat16 or wider, within the bound.
No kernel may reach another device: no remote copies, remote signals or barrier semaphores. Data moves between devices by JAX's collectives and lax.ppermute only.
A program may use at most 128 MiB of HBM per device.

```python
import math
import jax
import jax.numpy as jnp
from jax import lax

R = 16
C = 64
HEADS = 4
MLP = 128
OUT = 9
BR = 128
NBANDS = 8
NCOLS = 8
NROWS = 1024


def draw_shifts(key, part):
    first, second = jax.random.split(jax.random.fold_in(key, 11))
    values = jax.random.randint(first, (R, 2), -32, 33)
    picks = jax.random.permutation(second, R)
    values = values.at[picks[0], 0].set(32)
    values = values.at[picks[1], 0].set(-32)
    values = values.at[picks[2], 1].set(32)
    values = values.at[picks[3], 1].set(-32)
    return values.astype(jnp.int32)


def draw_flags(key, part):
    first, second = jax.random.split(jax.random.fold_in(key, 23))
    coins = jax.random.randint(first, (R, NBANDS), 0, 10) < 7
    keeper = jax.random.randint(second, (NBANDS,), 0, R)
    forced = jnp.arange(R)[:, None] == keeper[None, :]
    return (coins | forced).astype(jnp.int32)


def block_levels(key, shape, cuts, smallest, top_value):
    level, own = 1.0, jax.random.fold_in(key, 6)
    for dim, blocks in cuts:
        steps = jnp.exp(jax.random.uniform(jax.random.fold_in(own, dim), (blocks,), jnp.float32, smallest / len(cuts), top_value / len(cuts)))
        level = level * jnp.repeat(steps, shape[dim] // blocks).reshape([-1 if axis == dim else 1 for axis in range(len(shape))])
    return level


def bell_draw(rng, dims, spread, most, shards=(), held_as=jnp.bfloat16):
    level = block_levels(rng, dims, shards, -0.22, 0.18) if shards else 1.0
    array = jax.random.normal(rng, dims, jnp.float32) * spread * level
    return jnp.minimum(jnp.maximum(array, -most), most).astype(held_as)


def setup_inputs(seed: int = 0, part: int = 0) -> dict:
    seeds = jax.random.split(jax.random.key(seed), 16)
    own_keys = jax.random.split(jax.random.fold_in(seeds[15], part), 16)
    return {
        "revisits": bell_draw(own_keys[0], (R, NCOLS, C, NROWS), 1.0, 6.0, ((0, 2), (1, 8))),
        "shifts": draw_shifts(jax.random.fold_in(jax.random.fold_in(seeds[15], part), 71), part),
        "flags": draw_flags(jax.random.fold_in(jax.random.fold_in(seeds[15], part), 71), part),
        "norm1_gain": jnp.clip(1.0 + 0.18 * jax.random.normal(seeds[3], (C,), jnp.float32), 0.1, 1.9),
        "w_query": bell_draw(seeds[4], (C, C), C ** -0.5, 0.75),
        "w_key": bell_draw(seeds[5], (C, C), C ** -0.5, 0.75),
        "w_value": bell_draw(seeds[6], (C, C), C ** -0.5, 0.75),
        "query_gain": jnp.clip(1.0 + 0.18 * jax.random.normal(seeds[7], (C,), jnp.float32), 0.1, 1.9),
        "key_gain": jnp.clip(1.0 + 0.18 * jax.random.normal(seeds[8], (C,), jnp.float32), 0.1, 1.9),
        "w_out": bell_draw(seeds[9], (C, C), C ** -0.5, 0.75),
        "norm2_gain": jnp.clip(1.0 + 0.18 * jax.random.normal(seeds[10], (C,), jnp.float32), 0.1, 1.9),
        "w_in": bell_draw(seeds[11], (C, MLP), C ** -0.5, 0.75),
        "w_back": bell_draw(seeds[12], (MLP, C), MLP ** -0.5, 0.5),
        "conv_first": bell_draw(seeds[13], (3, 3, C, C), C ** -0.5, 0.75),
        "conv_second": bell_draw(seeds[14], (3, 3, C, OUT), (9 * C) ** -0.5, 0.25),
    }


eps = 1e-05
reach = 32

def rounded(values):
    return lax.optimization_barrier(values.astype(jnp.bfloat16)).astype(jnp.float32)

def rms_scale(values, gain):
    mean = lax.optimization_barrier(jnp.mean(values * values, axis=-2, keepdims=True))
    return values * lax.rsqrt(mean + eps) * gain[:, None]

def join_cells(cells_in, mask, norm1_gain, w_query, w_key, w_value, query_gain, key_gain, w_out, norm2_gain, w_in, w_back):
    f32 = jnp.float32
    count, width, chans, rows = cells_in.shape
    cells = cells_in.astype(f32)
    normed = rounded(rms_scale(cells, norm1_gain))
    query = jnp.einsum('rjcy,cd->rjdy', normed, w_query.astype(f32))
    keys = jnp.einsum('rjcy,cd->rjdy', normed, w_key.astype(f32))
    values = rounded(jnp.einsum('rjcy,cd->rjdy', normed, w_value.astype(f32)))
    q_hat = rounded(rms_scale(query, query_gain))
    k_hat = rounded(rms_scale(keys, key_gain))
    head_size = chans // HEADS
    q_heads = q_hat.reshape(count, width, HEADS, head_size, rows)
    k_heads = k_hat.reshape(count, width, HEADS, head_size, rows)
    v_heads = values.reshape(count, width, HEADS, head_size, rows)
    scores = jnp.einsum('rjhey,sjhey->hrsjy', q_heads, k_heads) * (1.0 / math.sqrt(head_size))
    weights = jnp.exp(scores) * mask[None, None, :, None, None]
    probs = rounded(weights / lax.optimization_barrier(jnp.sum(weights, axis=2, keepdims=True)))
    mixed = rounded(jnp.einsum('hrsjy,sjhey->rjhey', probs, v_heads)).reshape(count, width, chans, rows)
    hidden = cells + jnp.einsum('rjcy,cd->rjdy', mixed, w_out.astype(f32))
    normed_two = rounded(rms_scale(hidden, norm2_gain))
    inner = rounded(jax.nn.gelu(jnp.einsum('rjcy,cm->rjmy', normed_two, w_in.astype(f32)), approximate=True))
    tokens = hidden + jnp.einsum('rjmy,mc->rjcy', inner, w_back.astype(f32))
    total = lax.optimization_barrier(jnp.sum(tokens * mask[:, None, None, None], axis=0))
    return (total / jnp.sum(mask)).astype(jnp.bfloat16)

def convolve(values, weights):
    cols = values.shape[0]
    rows = values.shape[2]
    wide = jnp.pad(values.astype(jnp.float32), ((1, 1), (0, 0), (1, 1)))
    total = jnp.zeros((cols, weights.shape[3], rows), jnp.float32)
    for across in range(3):
        for down in range(3):
            total = total + jnp.einsum('xcy,co->xoy', wide[across:across + cols, :, down:down + rows], weights[across, down].astype(jnp.float32))
    return total

def reference(revisits, shifts, flags, norm1_gain, w_query, w_key, w_value, query_gain, key_gain, w_out, norm2_gain, w_in, w_back, conv_first, conv_second):
    padded = jnp.pad(revisits, ((0, 0), (reach, reach), (0, 0), (reach, reach)))

    def band_join(index):
        slab = lax.dynamic_slice_in_dim(padded, index * BR, BR + 2 * reach, 3)

        def single(entry, offset):
            return lax.dynamic_slice(entry, (reach + offset[1], jnp.int32(0), reach + offset[0]), (NCOLS, C, BR))
        aligned = jax.vmap(single)(slab, shifts)
        mask = lax.dynamic_slice_in_dim(flags, index, 1, 1)[:, 0].astype(jnp.float32)
        return join_cells(aligned, mask, norm1_gain, w_query, w_key, w_value, query_gain, key_gain, w_out, norm2_gain, w_in, w_back)
    bands = lax.map(band_join, jnp.arange(NBANDS, dtype=jnp.int32))
    joined = jnp.transpose(bands, (1, 2, 0, 3)).reshape(NCOLS, C, NROWS)
    act = jax.nn.gelu(convolve(joined, conv_first), approximate=True).astype(jnp.bfloat16)
    return convolve(act, conv_second)
```

```python
import functools

import jax
import jax.numpy as jnp
from jax import lax
from jax.experimental import pallas as pl
from jax.experimental.pallas import tpu as pltpu
from jax.sharding import PartitionSpec as P

HEADS = 4
eps = 1e-05
SLOTS = 2
LIMIT = 48 * 1024 * 1024
f32 = jnp.float32
half = jnp.bfloat16
SMEM = pltpu.MemorySpace.SMEM
VMEM = pltpu.MemorySpace.VMEM


def padded_2(block, sides, width):
    for axis, dim in sides:
        count = lax.axis_size(axis)
        forward = [(i, i + 1) for i in range(count - 1)]
        backward = [(target, source) for source, target in forward]
        low = lax.ppermute(
            lax.slice_in_dim(block, block.shape[dim] - width, None, axis=dim), axis, forward
        )
        high = lax.ppermute(lax.slice_in_dim(block, 0, width, axis=dim), axis, backward)
        block = jnp.concatenate([low, block, high], axis=dim)
    return block


def conv_valid(padded, weights, width_x, width_y):
    total = jnp.zeros((width_x, weights.shape[3], width_y), jnp.float32)
    for across in range(3):
        for down in range(3):
            total = total + jnp.einsum(
                "xcy,co->xoy",
                padded[across : across + width_x, :, down : down + width_y],
                weights[across, down],
                preferred_element_type=jnp.float32,
            )
    return total


def pack_kernel(width, ncols, shifts, info, revisits, out, held, sems):
    count = held.shape[0]
    chans, rows = held.shape[1:]
    slots, band = out.shape[2], out.shape[4]
    mine, base = info[0], info[1]
    places = []
    for r in range(count):
        place = mine - shifts[r, 1]
        inside = (place >= 0) & (place < ncols)
        owner = jnp.where(inside, lax.div(jnp.maximum(place, 0), jnp.int32(width)), -1)
        slot = -base
        for other, _, _ in places:
            slot = slot + jnp.where(other == owner, 1, 0)
        places.append((owner, slot, inside & (slot >= 0) & (slot < slots)))
    for r, (owner, slot, wanted) in enumerate(places):

        @pl.when(wanted)
        def _():
            pltpu.make_async_copy(revisits.at[r, 0], held.at[r], sems.at[r]).start()

    for r, (owner, slot, wanted) in enumerate(places):

        @pl.when(wanted)
        def _():
            pltpu.make_async_copy(revisits.at[r, 0], held.at[r], sems.at[r]).wait()
            offset = shifts[r, 0]
            turn = jnp.where(offset > 0, rows - offset, -offset)
            source = lax.broadcasted_iota(jnp.int32, (16, rows), 1) + offset
            inside = (source >= 0) & (source < rows)
            for c in range(0, chans, 16):
                piece = held[r, c : c + 16, :].astype(f32)
                piece = jnp.where(inside, pltpu.roll(piece, turn, 1), 0.0).astype(half)
                for b in range(rows // band):
                    out[owner, b, slot, c : c + 16, :] = piece[:, b * band : (b + 1) * band]


def pack(revisits, shifts, info, passes, bands, ncols):
    count, _, chans, rows = revisits.shape
    return pl.pallas_call(
        functools.partial(pack_kernel, ncols // passes, ncols),
        out_shape=jax.ShapeDtypeStruct((passes, bands, SLOTS, chans, rows // bands), half),
        in_specs=[
            pl.BlockSpec(memory_space=SMEM),
            pl.BlockSpec(memory_space=SMEM),
            pl.BlockSpec(memory_space=pl.ANY),
        ],
        out_specs=pl.BlockSpec(memory_space=VMEM),
        scratch_shapes=[
            pltpu.VMEM((count, chans, rows), half),
            pltpu.SemaphoreType.DMA((count,)),
        ],
        compiler_params=pltpu.CompilerParams(vmem_limit_bytes=LIMIT),
        name="pack",
    )(shifts, info, revisits)


def send(packed):
    passes, bands, slots, chans, band = packed.shape
    packed = packed.reshape(passes * bands, slots, chans, band)
    return lax.all_to_all(packed, ("pass", "tile", "row"), 0, 0, tiled=True)


def iota(shape, dim):
    return lax.broadcasted_iota(jnp.int32, shape, dim)


def dot(a, b, dims=((1,), (0,))):
    return lax.dot_general(a, b, (dims, ((), ())), preferred_element_type=f32)


def join_kernel(
    ncols,
    shifts,
    flags,
    info,
    parts,
    norm1_gain,
    w_query,
    w_key,
    w_value,
    query_gain,
    key_gain,
    w_out,
    norm2_gain,
    w_in,
    w_back,
    out,
    listed,
    tokens,
    queries,
    keys,
    values,
    w_qkv,
    w_mix,
    w_mlp,
    gains,
    sum_hidden,
    sum_inner,
    weights,
):
    total = shifts.shape[0]
    stages, sources, slots, chans, band = parts.shape
    width = out.shape[0]
    per = total // (sources // ncols)
    mlp = w_in.shape[1]
    head = chans // HEADS
    pair = 8 // width
    rows = width * chans
    mine = info[0] * width

    def channel_of(row):
        high = lax.div(row, jnp.int32(width * pair * head))
        e = lax.rem(lax.div(row, jnp.int32(width * pair)), jnp.int32(head))
        low = lax.rem(lax.div(row, jnp.int32(width)), jnp.int32(pair))
        return (high * pair + low) * head + e

    row_channel = channel_of(iota((rows, chans), 0))
    picked = row_channel == iota((rows, chans), 1)
    pick = jnp.where(picked, 1.0, 0.0).astype(half)
    spread = jnp.where(
        lax.rem(iota((chans, rows), 1), jnp.int32(chans)) == iota((chans, rows), 0), 1.0, 0.0
    ).astype(half)
    col_x = lax.div(iota((rows, rows), 1), jnp.int32(chans))
    row_x = lax.rem(iota((rows, rows), 0), jnp.int32(width))
    same = col_x == row_x
    for n, weight in enumerate((w_query, w_key, w_value)):
        chosen = dot(pick, weight[...], ((1,), (1,))).astype(half)
        w_qkv[n * rows : (n + 1) * rows, :] = jnp.where(same, dot(chosen, spread), 0.0).astype(half)
    mixing = dot(w_out[...], pick, ((0,), (1,)))
    mixing = jnp.concatenate([mixing] * width, axis=0)
    back_x = lax.rem(iota((rows, rows), 1), jnp.int32(width))
    from_x = lax.div(iota((rows, rows), 0), jnp.int32(chans))
    w_mix[...] = jnp.where(back_x == from_x, mixing, 0.0).astype(half)
    wide = dot(w_in[...], spread, ((0,), (0,)))
    wide = jnp.concatenate([wide] * width, axis=0)
    mlp_x = lax.div(iota((width * mlp, rows), 0), jnp.int32(mlp))
    in_x = lax.div(iota((width * mlp, rows), 1), jnp.int32(chans))
    w_mlp[...] = jnp.where(mlp_x == in_x, wide, 0.0).astype(half)
    plain = lax.rem(iota((rows, chans), 0), jnp.int32(chans)) == iota((rows, chans), 1)
    for n, (gain, where) in enumerate(
        ((norm1_gain, plain), (query_gain, picked), (key_gain, picked), (norm2_gain, plain))
    ):
        column = jnp.sum(jnp.where(where, gain[...], 0.0), axis=1, keepdims=True)
        gains[n] = jnp.broadcast_to(column, (rows, band))

    def choose(r, carry):
        found, blank = carry
        shift = shifts[r, 1]
        flagged = flags[r, 0] != 0
        reaches = (mine + width - 1 + shift >= 0) & (mine + shift < ncols)
        listed[found] = r
        return (
            found + jnp.where(flagged & reaches, 1, 0),
            blank + jnp.where(flagged & jnp.logical_not(reaches), 1, 0),
        )

    found, blank = lax.fori_loop(0, total, choose, (jnp.int32(0), jnp.int32(0)))

    def scale(tile, gain):
        mean = jnp.mean(tile * tile, axis=1, keepdims=True)
        return tile * lax.rsqrt(mean + eps) * gain

    def heads_scale(tile, gain):
        square = jnp.sum(tile * tile, axis=0)
        square = square.reshape(pair, width, band)
        mean = jnp.sum(square, axis=0, keepdims=True) * (1.0 / chans)
        factor = jnp.broadcast_to(lax.rsqrt(mean + eps), (pair, width, band))
        factor = factor.reshape(1, pair * width, band)
        scaled = tile * factor * gain.reshape(tile.shape)
        return scaled.astype(half).astype(f32)

    def project(i, carry):
        r = listed[i]
        first = lax.div(r, jnp.int32(per)) * per
        shift = shifts[r, 1]
        for x in range(width):
            column = mine + x + shift

            def earlier(j, slot):
                place = column - shifts[j, 1] - mine
                return slot + jnp.where((place >= 0) & (place < width), 1, 0)

            slot = lax.fori_loop(first, r, earlier, jnp.int32(0))
            inside = (column >= 0) & (column < ncols)
            source = lax.div(r, jnp.int32(per)) * ncols + jnp.clip(column, 0, ncols - 1)
            slot = jnp.where(inside, slot, 0)

            @pl.when(inside)
            def _():
                piece = parts[lax.div(slot, jnp.int32(slots)), source, lax.rem(slot, jnp.int32(slots))]
                tokens[i, x * chans : (x + 1) * chans, :] = piece

            @pl.when(jnp.logical_not(inside))
            def _():
                tokens[i, x * chans : (x + 1) * chans, :] = jnp.zeros((chans, band), half)

        token = tokens[i].astype(f32).reshape(width, chans, band)
        normed = scale(token, gains[0].reshape(width, chans, band)).astype(half)
        qkv = dot(w_qkv[...], normed.reshape(rows, band))
        tiles = (rows // 8, 8, band)
        query = heads_scale(qkv[:rows].reshape(tiles), gains[1])
        queries[i] = query * (1.0 / float(head) ** 0.5)
        keys[i] = heads_scale(qkv[rows : 2 * rows].reshape(tiles), gains[2])
        values[i] = qkv[2 * rows :].reshape(tiles).astype(half).astype(f32)
        return carry

    lax.fori_loop(0, found, project, 0)
    tokens[found] = jnp.zeros((rows, band), half)
    queries[found] = jnp.zeros((rows // 8, 8, band), f32)
    sum_hidden[...] = jnp.zeros((rows, band), f32)
    sum_inner[...] = jnp.zeros((width * mlp, band), f32)
    groups = HEADS // pair

    def attend(i, carry):
        query = queries[i]

        def score(s, norm):
            product = (query * keys[s]).reshape(groups, head, 8, band)
            weight = jnp.exp(jnp.sum(product, axis=1))
            weights[s] = weight
            return norm + weight

        norm = lax.fori_loop(0, found, score, jnp.zeros((groups, 8, band), f32) + blank.astype(f32))

        def mix(s, mixed):
            prob = (weights[s] / norm).astype(half).astype(f32)
            return mixed + prob[:, None] * values[s].reshape(groups, head, 8, band)

        mixed = lax.fori_loop(0, found, mix, jnp.zeros((groups, head, 8, band), f32))
        mixed = mixed.reshape(rows, band).astype(half)
        hidden = tokens[i].astype(f32) + dot(w_mix[...], mixed)
        normed = scale(
            hidden.reshape(width, chans, band), gains[3].reshape(width, chans, band)
        ).astype(half)
        inner = dot(w_mlp[...], normed.reshape(rows, band))
        inner = jax.nn.gelu(inner, approximate=True).astype(half).astype(f32)
        weight = jnp.where(i < found, 1.0, blank.astype(f32))
        sum_hidden[...] += hidden * weight
        sum_inner[...] += inner * weight
        return carry

    lax.fori_loop(0, found + jnp.where(blank > 0, 1, 0), attend, 0)
    inverse = (found + blank).astype(f32)
    for x in range(width):
        inner = sum_inner[x * mlp : (x + 1) * mlp, :]
        high = inner.astype(half)
        low = (inner - high.astype(f32)).astype(half)
        back = dot(w_back[...], high, ((0,), (0,))) + dot(w_back[...], low, ((0,), (0,)))
        sums = sum_hidden[x * chans : (x + 1) * chans, :] + back
        out[x] = (sums / inverse).astype(half)


def join(parts, shifts, flags, info, params, width, ncols):
    chans, band = parts.shape[3:]
    mlp = params[8].shape[1]
    total = shifts.shape[0]
    rows = width * chans
    params = [p.reshape(1, -1) if p.ndim == 1 else p for p in params]
    tiles = pltpu.VMEM((total + 1, rows // 8, 8, band), f32)
    return pl.pallas_call(
        functools.partial(join_kernel, ncols),
        out_shape=jax.ShapeDtypeStruct((width, chans, band), half),
        in_specs=[pl.BlockSpec(memory_space=SMEM)] * 3
        + [pl.BlockSpec(memory_space=VMEM)] * (1 + len(params)),
        out_specs=pl.BlockSpec(memory_space=VMEM),
        scratch_shapes=[
            pltpu.SMEM((total + 1,), jnp.int32),
            pltpu.VMEM((total + 1, rows, band), half),
            tiles,
            tiles,
            tiles,
            pltpu.VMEM((3 * rows, rows), half),
            pltpu.VMEM((rows, rows), half),
            pltpu.VMEM((width * mlp, rows), half),
            pltpu.VMEM((4, rows, band), f32),
            pltpu.VMEM((rows, band), f32),
            pltpu.VMEM((width * mlp, band), f32),
            pltpu.VMEM((total, HEADS // (8 // width), 8, band), f32),
        ],
        compiler_params=pltpu.CompilerParams(vmem_limit_bytes=LIMIT),
        name="join",
    )(shifts, flags, info, parts, *params)


def all_shifts(shifts):
    count = lax.axis_size("pass")
    me = lax.axis_index("pass")
    pieces = [shifts]
    for step in range(1, count):
        pieces.append(lax.ppermute(shifts, "pass", [(i, (i - step) % count) for i in range(count)]))
    stacked = jnp.stack(pieces)
    order = lax.rem(jnp.arange(count, dtype=jnp.int32) - me + count, count)
    return jnp.take(stacked, order, axis=0).reshape(-1, shifts.shape[1])


def most_slots(shifts, count, ncols, width):
    moved = shifts[:, 1].reshape(-1, count)
    place = jnp.arange(ncols, dtype=jnp.int32)[:, None, None] - moved
    low = jnp.arange(ncols // width, dtype=jnp.int32)[:, None, None, None] * width
    hits = (place >= low) & (place < low + width)
    return jnp.max(jnp.sum(hits.astype(jnp.int32), axis=-1))


def local(revisits, shifts, flags, *weights):
    params, (conv_first, conv_second) = weights[:10], weights[10:]
    passes = lax.axis_size("pass")
    bands = lax.axis_size(("tile", "row"))
    count = revisits.shape[0]
    ncols = revisits.shape[1] * bands
    assert revisits.shape[1] == 1
    width = ncols // passes
    pass_index = lax.axis_index("pass")
    mine = lax.axis_index(("tile", "row"))
    every = all_shifts(shifts)

    def packed(base):
        info = jnp.stack([mine, jnp.int32(0) + base]).astype(jnp.int32)
        return send(pack(revisits, shifts, info, passes, bands, ncols))

    info = pass_index.reshape(1).astype(jnp.int32)
    first = packed(0)
    stages = -(-count // SLOTS)
    if stages > 1:
        needed = most_slots(every, count, ncols, width)

        def more():
            held = jnp.zeros((stages,) + first.shape, half)
            held = lax.dynamic_update_index_in_dim(held, first, 0, 0)

            def step(i, held):
                return lax.dynamic_update_index_in_dim(held, packed(i * SLOTS), i, 0)

            held = lax.fori_loop(1, lax.div(needed + SLOTS - 1, SLOTS), step, held)
            return join(held, every, flags, info, params, width, ncols)

        def enough():
            return join(first[None], every, flags, info, params, width, ncols)

        joined = lax.cond(needed > SLOTS, more, enough)
    else:
        joined = join(first[None], every, flags, info, params, width, ncols)
    cols, chans, rows = joined.shape
    wide = padded_2(joined, (("pass", 0), (("tile", "row"), 2)), 2)
    act_wide = jax.nn.gelu(conv_valid(wide, conv_first, cols + 2, rows + 2), approximate=True)
    col_pos = lax.axis_index("pass") * cols - 1 + jnp.arange(cols + 2, dtype=jnp.int32)
    row_pos = lax.axis_index(("tile", "row")) * rows - 1 + jnp.arange(rows + 2, dtype=jnp.int32)
    col_inside = (col_pos >= 0) & (col_pos < cols * lax.axis_size("pass"))
    row_inside = (row_pos >= 0) & (row_pos < rows * lax.axis_size(("tile", "row")))
    inside = col_inside[:, None, None] & row_inside[None, None, :]
    act = jnp.where(inside, act_wide, 0.0).astype(jnp.bfloat16)
    return conv_valid(act, conv_second, cols, rows)


def solution(mesh):
    return jax.shard_map(
        local,
        mesh=mesh,
        in_specs=(
            P(("groups", "pass"), ("tile", "row"), None, None),
            P(("groups", "pass"), None),
            P("groups", ("tile", "row")),
        )
        + (P(),) * 12,
        out_specs=P(("groups", "pass"), None, ("tile", "row")),
        check_vma=False,
    )
```

```python
import functools

import jax
import jax.numpy as jnp
from jax import lax
from jax.experimental import pallas as pl
from jax.experimental.pallas import tpu as pltpu
from jax.sharding import PartitionSpec as P

HEADS = 4
eps = 1e-05
SLOTS = 3
LIMIT = 48 * 1024 * 1024
f32 = jnp.float32
half = jnp.bfloat16
SMEM = pltpu.MemorySpace.SMEM
VMEM = pltpu.MemorySpace.VMEM


def pack_kernel(window, ncols, shifts, info, revisits, out, held, sems):
    count = held.shape[0]
    chans, rows = held.shape[1:]
    bands, slots, part, band = out.shape[1:]
    mine, base = info[2], info[4]
    places = []
    for r in range(count):
        place = mine - shifts[r, 1]
        inside = (place >= 0) & (place < ncols)
        owner = jnp.where(inside, lax.div(jnp.maximum(place, 0), jnp.int32(window)), -1)
        slot = -base
        for other, _, _ in places:
            slot = slot + jnp.where(other == owner, 1, 0)
        places.append((owner, slot, inside & (slot >= 0) & (slot < slots)))
    for r, (owner, slot, wanted) in enumerate(places):

        @pl.when(wanted)
        def _():
            pltpu.make_async_copy(revisits.at[r, 0], held.at[r], sems.at[r]).start()

    for r, (owner, slot, wanted) in enumerate(places):

        @pl.when(wanted)
        def _():
            pltpu.make_async_copy(revisits.at[r, 0], held.at[r], sems.at[r]).wait()
            offset = shifts[r, 0]
            turn = jnp.where(offset > 0, rows - offset, -offset)
            source = iota((16, rows), 1) + offset
            inside = (source >= 0) & (source < rows)
            first = iota((16, band), 1) < band // 2
            for c in range(0, part, 16):
                halves = []
                for low in (c, part + c):
                    piece = held[r, low : low + 16, :].astype(f32)
                    halves.append(jnp.where(inside, pltpu.roll(piece, turn, 1), 0.0))
                for b in range(bands):
                    top, bottom = [h[:, b * band : (b + 1) * band] for h in halves]
                    out[2 * owner, b, slot, c : c + 16, :] = jnp.where(
                        first, top, pltpu.roll(bottom, band // 2, 1)
                    ).astype(half)
                    out[2 * owner + 1, b, slot, c : c + 16, :] = jnp.where(
                        first, pltpu.roll(top, band // 2, 1), bottom
                    ).astype(half)


def pack(revisits, shifts, info, passes, bands, ncols, slots):
    count, _, chans, rows = revisits.shape
    return pl.pallas_call(
        functools.partial(pack_kernel, 2 * ncols // passes, ncols),
        out_shape=jax.ShapeDtypeStruct((passes, bands, slots, chans // 2, rows // bands), half),
        in_specs=[
            pl.BlockSpec(memory_space=SMEM),
            pl.BlockSpec(memory_space=SMEM),
            pl.BlockSpec(memory_space=pl.ANY),
        ],
        out_specs=pl.BlockSpec(memory_space=VMEM),
        scratch_shapes=[
            pltpu.VMEM((count, chans, rows), half),
            pltpu.SemaphoreType.DMA((count,)),
        ],
        compiler_params=pltpu.CompilerParams(vmem_limit_bytes=LIMIT),
        name="pack",
    )(shifts, info, revisits)


def send(packed):
    passes, bands, slots, part, band = packed.shape
    packed = packed.reshape(passes * bands, slots * part, band)
    sent = lax.all_to_all(packed, ("pass", "tile", "row"), 0, 0, tiled=True)
    return sent.reshape(passes * bands, slots, part, band)


def iota(shape, dim):
    return lax.broadcasted_iota(jnp.int32, shape, dim)


def div(values, by):
    return lax.div(values, jnp.int32(by))


def rem(values, by):
    return lax.rem(values, jnp.int32(by))


def dot(a, b, dims=((1,), (0,))):
    return lax.dot_general(a, b, (dims, ((), ())), preferred_element_type=f32)


def weights_kernel(
    width,
    norm1_gain,
    w_query,
    w_key,
    w_value,
    query_gain,
    key_gain,
    w_out,
    norm2_gain,
    w_in,
    conv_first,
    conv_second,
    w_qkv,
    w_mix,
    w_mlp,
    norm_gains,
    head_gains,
    w_first,
    w_second,
):
    chans, mlp = w_in.shape
    head = chans // HEADS
    pair = 8 // width
    rows = width * chans
    band = norm_gains.shape[2]
    row = iota((rows, chans), 0)
    channel = (div(row, 8 * head) * pair + rem(div(row, width), pair)) * head + rem(div(row, 8), head)
    picked = channel == iota((rows, chans), 1)
    pick = jnp.where(picked, 1.0, 0.0).astype(half)
    spread = rem(iota((chans, rows), 1), chans) == iota((chans, rows), 0)
    spread = jnp.where(spread, 1.0, 0.0).astype(half)
    same = div(iota((rows, rows), 1), chans) == rem(iota((rows, rows), 0), width)
    for n, weight in enumerate((w_query, w_key, w_value)):
        chosen = dot(pick, weight[...], ((1,), (1,))).astype(half)
        w_qkv[n * rows : (n + 1) * rows, :] = jnp.where(same, dot(chosen, spread), 0.0).astype(half)
    mixing = dot(w_out[...], pick, ((0,), (1,)))
    mixing = jnp.concatenate([mixing] * width, axis=0)
    same = rem(iota((rows, rows), 1), width) == div(iota((rows, rows), 0), chans)
    w_mix[...] = jnp.where(same, mixing, 0.0).astype(half)
    wide = dot(w_in[...], spread, ((0,), (0,)))
    wide = jnp.concatenate([wide] * width, axis=0)
    same = div(iota((width * mlp, rows), 0), mlp) == div(iota((width * mlp, rows), 1), chans)
    w_mlp[...] = jnp.where(same, wide, 0.0).astype(half)
    plain = iota((chans, chans), 0) == iota((chans, chans), 1)
    for n, gain in enumerate((norm1_gain, norm2_gain)):
        column = jnp.sum(jnp.where(plain, gain[...], 0.0), axis=1, keepdims=True)
        norm_gains[n] = jnp.broadcast_to(column, (chans, band))
    for n, gain in enumerate((query_gain, key_gain)):
        column = jnp.sum(jnp.where(picked, gain[...], 0.0), axis=1, keepdims=True)
        head_gains[n] = jnp.broadcast_to(column, (rows, band))
    for kernel, result in ((conv_first, w_first), (conv_second, w_second)):
        outs = kernel.shape[3]
        for down in range(3):
            total = jnp.zeros((outs, 3 * chans), f32)
            for across in range(3):
                place = iota((chans, 3 * chans), 1) == iota((chans, 3 * chans), 0) + across * chans
                place = jnp.where(place, 1.0, 0.0).astype(half)
                total += dot(kernel[across, down], place, ((0,), (0,)))
            result[down * outs : (down + 1) * outs, :] = total.astype(half)


def arrange(params, conv_first, conv_second, width, band):
    chans, mlp = params[8].shape
    rows = width * chans
    outs = -(-conv_second.shape[3] // 16) * 16
    padding = ((0, 0), (0, 0), (0, 0), (0, outs - conv_second.shape[3]))
    conv_second = jnp.pad(conv_second, padding)
    arrays = [p.reshape(1, -1) if p.ndim == 1 else p for p in params[:9]]
    arrays += [conv_first, conv_second]
    return pl.pallas_call(
        functools.partial(weights_kernel, width),
        out_shape=[
            jax.ShapeDtypeStruct((3 * rows, rows), half),
            jax.ShapeDtypeStruct((rows, rows), half),
            jax.ShapeDtypeStruct((width * mlp, rows), half),
            jax.ShapeDtypeStruct((2, chans, band), f32),
            jax.ShapeDtypeStruct((2, rows, band), f32),
            jax.ShapeDtypeStruct((3 * conv_first.shape[3], 3 * chans), half),
            jax.ShapeDtypeStruct((3 * outs, 3 * chans), half),
        ],
        in_specs=[pl.BlockSpec(memory_space=VMEM)] * len(arrays),
        out_specs=[pl.BlockSpec(memory_space=VMEM)] * 7,
        compiler_params=pltpu.CompilerParams(vmem_limit_bytes=LIMIT),
        name="weights",
    )(*arrays)


def join_kernel(
    ncols,
    shifts,
    flags,
    info,
    parts,
    w_qkv,
    w_mix,
    w_mlp,
    norm_gains,
    head_gains,
    w_back,
    out,
    listed,
    tokens,
    queries,
    keys,
    values,
    weights,
    sum_hidden,
    sum_inner,
):
    total = shifts.shape[0]
    sources, slots, part, band = parts.shape
    width, chans = out.shape[:2]
    per = total // (sources // ncols)
    mlp = w_mlp.shape[0] // width
    head = chans // HEADS
    rows = width * chans
    groups = HEADS * width // 8
    window = 2 * width
    base = info[1] * window
    first_lanes = iota((part, band), 1) < band // 2

    def choose(r, carry):
        found, blank = carry
        shift = shifts[r, 1]
        flagged = flags[r, 0] != 0
        reaches = (base + window - 1 + shift >= 0) & (base + shift < ncols)
        listed[found] = r
        return (
            found + jnp.where(flagged & reaches, 1, 0),
            blank + jnp.where(flagged & jnp.logical_not(reaches), 1, 0),
        )

    found, blank = lax.fori_loop(0, total, choose, (jnp.int32(0), jnp.int32(0)))

    def scale(tile, gain):
        tile = tile.reshape(width, chans, band)
        mean = jnp.mean(tile * tile, axis=1, keepdims=True)
        scaled = tile * lax.rsqrt(mean + eps) * gain
        return scaled.astype(half).reshape(rows, band)

    def heads_scale(tile, gain):
        square = jnp.sum(tile * tile, axis=0)
        square = square.reshape(8 // width, width, band)
        mean = jnp.sum(square, axis=0, keepdims=True) * (1.0 / chans)
        factor = jnp.broadcast_to(lax.rsqrt(mean + eps), (8 // width, width, band))
        factor = factor.reshape(1, 8, band)
        scaled = tile * factor * gain.reshape(tile.shape)
        return scaled.astype(half).astype(f32)

    def project(i, carry):
        r = listed[i]
        owner = div(r, per)
        shift = shifts[r, 1]
        others = [
            (shifts[owner * per + j, 1], owner * per + j < r) for j in range(per)
        ]

        def piece(x):
            column = base + x + shift
            slot = jnp.int32(0)
            for other, before in others:
                place = x + shift - other
                hit = before & (place >= 0) & (place < window)
                slot = slot + jnp.where(hit, 1, 0)
            inside = (column >= 0) & (column < ncols)
            source = owner * ncols + jnp.clip(column, 0, ncols - 1)
            found_piece = parts[source, jnp.where(inside, slot, 0)].astype(f32)
            return jnp.where(inside, found_piece, 0.0)

        for x in range(width):
            left, right = piece(x), piece(x + width)
            tokens[i, x * chans : x * chans + part, :] = jnp.where(
                first_lanes, left, pltpu.roll(right, band // 2, 1)
            )
            tokens[i, x * chans + part : (x + 1) * chans, :] = jnp.where(
                first_lanes, pltpu.roll(left, band // 2, 1), right
            )
        qkv = dot(w_qkv[...], scale(tokens[i], norm_gains[0]))
        tiles = (rows // 8, 8, band)
        query = heads_scale(qkv[:rows].reshape(tiles), head_gains[0])
        queries[i] = query * (1.0 / float(head) ** 0.5)
        keys[i] = heads_scale(qkv[rows : 2 * rows].reshape(tiles), head_gains[1])
        values[i] = qkv[2 * rows :].reshape(tiles).astype(half).astype(f32)
        return carry

    lax.fori_loop(0, found, project, 0)
    tokens[found] = jnp.zeros((rows, band), f32)
    queries[found] = jnp.zeros((rows // 8, 8, band), f32)
    sum_hidden[...] = jnp.zeros((rows, band), f32)
    sum_inner[...] = jnp.zeros((width * mlp, band), f32)

    def attend(i, carry):
        query = queries[i]

        def score(s, norm):
            product = (query * keys[s]).reshape(groups, head, 8, band)
            weight = jnp.exp(jnp.sum(product, axis=1))
            weights[s] = weight
            return norm + weight

        norm = jnp.zeros((groups, 8, band), f32) + blank.astype(f32)
        norm = lax.fori_loop(0, found, score, norm)

        def mix(s, mixed):
            prob = (weights[s] / norm).astype(half).astype(f32)
            return mixed + prob[:, None] * values[s].reshape(groups, head, 8, band)

        mixed = lax.fori_loop(0, found, mix, jnp.zeros((groups, head, 8, band), f32))
        hidden = tokens[i] + dot(w_mix[...], mixed.reshape(rows, band).astype(half))
        inner = dot(w_mlp[...], scale(hidden, norm_gains[1]))
        inner = jax.nn.gelu(inner, approximate=True).astype(half).astype(f32)
        weight = jnp.where(i < found, 1.0, blank.astype(f32))
        sum_hidden[...] += hidden * weight
        sum_inner[...] += inner * weight
        return carry

    lax.fori_loop(0, found + jnp.where(blank > 0, 1, 0), attend, 0)
    inverse = (found + blank).astype(f32)
    for x in range(width):
        inner = sum_inner[x * mlp : (x + 1) * mlp, :]
        high = inner.astype(half)
        low = (inner - high.astype(f32)).astype(half)
        back = dot(w_back[...], high, ((0,), (0,))) + dot(w_back[...], low, ((0,), (0,)))
        sums = sum_hidden[x * chans : (x + 1) * chans, :] + back
        out[x] = (sums / inverse).astype(half)


def join(parts, shifts, flags, info, arranged, w_back, width, ncols):
    part, band = parts.shape[2:]
    mlp, chans = w_back.shape
    total = shifts.shape[0]
    rows = width * chans
    arrays = (parts, *arranged[:5], w_back)
    tiles = pltpu.VMEM((total + 1, rows // 8, 8, band), f32)
    return pl.pallas_call(
        functools.partial(join_kernel, ncols),
        out_shape=jax.ShapeDtypeStruct((width, chans, band), half),
        in_specs=[pl.BlockSpec(memory_space=SMEM)] * 3
        + [pl.BlockSpec(memory_space=VMEM)] * len(arrays),
        out_specs=pl.BlockSpec(memory_space=VMEM),
        scratch_shapes=[
            pltpu.SMEM((total + 1,), jnp.int32),
            pltpu.VMEM((total + 1, rows, band), f32),
            tiles,
            tiles,
            tiles,
            pltpu.VMEM((total, HEADS * width // 8, 8, band), f32),
            pltpu.VMEM((rows, band), f32),
            pltpu.VMEM((width * mlp, band), f32),
        ],
        compiler_params=pltpu.CompilerParams(vmem_limit_bytes=LIMIT),
        name="join",
    )(shifts, flags, info, *arrays)


def frame_kernel(info, mine, theirs, far, cols, strip_a, strip_b):
    width, chans, band = mine.shape
    side, odd = info[0], rem(info[2], 2)
    lane = iota((chans, band), 1)
    own = div(lane, band // 2) == side
    for j in range(width):
        here, there = mine[j].astype(f32), theirs[j].astype(f32)
        cols[2 + j] = jnp.where(own, here, pltpu.roll(there, band // 2, 1)).astype(half)

    def near(j):
        here, there = mine[j].astype(f32), theirs[j].astype(f32)
        return jnp.where(own, pltpu.roll(here, band // 2, 1), there).astype(half)

    for j in range(2):

        @pl.when(side == 0)
        def _():
            cols[width + 2 + j] = near(j)
            cols[j] = far[j]

        @pl.when(side == 1)
        def _():
            cols[j] = near(width - 2 + j)
            cols[width + 2 + j] = far[j]

    low = jnp.zeros((chans, band), f32)
    high = low
    for j in range(width + 4):
        column = cols[j].astype(f32)
        place = div(lane, 2) == j
        low = jnp.where(place, column if j == 0 else pltpu.roll(column, 2 * j, 1), low)
        high = jnp.where(place, pltpu.roll(column, 2 * j + 2, 1), high)
    strip_a[...] = jnp.where(odd == 0, high, low).astype(half)
    strip_b[...] = jnp.where(odd == 0, low, high).astype(half)


def frame(info, mine, theirs, far):
    width, chans, band = mine.shape
    strip = jax.ShapeDtypeStruct((chans, band), half)
    return pl.pallas_call(
        frame_kernel,
        out_shape=[jax.ShapeDtypeStruct((width + 4, chans, band), half), strip, strip],
        in_specs=[pl.BlockSpec(memory_space=SMEM)] + [pl.BlockSpec(memory_space=VMEM)] * 3,
        out_specs=[pl.BlockSpec(memory_space=VMEM)] * 3,
        compiler_params=pltpu.CompilerParams(vmem_limit_bytes=LIMIT),
        name="frame",
    )(info, mine, theirs, far)


def decode_kernel(ncols, nrows, info, cols, strip_a, strip_b, w_first, w_second, out, wide, act):
    chans, band = strip_a.shape
    width, outs = out.shape[:2]
    odd = rem(info[2], 2)
    from_a, from_b = strip_a[...].astype(f32), strip_b[...].astype(f32)
    low = jnp.where(odd == 1, from_a, from_b)
    high = jnp.where(odd == 0, from_a, from_b)
    lane = iota((chans, band), 1)
    for j in range(width + 4):
        wide[j * chans : (j + 1) * chans, :band] = cols[j]
        after = high if j == 0 else pltpu.roll(high, band - 2 * j, 1)
        before = pltpu.roll(low, band - 2 - 2 * j, 1)
        edge = jnp.where(lane < 2, after, jnp.where(lane >= band - 2, before, 0.0))
        wide[j * chans : (j + 1) * chans, band:] = edge.astype(half)

    def shifted(products, count):
        above, level, below = [products[n * count : (n + 1) * count] for n in range(3)]
        return pltpu.roll(above, 1, 1) + level + pltpu.roll(below, 2 * band - 1, 1)

    lane = iota((chans, 2 * band), 1)
    row = info[2] * band + jnp.where(lane < band + band // 2, lane, lane - 2 * band)
    row_inside = (row >= 0) & (row < nrows)
    for x in range(width + 2):
        column = info[3] * width + (x - 1)
        products = dot(w_first[...], wide[x * chans : (x + 3) * chans, :])
        hidden = jax.nn.gelu(shifted(products, chans), approximate=True)
        inside = row_inside & (column >= 0) & (column < ncols)
        act[x * chans : (x + 1) * chans, :] = jnp.where(inside, hidden, 0.0).astype(half)
    for x in range(width):
        products = dot(w_second[...], act[x * chans : (x + 3) * chans, :])
        out[x] = shifted(products, products.shape[0] // 3)[:outs, :band]


def decode(info, cols, strip_a, strip_b, w_first, w_second, outs, ncols, nrows):
    wide, chans, band = cols.shape
    return pl.pallas_call(
        functools.partial(decode_kernel, ncols, nrows),
        out_shape=jax.ShapeDtypeStruct((wide - 4, outs, band), f32),
        in_specs=[pl.BlockSpec(memory_space=SMEM)] + [pl.BlockSpec(memory_space=VMEM)] * 5,
        out_specs=pl.BlockSpec(memory_space=VMEM),
        scratch_shapes=[
            pltpu.VMEM((wide * chans, 2 * band), half),
            pltpu.VMEM(((wide - 2) * chans, 2 * band), half),
        ],
        compiler_params=pltpu.CompilerParams(vmem_limit_bytes=LIMIT),
        name="decode",
    )(info, cols, strip_a, strip_b, w_first, w_second)


def swap(values, axis, first):
    count = lax.axis_size(axis)
    pairs = [(i, i + 1) for i in range(first, count - 1, 2)]
    if not pairs:
        return jnp.zeros_like(values)
    return lax.ppermute(values, axis, pairs + [(b, a) for a, b in pairs])


def all_shifts(shifts):
    count = lax.axis_size("pass")
    me = lax.axis_index("pass")
    pieces = [shifts]
    for step in range(1, count):
        pieces.append(lax.ppermute(shifts, "pass", [(i, (i - step) % count) for i in range(count)]))
    start = rem(count - me, count) * shifts.shape[0]
    return lax.dynamic_slice_in_dim(
        jnp.concatenate(pieces * 2), start, count * shifts.shape[0], 0
    )


def most_slots(shifts, count, ncols, window):
    moved = shifts[:, 1].reshape(-1, count)
    place = jnp.arange(ncols, dtype=jnp.int32)[:, None, None] - moved
    low = jnp.arange(ncols // window, dtype=jnp.int32)[:, None, None, None] * window
    hits = (place >= low) & (place < low + window)
    return jnp.max(jnp.sum(hits.astype(jnp.int32), axis=-1))


def local(revisits, shifts, flags, *weights):
    params, (conv_first, conv_second) = weights[:10], weights[10:]
    passes = lax.axis_size("pass")
    bands = lax.axis_size(("tile", "row"))
    count, per_device, chans, nrows = revisits.shape
    assert per_device == 1 and passes % 2 == 0
    ncols = bands
    width = ncols // passes
    pass_index = lax.axis_index("pass")
    side = rem(pass_index, 2)
    mine = lax.axis_index(("tile", "row"))

    def info(base):
        return jnp.stack([side, div(pass_index, 2), mine, pass_index, jnp.int32(0) + base])

    def packed(base, slots):
        return pack(revisits, shifts, info(base), passes, bands, ncols, slots)

    slots = min(SLOTS, count)
    first = packed(0, slots)
    own_shifts, first = lax.optimization_barrier((shifts, first))
    first = send(first)
    every = all_shifts(own_shifts)
    arranged = arrange(params, conv_first, conv_second, width, nrows // bands)
    constant = info(0)

    def joined_from(parts):
        return join(parts, every, flags, constant, arranged, params[9], width, ncols)

    if count > slots:
        needed = most_slots(every, count, ncols, 2 * width)

        def more():
            held = jnp.zeros((first.shape[0], count) + first.shape[2:], half)
            held = lax.dynamic_update_slice_in_dim(held, first, 0, 1)

            def step(i, held):
                return lax.dynamic_update_slice_in_dim(held, send(packed(i, 1)), i, 1)

            return joined_from(lax.fori_loop(slots, needed, step, held))

        joined = lax.cond(needed > slots, more, lambda: joined_from(first))
    else:
        joined = joined_from(first)

    theirs = swap(joined, "pass", 0)
    if passes > 2:
        here = jnp.where(side == 0, joined[:2], joined[-2:]).astype(f32)
        there = jnp.where(side == 0, theirs[:2], theirs[-2:]).astype(f32)
        band = nrows // bands
        own = div(jnp.arange(band, dtype=jnp.int32), band // 2) == side
        edge = jnp.where(own, here, jnp.roll(there, band // 2, -1)).astype(half)
        far = swap(edge, "pass", 1)
    else:
        far = jnp.zeros_like(joined[:2])
    cols, strip_a, strip_b = frame(constant, joined, theirs, far)
    axis = ("tile", "row")
    strip_a, strip_b = swap(strip_a, axis, 0), swap(strip_b, axis, 1)
    return decode(
        constant, cols, strip_a, strip_b, *arranged[5:], conv_second.shape[3], ncols, nrows
    )


def solution(mesh):
    return jax.shard_map(
        local,
        mesh=mesh,
        in_specs=(
            P(("groups", "pass"), ("tile", "row"), None, None),
            P(("groups", "pass"), None),
            P("groups", ("tile", "row")),
        )
        + (P(),) * 12,
        out_specs=P(("groups", "pass"), None, ("tile", "row")),
        check_vma=False,
    )
```

```python
import functools

import jax
import jax.numpy as jnp
from jax import lax
from jax.experimental import pallas as pl
from jax.experimental.pallas import tpu as pltpu
from jax.sharding import PartitionSpec as P

HEADS = 4
eps = 1e-05
SLOTS = 3
LIMIT = 48 * 1024 * 1024
f32 = jnp.float32
half = jnp.bfloat16
SMEM = pltpu.MemorySpace.SMEM
VMEM = pltpu.MemorySpace.VMEM


def pack_kernel(window, ncols, first_slot, moves, revisits, *rest):
    if first_slot is None:
        base, out, table, held, staged, sems, out_sems = rest
        first_slot = base[0]
    else:
        out, table, held, staged, sems, out_sems = rest
    count = held.shape[0]
    chans, rows = held.shape[1:]
    bands, slots, part, band = out.shape[1:]
    mine = lax.axis_index("tile") * lax.axis_size("row") + lax.axis_index("row")
    read = pltpu.make_async_copy(moves, table, out_sems.at[0, 0])
    read.start()
    loads = [
        pltpu.make_async_copy(revisits.at[r, 0], held.at[r], sems.at[r]) for r in range(count)
    ]
    for load in loads:
        load.start()
    read.wait()
    places = []
    for r in range(count):
        place = mine - table[1, r]
        inside = (place >= 0) & (place < ncols)
        owner = jnp.where(inside, lax.div(jnp.maximum(place, 0), jnp.int32(window)), -1)
        slot = jnp.int32(0) - first_slot
        for other, _, _ in places:
            slot = slot + jnp.where(other == owner, 1, 0)
        places.append((owner, slot, inside & (slot >= 0) & (slot < slots)))

    def writes(r):
        owner, slot, _ = places[r]
        return [
            pltpu.make_async_copy(
                staged.at[r, side], out.at[2 * owner + side, :, slot], out_sems.at[r, side]
            )
            for side in range(2)
        ]

    for r in range(count):
        loads[r].wait()

        @pl.when(places[r][2])
        def _():
            offset = table[0, r]
            turn = jnp.where(offset > 0, band - offset, -offset)
            lane = iota((16, band), 1)
            stays = (lane + offset >= 0) & (lane + offset < band)
            later = jnp.broadcast_to(offset > 0, (16, band))
            first = lane < band // 2
            none = jnp.zeros((16, band), f32)
            for c in range(0, part, 16):
                halves = []
                for low in (c, part + c):
                    turned = [
                        pltpu.roll(
                            held[r, low : low + 16, b * band : (b + 1) * band].astype(f32), turn, 1
                        )
                        for b in range(bands)
                    ]
                    turned = [none] + turned + [none]
                    halves.append(
                        [
                            jnp.where(
                                stays, turned[b + 1], jnp.where(later, turned[b + 2], turned[b])
                            )
                            for b in range(bands)
                        ]
                    )
                for b in range(bands):
                    top, bottom = halves[0][b], halves[1][b]
                    staged[r, 0, b, c : c + 16, :] = jnp.where(
                        first, top, pltpu.roll(bottom, band // 2, 1)
                    ).astype(half)
                    staged[r, 1, b, c : c + 16, :] = jnp.where(
                        first, pltpu.roll(top, band // 2, 1), bottom
                    ).astype(half)
            for write in writes(r):
                write.start()

    for r in range(count):

        @pl.when(places[r][2])
        def _():
            for write in writes(r):
                write.wait()


def pack(revisits, moves, passes, bands, ncols, slots, base=None):
    count, _, chans, rows = revisits.shape
    part, band = chans // 2, rows // bands
    first_slot = 0 if base is None else None
    scalars = [] if base is None else [base.reshape(1)]
    return pl.pallas_call(
        functools.partial(pack_kernel, 2 * ncols // passes, ncols, first_slot),
        out_shape=jax.ShapeDtypeStruct((passes, bands, slots, part, band), half),
        in_specs=[pl.BlockSpec(memory_space=pl.ANY)] * 2
        + [pl.BlockSpec(memory_space=SMEM)] * len(scalars),
        out_specs=pl.BlockSpec(memory_space=pl.ANY),
        scratch_shapes=[
            pltpu.SMEM(moves.shape, jnp.int32),
            pltpu.VMEM((count, chans, rows), half),
            pltpu.VMEM((count, 2, bands, part, band), half),
            pltpu.SemaphoreType.DMA((count,)),
            pltpu.SemaphoreType.DMA((count, 2)),
        ],
        compiler_params=pltpu.CompilerParams(vmem_limit_bytes=LIMIT),
        name="pack",
    )(moves, revisits, *scalars)


def send(packed):
    passes, bands, slots, part, band = packed.shape
    packed = packed.reshape(passes * bands, slots * part, band)
    sent = lax.all_to_all(packed, ("pass", "tile", "row"), 0, 0, tiled=True)
    return sent.reshape(passes * bands, slots, part, band)


def iota(shape, dim):
    return lax.broadcasted_iota(jnp.int32, shape, dim)


def div(values, by):
    return lax.div(values, jnp.int32(by))


def rem(values, by):
    return lax.rem(values, jnp.int32(by))


def dot(a, b, dims=((1,), (0,))):
    return lax.dot_general(a, b, (dims, ((), ())), preferred_element_type=f32)


def make_plan(width, ncols, windows, moves, flags, info, plan, seen, filled):
    window = 2 * width
    total = flags.shape[1]
    sources = seen.shape[0]
    per = total // (sources // ncols)
    listed = (total + 2) * window

    def fill(ref, count, value):
        def one(i, carry):
            ref[i] = value
            return carry

        lax.fori_loop(0, count, one, 0)

    fill(plan, listed, jnp.int32(-1))
    fill(filled, window, jnp.int32(0))
    most = jnp.int32(0)
    for w in range(windows):
        base = w * window
        fill(seen, sources, jnp.int32(0))

        def revisit(r, most):
            shift = moves[1, r]
            counts = (flags[0, r] != 0) & (info[1] == w)
            first_source = div(r, per) * ncols + shift + base

            def column(x, most):
                source = first_source + x
                slot = seen[source]
                seen[source] = slot + 1

                @pl.when(counts)
                def _():
                    place = filled[x]
                    filled[x] = place + 1
                    plan[place * window + x] = source * 32 + slot

                return jnp.maximum(most, slot + 1)

            low = jnp.maximum(0, -shift - base)
            return lax.fori_loop(low, jnp.minimum(window, ncols - shift - base), column, most)

        most = lax.fori_loop(0, total, revisit, most)
    longest = lax.fori_loop(0, window, lambda x, n: jnp.maximum(n, filled[x]), jnp.int32(0))
    counting = lax.fori_loop(
        0, total, lambda r, n: n + jnp.where(flags[0, r] != 0, 1, 0), jnp.int32(0)
    )
    plan[listed] = longest
    plan[listed + 1] = counting
    plan[listed + 2] = most


def weights_kernel(
    width,
    ncols,
    windows,
    moves,
    flags,
    info,
    norm1_gain,
    w_query,
    w_key,
    w_value,
    query_gain,
    key_gain,
    w_out,
    norm2_gain,
    w_in,
    conv_first,
    conv_second,
    w_qkv,
    w_mix,
    w_mlp,
    norm_gains,
    head_gains,
    w_first,
    w_second,
    plan,
    seen,
    filled,
):
    make_plan(width, ncols, windows, moves, flags, info, plan, seen, filled)
    chans, mlp = w_in.shape
    head = chans // HEADS
    pair = 8 // width
    rows = width * chans
    band = norm_gains.shape[2]
    row = iota((rows, chans), 0)
    channel = (div(row, 8 * head) * pair + rem(div(row, width), pair)) * head + rem(div(row, 8), head)
    picked = channel == iota((rows, chans), 1)
    pick = jnp.where(picked, 1.0, 0.0).astype(half)
    spread = rem(iota((chans, rows), 1), chans) == iota((chans, rows), 0)
    spread = jnp.where(spread, 1.0, 0.0).astype(half)
    same = div(iota((rows, rows), 1), chans) == rem(iota((rows, rows), 0), width)
    for n, weight in enumerate((w_query, w_key, w_value)):
        chosen = dot(pick, weight[...], ((1,), (1,))).astype(half)
        w_qkv[n * rows : (n + 1) * rows, :] = jnp.where(same, dot(chosen, spread), 0.0).astype(half)
    mixing = dot(w_out[...], pick, ((0,), (1,)))
    mixing = jnp.concatenate([mixing] * width, axis=0)
    same = rem(iota((rows, rows), 1), width) == div(iota((rows, rows), 0), chans)
    w_mix[...] = jnp.where(same, mixing, 0.0).astype(half)
    wide = dot(w_in[...], spread, ((0,), (0,)))
    wide = jnp.concatenate([wide] * width, axis=0)
    same = div(iota((width * mlp, rows), 0), mlp) == div(iota((width * mlp, rows), 1), chans)
    w_mlp[...] = jnp.where(same, wide, 0.0).astype(half)
    plain = iota((chans, chans), 0) == iota((chans, chans), 1)
    for n, gain in enumerate((norm1_gain, norm2_gain)):
        column = jnp.sum(jnp.where(plain, gain[...], 0.0), axis=1, keepdims=True)
        norm_gains[n] = jnp.broadcast_to(column, (chans, band))
    for n, gain in enumerate((query_gain, key_gain)):
        column = jnp.sum(jnp.where(picked, gain[...], 0.0), axis=1, keepdims=True)
        head_gains[n] = jnp.broadcast_to(column, (rows, band))
    for kernel, result in ((conv_first, w_first), (conv_second, w_second)):
        outs = kernel.shape[3]
        for down in range(3):
            total = jnp.zeros((outs, 3 * chans), f32)
            for across in range(3):
                place = iota((chans, 3 * chans), 1) == iota((chans, 3 * chans), 0) + across * chans
                place = jnp.where(place, 1.0, 0.0).astype(half)
                total += dot(kernel[across, down], place, ((0,), (0,)))
            result[down * outs : (down + 1) * outs, :] = total.astype(half)


def arrange(params, conv_first, conv_second, moves, flags, info, passes, ncols, band):
    chans, mlp = params[8].shape
    width = ncols // passes
    rows = width * chans
    total = flags.shape[1]
    sources = passes * ncols
    outs = -(-conv_second.shape[3] // 16) * 16
    padding = ((0, 0), (0, 0), (0, 0), (0, outs - conv_second.shape[3]))
    conv_second = jnp.pad(conv_second, padding)
    arrays = [p.reshape(1, -1) if p.ndim == 1 else p for p in params[:9]]
    arrays += [conv_first, conv_second]
    return pl.pallas_call(
        functools.partial(weights_kernel, width, ncols, passes // 2),
        out_shape=[
            jax.ShapeDtypeStruct((3 * rows, rows), half),
            jax.ShapeDtypeStruct((rows, rows), half),
            jax.ShapeDtypeStruct((width * mlp, rows), half),
            jax.ShapeDtypeStruct((2, chans, band), f32),
            jax.ShapeDtypeStruct((2, rows, band), f32),
            jax.ShapeDtypeStruct((3 * conv_first.shape[3], 3 * chans), half),
            jax.ShapeDtypeStruct((3 * outs, 3 * chans), half),
            jax.ShapeDtypeStruct(((total + 2) * 2 * width + 3,), jnp.int32),
        ],
        in_specs=[pl.BlockSpec(memory_space=SMEM)] * 3
        + [pl.BlockSpec(memory_space=VMEM)] * len(arrays),
        out_specs=[pl.BlockSpec(memory_space=VMEM)] * 7 + [pl.BlockSpec(memory_space=SMEM)],
        scratch_shapes=[
            pltpu.SMEM((sources,), jnp.int32),
            pltpu.SMEM((2 * width,), jnp.int32),
        ],
        compiler_params=pltpu.CompilerParams(vmem_limit_bytes=LIMIT),
        name="weights",
    )(moves, flags, info, *arrays)


def join_kernel(
    plan,
    info,
    parts,
    w_qkv,
    w_mix,
    w_mlp,
    norm_gains,
    head_gains,
    w_back,
    out,
    strip,
    tokens,
    queries,
    keys,
    values,
    weights,
    sum_hidden,
    sum_inner,
):
    sources, slots, part, band = parts.shape
    width, chans = out.shape[:2]
    mlp = w_mlp.shape[0] // width
    head = chans // HEADS
    rows = width * chans
    groups = HEADS * width // 8
    window = 2 * width
    listed = plan.shape[0] - 3
    found, counting = plan[listed], plan[listed + 1]
    blank = (counting - found).astype(f32)
    pairs = div(found + jnp.where(counting > found, 2, 1), 2)
    first_lanes = iota((part, band), 1) < band // 2
    side = info[0]

    def scale(tile, gain):
        tile = tile.reshape(width, chans, 2 * band)
        mean = jnp.mean(tile * tile, axis=1, keepdims=True)
        scaled = tile * lax.rsqrt(mean + eps) * jnp.concatenate([gain, gain], axis=1)
        return scaled.astype(half).reshape(rows, 2 * band)

    def heads_scale(tile, gain):
        square = jnp.sum(tile * tile, axis=0)
        square = square.reshape(8 // width, width, band)
        mean = jnp.sum(square, axis=0, keepdims=True) * (1.0 / chans)
        factor = jnp.broadcast_to(lax.rsqrt(mean + eps), (8 // width, width, band))
        factor = factor.reshape(1, 8, band)
        scaled = tile * factor * gain.reshape(tile.shape)
        return scaled.astype(half).astype(f32)

    def project(n, carry):
        for t in range(2):
            i = 2 * n + t
            lanes = slice(t * band, (t + 1) * band)

            def piece(x):
                entry = plan[i * window + x]
                held = jnp.maximum(entry, 0)
                value = parts[lax.shift_right_logical(held, 5), held & 31].astype(f32)
                return jnp.where(entry >= 0, value, 0.0)

            for x in range(width):
                left, right = piece(x), piece(x + width)
                tokens[n, x * chans : x * chans + part, lanes] = jnp.where(
                    first_lanes, left, pltpu.roll(right, band // 2, 1)
                )
                tokens[n, x * chans + part : (x + 1) * chans, lanes] = jnp.where(
                    first_lanes, pltpu.roll(left, band // 2, 1), right
                )
        qkv = dot(w_qkv[...], scale(tokens[n], norm_gains[0]))
        tiles = (rows // 8, 8, band)
        for t in range(2):
            i = 2 * n + t
            one = qkv[:, t * band : (t + 1) * band]
            query = heads_scale(one[:rows].reshape(tiles), head_gains[0])
            queries[i] = query * (1.0 / float(head) ** 0.5)
            keys[i] = heads_scale(one[rows : 2 * rows].reshape(tiles), head_gains[1])
            values[i] = one[2 * rows :].reshape(tiles).astype(half).astype(f32)
        return carry

    lax.fori_loop(0, pairs, project, 0)
    sum_hidden[...] = jnp.zeros((rows, band), f32)
    sum_inner[...] = jnp.zeros((width * mlp, band), f32)

    def attend(n, carry):
        def score(s, norms):
            added = []
            for t in range(2):
                product = (queries[2 * n + t] * keys[s]).reshape(groups, head, 8, band)
                weight = jnp.exp(jnp.sum(product, axis=1))
                weights[t, s] = weight
                added.append(norms[t] + weight)
            return tuple(added)

        norm = jnp.zeros((groups, 8, band), f32) + blank
        norms = lax.fori_loop(0, found, score, (norm, norm))
        inverses = [1.0 / norm for norm in norms]
        mixed = []
        for g in range(groups):

            def mix(s, sums):
                value = values[s, g * head : (g + 1) * head]
                probs = [(weights[t, s, g] * inverses[t][g]).astype(half).astype(f32) for t in range(2)]
                return tuple(sums[t] + probs[t][None] * value for t in range(2))

            none = jnp.zeros((head, 8, band), f32)
            mixed.append(lax.fori_loop(0, found, mix, (none, none)))
        mixed = [
            jnp.concatenate([m[t].reshape(head * 8, band).astype(half) for m in mixed], axis=0)
            for t in range(2)
        ]
        hidden = tokens[n] + dot(w_mix[...], jnp.concatenate(mixed, axis=1))
        inner = dot(w_mlp[...], scale(hidden, norm_gains[1]))
        inner = jax.nn.gelu(inner, approximate=True).astype(half).astype(f32)
        rest = jnp.where(found == 2 * n, blank, 0.0)
        rest_after = jnp.where(found == 2 * n + 1, blank, 0.0)
        first_weight = jnp.where(2 * n < found, 1.0, rest)
        second_weight = jnp.where(2 * n + 1 < found, 1.0, rest_after)
        sum_hidden[...] += hidden[:, :band] * first_weight + hidden[:, band:] * second_weight
        sum_inner[...] += inner[:, :band] * first_weight + inner[:, band:] * second_weight
        return carry

    lax.fori_loop(0, pairs, attend, 0)
    inverse = 1.0 / counting.astype(f32)
    lane = iota((chans, band), 1)
    edges = jnp.zeros((chans, band), f32)
    taken = jnp.where(side == 0, 0, band // 2 - 2)
    for x in range(width):
        inner = sum_inner[x * mlp : (x + 1) * mlp, :]
        high = inner.astype(half)
        low = (inner - high.astype(f32)).astype(half)
        back = dot(w_back[...], jnp.concatenate([high, low], axis=1))
        sums = sum_hidden[x * chans : (x + 1) * chans, :] + back[:, :band] + back[:, band:]
        joined = (sums * inverse).astype(half)
        out[x] = joined
        joined = joined.astype(f32)
        for column, start in ((x, 0), (x + width, band // 2)):
            turn = rem(2 * column - start - taken + 2 * band, band)
            edges = jnp.where(div(lane, 2) == column, pltpu.roll(joined, turn, 1), edges)
    strip[...] = edges.astype(half)


def join(parts, plan, info, arranged, w_back, width):
    part, band = parts.shape[2:]
    chans, mlp = w_back.shape
    total = (plan.shape[0] - 3) // (2 * width) - 2
    rows = width * chans
    groups = HEADS * width // 8
    arrays = (parts, *arranged[:5], w_back)
    tiles = pltpu.VMEM((total + 2, rows // 8, 8, band), f32)
    return pl.pallas_call(
        join_kernel,
        out_shape=[
            jax.ShapeDtypeStruct((width, chans, band), half),
            jax.ShapeDtypeStruct((chans, band), half),
        ],
        in_specs=[pl.BlockSpec(memory_space=SMEM)] * 2
        + [pl.BlockSpec(memory_space=VMEM)] * len(arrays),
        out_specs=[pl.BlockSpec(memory_space=VMEM)] * 2,
        scratch_shapes=[
            pltpu.VMEM((total // 2 + 1, rows, 2 * band), f32),
            tiles,
            tiles,
            tiles,
            pltpu.VMEM((2, total, groups, 8, band), f32),
            pltpu.VMEM((rows, band), f32),
            pltpu.VMEM((width * mlp, band), f32),
        ],
        compiler_params=pltpu.CompilerParams(vmem_limit_bytes=LIMIT),
        name="join",
    )(plan, info, *arrays)


def frame_columns(info, mine, theirs, far, put):
    width, chans, band = mine.shape
    side = info[0]
    own = div(iota((chans, band), 1), band // 2) == side
    for j in range(width):
        here, there = mine[j].astype(f32), theirs[j].astype(f32)
        put(2 + j, jnp.where(own, here, pltpu.roll(there, band // 2, 1)).astype(half))

    def near(j):
        here, there = mine[j].astype(f32), theirs[j].astype(f32)
        return jnp.where(own, pltpu.roll(here, band // 2, 1), there).astype(half)

    @pl.when(side == 0)
    def _():
        for j in range(2):
            put(width + 2 + j, near(j))
            put(j, far(j))

    @pl.when(side == 1)
    def _():
        for j in range(2):
            put(j, near(width - 2 + j))
            put(width + 2 + j, far(j))


def frame_kernel(info, mine, theirs, far, cols, strip_a, strip_b):
    width, chans, band = mine.shape
    odd = rem(info[2], 2)
    lane = iota((chans, band), 1)

    def put(j, column):
        cols[j] = column

    frame_columns(info, mine, theirs, lambda j: far[j], put)
    low = jnp.zeros((chans, band), f32)
    high = low
    for j in range(width + 4):
        column = cols[j].astype(f32)
        place = div(lane, 2) == j
        low = jnp.where(place, column if j == 0 else pltpu.roll(column, 2 * j, 1), low)
        high = jnp.where(place, pltpu.roll(column, 2 * j + 2, 1), high)
    strip_a[...] = jnp.where(odd == 0, high, low).astype(half)
    strip_b[...] = jnp.where(odd == 0, low, high).astype(half)


def frame(info, mine, theirs, far):
    width, chans, band = mine.shape
    strip = jax.ShapeDtypeStruct((chans, band), half)
    return pl.pallas_call(
        frame_kernel,
        out_shape=[jax.ShapeDtypeStruct((width + 4, chans, band), half), strip, strip],
        in_specs=[pl.BlockSpec(memory_space=SMEM)] + [pl.BlockSpec(memory_space=VMEM)] * 3,
        out_specs=[pl.BlockSpec(memory_space=VMEM)] * 3,
        compiler_params=pltpu.CompilerParams(vmem_limit_bytes=LIMIT),
        name="frame",
    )(info, mine, theirs, far)


def convolve(ncols, nrows, info, low, high, w_first, w_second, out, wide, act):
    chans, band = low.shape
    outs, width = out.shape[:2]
    lane = iota((chans, band), 1)
    for j in range(width + 4):
        after = high if j == 0 else pltpu.roll(high, band - 2 * j, 1)
        before = pltpu.roll(low, band - 2 - 2 * j, 1)
        edge = jnp.where(lane < 2, after, jnp.where(lane >= band - 2, before, 0.0))
        wide[j * chans : (j + 1) * chans, band:] = edge.astype(half)

    def shifted(products, count):
        above, level, below = [products[n * count : (n + 1) * count] for n in range(3)]
        return pltpu.roll(above, 1, 1) + level + pltpu.roll(below, 2 * band - 1, 1)

    lane = iota((chans, 2 * band), 1)
    row = info[2] * band + jnp.where(lane < band + band // 2, lane, lane - 2 * band)
    row_inside = (row >= 0) & (row < nrows)
    for x in range(width + 2):
        column = info[3] * width + (x - 1)
        products = dot(w_first[...], wide[x * chans : (x + 3) * chans, :])
        hidden = jax.nn.gelu(shifted(products, chans), approximate=True)
        inside = row_inside & (column >= 0) & (column < ncols)
        act[x * chans : (x + 1) * chans, :] = jnp.where(inside, hidden, 0.0).astype(half)
    for x in range(width):
        products = dot(w_second[...], act[x * chans : (x + 3) * chans, :])
        out[:, x, :] = shifted(products, products.shape[0] // 3)[:outs, :band]


def decode_kernel(ncols, nrows, info, cols, strip_a, strip_b, w_first, w_second, out, wide, act):
    chans, band = strip_a.shape
    odd = rem(info[2], 2)
    from_a, from_b = strip_a[...].astype(f32), strip_b[...].astype(f32)
    for j in range(cols.shape[0]):
        wide[j * chans : (j + 1) * chans, :band] = cols[j]
    low = jnp.where(odd == 1, from_a, from_b)
    high = jnp.where(odd == 0, from_a, from_b)
    convolve(ncols, nrows, info, low, high, w_first, w_second, out, wide, act)


def decode_pair_kernel(
    ncols, nrows, info, mine, theirs, strip_a, strip_b, w_first, w_second, out, wide, act
):
    width, chans, band = mine.shape
    side = info[0]

    def put(j, column):
        wide[j * chans : (j + 1) * chans, :band] = column

    frame_columns(info, mine, theirs, lambda j: jnp.zeros((chans, band), half), put)
    turn = jnp.where(side == 0, 4, band + 4 - 2 * width)
    from_a = pltpu.roll(strip_a[...].astype(f32), turn, 1)
    from_b = pltpu.roll(strip_b[...].astype(f32), turn, 1)
    low = jnp.where(side == 1, from_a, from_b)
    high = jnp.where(side == 0, from_a, from_b)
    convolve(ncols, nrows, info, low, high, w_first, w_second, out, wide, act)


def decode(kernel, info, arrays, width, outs, ncols, nrows):
    chans, band = arrays[0].shape[1:]
    out = pl.pallas_call(
        functools.partial(kernel, ncols, nrows),
        out_shape=jax.ShapeDtypeStruct((outs, width, band), f32),
        in_specs=[pl.BlockSpec(memory_space=SMEM)] + [pl.BlockSpec(memory_space=VMEM)] * len(arrays),
        out_specs=pl.BlockSpec(memory_space=VMEM),
        scratch_shapes=[
            pltpu.VMEM(((width + 4) * chans, 2 * band), half),
            pltpu.VMEM(((width + 2) * chans, 2 * band), half),
        ],
        compiler_params=pltpu.CompilerParams(vmem_limit_bytes=LIMIT),
        name="decode",
    )(info, *arrays)
    return jnp.transpose(out, (1, 0, 2))


def swap(values, axis, first):
    count = lax.axis_size(axis)
    pairs = [(i, i + 1) for i in range(first, count - 1, 2)]
    if not pairs:
        return jnp.zeros_like(values)
    return lax.ppermute(values, axis, pairs + [(b, a) for a, b in pairs])


def all_moves(moves):
    count = lax.axis_size("pass")
    me = lax.axis_index("pass")
    pieces = [moves]
    for step in range(1, count):
        pieces.append(lax.ppermute(moves, "pass", [(i, (i - step) % count) for i in range(count)]))
    start = rem(count - me, count) * moves.shape[1]
    return lax.dynamic_slice_in_dim(
        jnp.concatenate(pieces * 2, axis=1), start, count * moves.shape[1], 1
    )


def to_band(strip, other):
    tiles, passes, cores = [lax.axis_size(a) for a in ("tile", "pass", "row")]

    def index(band, side):
        return (band // cores) * passes * cores + side * cores + band % cores

    bands = tiles * cores
    pairs = [(index(b, 0), index(b - 1, other)) for b in range(1, bands)]
    pairs += [(index(b, 1), index(b + 1, 1 - other)) for b in range(bands - 1)]
    return lax.ppermute(strip, ("tile", "pass", "row"), pairs)


def local(revisits, shifts, flags, *weights):
    params, (conv_first, conv_second) = weights[:10], weights[10:]
    passes = lax.axis_size("pass")
    bands = lax.axis_size(("tile", "row"))
    count, per_device, chans, nrows = revisits.shape
    assert per_device == 1 and passes % 2 == 0 and count <= 32
    ncols = bands
    width = ncols // passes
    band = nrows // bands
    pass_index = lax.axis_index("pass")
    side = rem(pass_index, 2)
    mine = lax.axis_index(("tile", "row"))
    info = jnp.stack([side, div(pass_index, 2), mine, pass_index])
    moves = shifts.T
    slots = min(SLOTS, count)
    first = pack(revisits, moves, passes, bands, ncols, slots)
    moves_after, first = lax.optimization_barrier((moves, first))
    first = send(first)
    every = all_moves(moves_after)
    arranged = arrange(
        params, conv_first, conv_second, every, flags.T, info, passes, ncols, band
    )
    plan = arranged[7]

    def joined_from(parts):
        return join(parts, plan, info, arranged, params[9].T, width)

    if count > slots:
        needed = plan[plan.shape[0] - 1]

        def more():
            held = jnp.zeros((first.shape[0], count) + first.shape[2:], half)
            held = lax.dynamic_update_slice_in_dim(held, first, 0, 1)

            def step(i, held):
                sent = send(pack(revisits, moves, passes, bands, ncols, 1, i))
                return lax.dynamic_update_slice_in_dim(held, sent, i, 1)

            return joined_from(lax.fori_loop(slots, needed, step, held))

        joined, strip = lax.cond(needed > slots, more, lambda: joined_from(first))
    else:
        joined, strip = joined_from(first)

    outs = conv_second.shape[3]
    theirs = swap(joined, "pass", 0)
    if passes == 2:
        arrays = (joined, theirs, to_band(strip, 0), to_band(strip, 1), *arranged[5:7])
        return decode(decode_pair_kernel, info, arrays, width, outs, ncols, nrows)
    here = jnp.where(side == 0, joined[:2], joined[-2:]).astype(f32)
    there = jnp.where(side == 0, theirs[:2], theirs[-2:]).astype(f32)
    own = div(jnp.arange(band, dtype=jnp.int32), band // 2) == side
    edge = jnp.where(own, here, jnp.roll(there, band // 2, -1)).astype(half)
    cols, strip_a, strip_b = frame(info, joined, theirs, swap(edge, "pass", 1))
    strip_a, strip_b = swap(strip_a, ("tile", "row"), 0), swap(strip_b, ("tile", "row"), 1)
    arrays = (cols, strip_a, strip_b, *arranged[5:7])
    return decode(decode_kernel, info, arrays, width, outs, ncols, nrows)


def solution(mesh):
    return jax.shard_map(
        local,
        mesh=mesh,
        in_specs=(
            P(("groups", "pass"), ("tile", "row"), None, None),
            P(("groups", "pass"), None),
            P("groups", ("tile", "row")),
        )
        + (P(),) * 12,
        out_specs=P(("groups", "pass"), None, ("tile", "row")),
        check_vma=False,
    )
```

```python
import functools

import jax
import jax.numpy as jnp
from jax import lax
from jax.experimental import pallas as pl
from jax.experimental.pallas import tpu as pltpu
from jax.sharding import PartitionSpec as P

HEADS = 4
eps = 1e-05
SLOTS = 3
LIMIT = 48 * 1024 * 1024
PACK_LIMIT = 63 * 1024 * 1024
f32 = jnp.float32
half = jnp.bfloat16
SMEM = pltpu.MemorySpace.SMEM
VMEM = pltpu.MemorySpace.VMEM
HBM = pltpu.MemorySpace.HBM


def pack_kernel(window, ncols, first_slot, moves, revisits, *rest):
    if first_slot is None:
        base, out, moves_out, table, held, staged, sems, out_sems, echo_sem = rest
        first_slot = base[0]
    else:
        out, moves_out, table, held, staged, sems, out_sems, echo_sem = rest
    count = held.shape[0]
    chans, rows = held.shape[1:]
    bands, slots, part, band = out.shape[1:]
    mine = here()[2]
    read = pltpu.make_async_copy(moves, table, echo_sem.at[0])
    read.start()
    loads = [
        pltpu.make_async_copy(revisits.at[r, 0], held.at[r], sems.at[r]) for r in range(count)
    ]
    for load in loads:
        load.start()
    read.wait()
    echo = pltpu.make_async_copy(table, moves_out, echo_sem.at[1])
    echo.start()
    places = []
    for r in range(count):
        place = mine - table[1, r]
        inside = (place >= 0) & (place < ncols)
        owner = jnp.where(inside, lax.div(jnp.maximum(place, 0), jnp.int32(window)), -1)
        slot = jnp.int32(0) - first_slot
        for other, _, _ in places:
            slot = slot + jnp.where(other == owner, 1, 0)
        places.append((owner, slot, inside & (slot >= 0) & (slot < slots)))

    def writes(r):
        owner, slot, _ = places[r]
        return [
            pltpu.make_async_copy(
                staged.at[r, side], out.at[2 * owner + side, :, slot], out_sems.at[r, side]
            )
            for side in range(2)
        ]

    for r in range(count):
        loads[r].wait()

        @pl.when(places[r][2])
        def _():
            offset = table[0, r]
            turn = jnp.where(offset > 0, band - offset, -offset)
            lane = iota((16, band), 1)
            stays = (lane + offset >= 0) & (lane + offset < band)
            later = jnp.broadcast_to(offset > 0, (16, band))
            first = lane < band // 2
            none = jnp.zeros((16, band), f32)
            for c in range(0, part, 16):
                halves = []
                for low in (c, part + c):
                    turned = [
                        pltpu.roll(
                            held[r, low : low + 16, b * band : (b + 1) * band].astype(f32), turn, 1
                        )
                        for b in range(bands)
                    ]
                    turned = [none] + turned + [none]
                    halves.append(
                        [
                            jnp.where(
                                stays, turned[b + 1], jnp.where(later, turned[b + 2], turned[b])
                            )
                            for b in range(bands)
                        ]
                    )
                for b in range(bands):
                    top, bottom = halves[0][b], halves[1][b]
                    staged[r, 0, b, c : c + 16, :] = jnp.where(
                        first, top, pltpu.roll(bottom, band // 2, 1)
                    ).astype(half)
                    staged[r, 1, b, c : c + 16, :] = jnp.where(
                        first, pltpu.roll(top, band // 2, 1), bottom
                    ).astype(half)
            for write in writes(r):
                write.start()

    for r in range(count):

        @pl.when(places[r][2])
        def _():
            for write in writes(r):
                write.wait()

    echo.wait()


def pack(revisits, moves, passes, bands, ncols, slots, base=None):
    count, _, chans, rows = revisits.shape
    part, band = chans // 2, rows // bands
    first_slot = 0 if base is None else None
    scalars = [] if base is None else [base.reshape(1)]
    return pl.pallas_call(
        functools.partial(pack_kernel, 2 * ncols // passes, ncols, first_slot),
        out_shape=[
            jax.ShapeDtypeStruct((passes, bands, slots, part, band), half),
            jax.ShapeDtypeStruct(moves.shape, jnp.int32),
        ],
        in_specs=[pl.BlockSpec(memory_space=HBM)] * 2
        + [pl.BlockSpec(memory_space=SMEM)] * len(scalars),
        out_specs=[pl.BlockSpec(memory_space=HBM)] * 2,
        scratch_shapes=[
            pltpu.SMEM(moves.shape, jnp.int32),
            pltpu.VMEM((count, chans, rows), half),
            pltpu.VMEM((count, 2, bands, part, band), half),
            pltpu.SemaphoreType.DMA((count,)),
            pltpu.SemaphoreType.DMA((count, 2)),
            pltpu.SemaphoreType.DMA((2,)),
        ],
        compiler_params=pltpu.CompilerParams(vmem_limit_bytes=PACK_LIMIT),
        name="pack",
    )(moves, revisits, *scalars)


def send(packed):
    passes, bands, slots, part, band = packed.shape
    packed = packed.reshape(passes * bands, slots * part, band)
    sent = lax.all_to_all(packed, ("pass", "tile", "row"), 0, 0, tiled=True)
    return sent.reshape(passes * bands, slots, part, band)


def here():
    index = lax.axis_index("pass")
    band = lax.axis_index("tile") * lax.axis_size("row") + lax.axis_index("row")
    return rem(index, 2), div(index, 2), band


def iota(shape, dim):
    return lax.broadcasted_iota(jnp.int32, shape, dim)


def div(values, by):
    return lax.div(values, jnp.int32(by))


def rem(values, by):
    return lax.rem(values, jnp.int32(by))


def dot(a, b, dims=((1,), (0,))):
    return lax.dot_general(a, b, (dims, ((), ())), preferred_element_type=f32)


def make_plan(width, ncols, windows, moves, flags, plan, seen, filled):
    window = 2 * width
    total = flags.shape[1]
    sources = seen.shape[0]
    per = total // (sources // ncols)
    listed = (total + 2) * window

    def fill(ref, count, value):
        def one(i, carry):
            ref[i] = value
            return carry

        lax.fori_loop(0, count, one, 0)

    fill(plan, listed, jnp.int32(-1))
    fill(filled, window, jnp.int32(0))
    pair = here()[1]
    most = jnp.int32(0)
    for w in range(windows):
        base = w * window
        fill(seen, sources, jnp.int32(0))

        def revisit(r, most):
            shift = moves[1, r]
            counts = (flags[0, r] != 0) & (pair == w)
            first_source = div(r, per) * ncols + shift + base

            def column(x, most):
                source = first_source + x
                slot = seen[source]
                seen[source] = slot + 1

                @pl.when(counts)
                def _():
                    place = filled[x]
                    filled[x] = place + 1
                    plan[place * window + x] = source * 32 + slot

                return jnp.maximum(most, slot + 1)

            low = jnp.maximum(0, -shift - base)
            return lax.fori_loop(low, jnp.minimum(window, ncols - shift - base), column, most)

        most = lax.fori_loop(0, total, revisit, most)
    longest = lax.fori_loop(0, window, lambda x, n: jnp.maximum(n, filled[x]), jnp.int32(0))
    counting = lax.fori_loop(
        0, total, lambda r, n: n + jnp.where(flags[0, r] != 0, 1, 0), jnp.int32(0)
    )
    plan[listed] = longest
    plan[listed + 1] = counting
    plan[listed + 2] = most


def weights_kernel(
    width,
    ncols,
    windows,
    moves,
    flags,
    norm1_gain,
    w_query,
    w_key,
    w_value,
    query_gain,
    key_gain,
    w_out,
    norm2_gain,
    w_in,
    conv_first,
    conv_second,
    w_qkv,
    w_mix,
    w_mlp,
    norm_gains,
    head_gains,
    w_first,
    w_second,
    plan,
    seen,
    filled,
):
    make_plan(width, ncols, windows, moves, flags, plan, seen, filled)
    chans, mlp = w_in.shape
    head = chans // HEADS
    pair = 8 // width
    rows = width * chans
    band = norm_gains.shape[2]
    row = iota((rows, chans), 0)
    channel = (div(row, 8 * head) * pair + rem(div(row, width), pair)) * head + rem(div(row, 8), head)
    picked = channel == iota((rows, chans), 1)
    pick = jnp.where(picked, 1.0, 0.0).astype(half)
    spread = rem(iota((chans, rows), 1), chans) == iota((chans, rows), 0)
    spread = jnp.where(spread, 1.0, 0.0).astype(half)
    same = div(iota((rows, rows), 1), chans) == rem(iota((rows, rows), 0), width)
    for n, weight in enumerate((w_query, w_key, w_value)):
        chosen = dot(pick, weight[...], ((1,), (1,))).astype(half)
        w_qkv[n * rows : (n + 1) * rows, :] = jnp.where(same, dot(chosen, spread), 0.0).astype(half)
    mixing = dot(w_out[...], pick, ((0,), (1,)))
    mixing = jnp.concatenate([mixing] * width, axis=0)
    same = rem(iota((rows, rows), 1), width) == div(iota((rows, rows), 0), chans)
    w_mix[...] = jnp.where(same, mixing, 0.0).astype(half)
    wide = dot(w_in[...], spread, ((0,), (0,)))
    wide = jnp.concatenate([wide] * width, axis=0)
    same = div(iota((width * mlp, rows), 0), mlp) == div(iota((width * mlp, rows), 1), chans)
    w_mlp[...] = jnp.where(same, wide, 0.0).astype(half)
    plain = iota((chans, chans), 0) == iota((chans, chans), 1)
    for n, gain in enumerate((norm1_gain, norm2_gain)):
        column = jnp.sum(jnp.where(plain, gain[...], 0.0), axis=1, keepdims=True)
        norm_gains[n] = jnp.broadcast_to(column, (chans, band))
    for n, gain in enumerate((query_gain, key_gain)):
        column = jnp.sum(jnp.where(picked, gain[...], 0.0), axis=1, keepdims=True)
        head_gains[n] = jnp.broadcast_to(column, (rows, band))
    for kernel, result in ((conv_first, w_first), (conv_second, w_second)):
        outs = kernel.shape[3]
        for down in range(3):
            total = jnp.zeros((outs, 3 * chans), f32)
            for across in range(3):
                place = iota((chans, 3 * chans), 1) == iota((chans, 3 * chans), 0) + across * chans
                place = jnp.where(place, 1.0, 0.0).astype(half)
                total += dot(kernel[across, down], place, ((0,), (0,)))
            result[down * outs : (down + 1) * outs, :] = total.astype(half)


def arrange(params, conv_first, conv_second, moves, flags, passes, ncols, band):
    chans, mlp = params[8].shape
    width = ncols // passes
    rows = width * chans
    total = flags.shape[1]
    sources = passes * ncols
    outs = -(-conv_second.shape[3] // 16) * 16
    padding = ((0, 0), (0, 0), (0, 0), (0, outs - conv_second.shape[3]))
    conv_second = jnp.pad(conv_second, padding)
    arrays = [p.reshape(1, -1) if p.ndim == 1 else p for p in params[:9]]
    arrays += [conv_first, conv_second]
    return pl.pallas_call(
        functools.partial(weights_kernel, width, ncols, passes // 2),
        out_shape=[
            jax.ShapeDtypeStruct((3 * rows, rows), half),
            jax.ShapeDtypeStruct((rows, rows), half),
            jax.ShapeDtypeStruct((width * mlp, rows), half),
            jax.ShapeDtypeStruct((2, chans, band), f32),
            jax.ShapeDtypeStruct((2, rows, band), f32),
            jax.ShapeDtypeStruct((3 * conv_first.shape[3], 3 * chans), half),
            jax.ShapeDtypeStruct((3 * outs, 3 * chans), half),
            jax.ShapeDtypeStruct(((total + 2) * 2 * width + 3,), jnp.int32),
        ],
        in_specs=[pl.BlockSpec(memory_space=SMEM)] * 2
        + [pl.BlockSpec(memory_space=VMEM)] * len(arrays),
        out_specs=[pl.BlockSpec(memory_space=VMEM)] * 7 + [pl.BlockSpec(memory_space=SMEM)],
        scratch_shapes=[
            pltpu.SMEM((sources,), jnp.int32),
            pltpu.SMEM((2 * width,), jnp.int32),
        ],
        compiler_params=pltpu.CompilerParams(vmem_limit_bytes=LIMIT),
        name="weights",
    )(moves, flags, *arrays)


def join_kernel(
    plan,
    parts,
    w_qkv,
    w_mix,
    w_mlp,
    norm_gains,
    head_gains,
    w_back,
    out,
    strip,
    tokens,
    queries,
    keys,
    values,
    weights,
    sum_hidden,
    sum_inner,
):
    sources, slots, part, band = parts.shape
    width, chans = out.shape[:2]
    mlp = w_mlp.shape[0] // width
    head = chans // HEADS
    rows = width * chans
    groups = HEADS * width // 8
    window = 2 * width
    listed = plan.shape[0] - 3
    found, counting = plan[listed], plan[listed + 1]
    blank = (counting - found).astype(f32)
    pairs = div(found + jnp.where(counting > found, 2, 1), 2)
    first_lanes = iota((part, band), 1) < band // 2
    side = here()[0]
    def scale(tile, gain):
        tile = tile.reshape(width, chans, 2 * band)
        mean = jnp.mean(tile * tile, axis=1, keepdims=True)
        scaled = tile * lax.rsqrt(mean + eps) * jnp.concatenate([gain, gain], axis=1)
        return scaled.astype(half).reshape(rows, 2 * band)

    def heads_scale(tile, gain):
        square = jnp.sum(tile * tile, axis=0)
        square = square.reshape(8 // width, width, band)
        mean = jnp.sum(square, axis=0, keepdims=True) * (1.0 / chans)
        factor = jnp.broadcast_to(lax.rsqrt(mean + eps), (8 // width, width, band))
        factor = factor.reshape(1, 8, band)
        scaled = tile * factor * gain.reshape(tile.shape)
        return scaled.astype(half).astype(f32)

    def project(n, carry):
        for t in range(2):
            i = 2 * n + t
            lanes = slice(t * band, (t + 1) * band)

            def piece(x):
                entry = plan[i * window + x]
                held = jnp.maximum(entry, 0)
                source, slot = lax.shift_right_logical(held, 5), held & 31
                return jnp.where(entry >= 0, parts[source, slot].astype(f32), 0.0)

            for x in range(width):
                left, right = piece(x), piece(x + width)
                tokens[n, x * chans : x * chans + part, lanes] = jnp.where(
                    first_lanes, left, pltpu.roll(right, band // 2, 1)
                )
                tokens[n, x * chans + part : (x + 1) * chans, lanes] = jnp.where(
                    first_lanes, pltpu.roll(left, band // 2, 1), right
                )
        qkv = dot(w_qkv[...], scale(tokens[n], norm_gains[0]))
        tiles = (rows // 8, 8, band)
        for t in range(2):
            i = 2 * n + t
            one = qkv[:, t * band : (t + 1) * band]
            query = heads_scale(one[:rows].reshape(tiles), head_gains[0])
            queries[i] = query * (1.0 / float(head) ** 0.5)
            keys[i] = heads_scale(one[rows : 2 * rows].reshape(tiles), head_gains[1])
            values[i] = one[2 * rows :].reshape(tiles).astype(half).astype(f32)
        return carry

    lax.fori_loop(0, pairs, project, 0)
    sum_hidden[...] = jnp.zeros((rows, band), f32)
    sum_inner[...] = jnp.zeros((width * mlp, band), f32)

    def attend(n, carry):
        def score(s, norms):
            added = []
            for t in range(2):
                product = (queries[2 * n + t] * keys[s]).reshape(groups, head, 8, band)
                weight = jnp.exp(jnp.sum(product, axis=1))
                weights[t, s] = weight
                added.append(norms[t] + weight)
            return tuple(added)

        norm = jnp.zeros((groups, 8, band), f32) + blank
        norms = lax.fori_loop(0, found, score, (norm, norm))
        inverses = [1.0 / norm for norm in norms]
        mixed = []
        for g in range(groups):

            def mix(s, sums):
                value = values[s, g * head : (g + 1) * head]
                probs = [(weights[t, s, g] * inverses[t][g]).astype(half).astype(f32) for t in range(2)]
                return tuple(sums[t] + probs[t][None] * value for t in range(2))

            none = jnp.zeros((head, 8, band), f32)
            mixed.append(lax.fori_loop(0, found, mix, (none, none)))
        mixed = [
            jnp.concatenate([m[t].reshape(head * 8, band).astype(half) for m in mixed], axis=0)
            for t in range(2)
        ]
        hidden = tokens[n] + dot(w_mix[...], jnp.concatenate(mixed, axis=1))
        inner = dot(w_mlp[...], scale(hidden, norm_gains[1]))
        inner = jax.nn.gelu(inner, approximate=True).astype(half).astype(f32)
        rest = jnp.where(found == 2 * n, blank, 0.0)
        rest_after = jnp.where(found == 2 * n + 1, blank, 0.0)
        first_weight = jnp.where(2 * n < found, 1.0, rest)
        second_weight = jnp.where(2 * n + 1 < found, 1.0, rest_after)
        sum_hidden[...] += hidden[:, :band] * first_weight + hidden[:, band:] * second_weight
        sum_inner[...] += inner[:, :band] * first_weight + inner[:, band:] * second_weight
        return carry

    lax.fori_loop(0, pairs, attend, 0)
    inverse = 1.0 / counting.astype(f32)
    lane = iota((chans, band), 1)
    edges = jnp.zeros((chans, band), f32)
    taken = jnp.where(side == 0, 0, band // 2 - 2)
    for x in range(width):
        inner = sum_inner[x * mlp : (x + 1) * mlp, :]
        high = inner.astype(half)
        low = (inner - high.astype(f32)).astype(half)
        back = dot(w_back[...], jnp.concatenate([high, low], axis=1))
        sums = sum_hidden[x * chans : (x + 1) * chans, :] + back[:, :band] + back[:, band:]
        joined = (sums * inverse).astype(half)
        out[x] = joined
        joined = joined.astype(f32)
        for column, start in ((x, 0), (x + width, band // 2)):
            turn = rem(2 * column - start - taken + 2 * band, band)
            edges = jnp.where(div(lane, 2) == column, pltpu.roll(joined, turn, 1), edges)
    strip[...] = edges.astype(half)


def join(parts, plan, arranged, w_back, width):
    part, band = parts.shape[2:]
    chans, mlp = w_back.shape
    total = (plan.shape[0] - 3) // (2 * width) - 2
    rows = width * chans
    groups = HEADS * width // 8
    arrays = (parts, *arranged[:5], w_back)
    tiles = pltpu.VMEM((total + 2, rows // 8, 8, band), f32)
    return pl.pallas_call(
        join_kernel,
        out_shape=[
            jax.ShapeDtypeStruct((width, chans, band), half),
            jax.ShapeDtypeStruct((chans, band), half),
        ],
        in_specs=[pl.BlockSpec(memory_space=SMEM)]
        + [pl.BlockSpec(memory_space=VMEM)] * len(arrays),
        out_specs=[pl.BlockSpec(memory_space=VMEM)] * 2,
        scratch_shapes=[
            pltpu.VMEM((total // 2 + 1, rows, 2 * band), f32),
            tiles,
            tiles,
            tiles,
            pltpu.VMEM((2, total, groups, 8, band), f32),
            pltpu.VMEM((rows, band), f32),
            pltpu.VMEM((width * mlp, band), f32),
        ],
        compiler_params=pltpu.CompilerParams(vmem_limit_bytes=LIMIT),
        name="join",
    )(plan, *arrays)


def frame_columns(mine, theirs, far, w_first, wide, products):
    width, chans, band = mine.shape
    side = here()[0]
    own = div(iota((chans, band), 1), band // 2) == side

    def put(j, column):
        wide[j * chans : (j + 1) * chans, :] = column

    for j in range(width):
        first, second = mine[j].astype(f32), theirs[j].astype(f32)
        put(2 + j, jnp.where(own, first, pltpu.roll(second, band // 2, 1)).astype(half))

    def near(j):
        first, second = mine[j].astype(f32), theirs[j].astype(f32)
        return jnp.where(own, pltpu.roll(first, band // 2, 1), second).astype(half)

    @pl.when(side == 0)
    def _():
        for j in range(2):
            put(width + 2 + j, near(j))
            put(j, far(j))

    @pl.when(side == 1)
    def _():
        for j in range(2):
            put(j, near(width - 2 + j))
            put(width + 2 + j, far(j))

    for x in range(width + 2):
        products[x] = dot(w_first[...], wide[x * chans : (x + 3) * chans, :])


def frame_pair_kernel(mine, theirs, w_first, products, wide):
    none = jnp.zeros(mine.shape[1:], half)
    frame_columns(mine, theirs, lambda j: none, w_first, wide, products)


def frame_kernel(mine, theirs, w_first, far, products, strip_a, strip_b, wide):
    width, chans, band = mine.shape
    odd = rem(here()[2], 2)
    lane = iota((chans, band), 1)
    frame_columns(mine, theirs, lambda j: far[j], w_first, wide, products)
    low = jnp.zeros((chans, band), f32)
    high = low
    for j in range(width + 4):
        column = wide[j * chans : (j + 1) * chans, :].astype(f32)
        place = div(lane, 2) == j
        low = jnp.where(place, column if j == 0 else pltpu.roll(column, 2 * j, 1), low)
        high = jnp.where(place, pltpu.roll(column, 2 * j + 2, 1), high)
    strip_a[...] = jnp.where(odd == 0, high, low).astype(half)
    strip_b[...] = jnp.where(odd == 0, low, high).astype(half)


def frame(kernel, arrays):
    width, chans, band = arrays[0].shape
    strip = jax.ShapeDtypeStruct((chans, band), half)
    shapes = [jax.ShapeDtypeStruct((width + 2, 3 * chans, band), f32)]
    if kernel is frame_kernel:
        shapes += [strip, strip]
    return pl.pallas_call(
        kernel,
        out_shape=shapes,
        in_specs=[pl.BlockSpec(memory_space=VMEM)] * len(arrays),
        out_specs=[pl.BlockSpec(memory_space=VMEM)] * len(shapes),
        scratch_shapes=[pltpu.VMEM(((width + 4) * chans, band), half)],
        compiler_params=pltpu.CompilerParams(vmem_limit_bytes=LIMIT),
        name="frame",
    )(*arrays)


def decode_kernel(
    single, ncols, nrows, inner, strip_a, strip_b, w_first, w_second, out, wide, act
):
    chans, band = strip_a.shape
    outs, width = out.shape[:2]
    side, pair, index = here()
    odd = rem(index, 2)
    from_a, from_b = strip_a[...].astype(f32), strip_b[...].astype(f32)
    if single:
        turn = jnp.where(side == 0, 4, band + 4 - 2 * width)
        from_a, from_b = pltpu.roll(from_a, turn, 1), pltpu.roll(from_b, turn, 1)
    low_in_a = side == 1 if single else odd == 1
    low = jnp.where(low_in_a, from_a, from_b)
    high = jnp.where(low_in_a, from_b, from_a)
    lane = iota((chans, band), 1)
    for j in range(width + 4):
        after = high if j == 0 else pltpu.roll(high, band - 2 * j, 1)
        before = pltpu.roll(low, band - 2 - 2 * j, 1)
        edge = jnp.where(lane < 2, after, jnp.where(lane >= band - 2, before, 0.0))
        wide[j * chans : (j + 1) * chans, :] = edge.astype(half)

    def shifted(products, count):
        above, level, below = [products[n * count : (n + 1) * count] for n in range(3)]
        return pltpu.roll(above, 1, 1) + level + pltpu.roll(below, 2 * band - 1, 1)

    lane = iota((chans, 2 * band), 1)
    row = index * band + jnp.where(lane < band + band // 2, lane, lane - 2 * band)
    row_inside = (row >= 0) & (row < nrows)
    for x in range(width + 2):
        column = (2 * pair + side) * width + (x - 1)
        outer = dot(w_first[...], wide[x * chans : (x + 3) * chans, :])
        products = jnp.concatenate([inner[x], outer], axis=1)
        hidden = jax.nn.gelu(shifted(products, chans), approximate=True)
        inside = row_inside & (column >= 0) & (column < ncols)
        act[x * chans : (x + 1) * chans, :] = jnp.where(inside, hidden, 0.0).astype(half)
    for x in range(width):
        products = dot(w_second[...], act[x * chans : (x + 3) * chans, :])
        out[:, x, :] = shifted(products, products.shape[0] // 3)[:outs, :band]


def decode(single, arrays, outs, ncols, nrows):
    width = arrays[0].shape[0] - 2
    chans, band = arrays[1].shape
    out = pl.pallas_call(
        functools.partial(decode_kernel, single, ncols, nrows),
        out_shape=jax.ShapeDtypeStruct((outs, width, band), f32),
        in_specs=[pl.BlockSpec(memory_space=VMEM)] * len(arrays),
        out_specs=pl.BlockSpec(memory_space=VMEM),
        scratch_shapes=[
            pltpu.VMEM(((width + 4) * chans, band), half),
            pltpu.VMEM(((width + 2) * chans, 2 * band), half),
        ],
        compiler_params=pltpu.CompilerParams(vmem_limit_bytes=LIMIT),
        name="decode",
    )(*arrays)
    return jnp.transpose(out, (1, 0, 2))


def swap(values, axis, first):
    count = lax.axis_size(axis)
    pairs = [(i, i + 1) for i in range(first, count - 1, 2)]
    if not pairs:
        return jnp.zeros_like(values)
    return lax.ppermute(values, axis, pairs + [(b, a) for a, b in pairs])


def all_moves(moves):
    count = lax.axis_size("pass")
    me = lax.axis_index("pass")
    pieces = [moves]
    for step in range(1, count):
        pieces.append(lax.ppermute(moves, "pass", [(i, (i - step) % count) for i in range(count)]))
    start = rem(count - me, count) * moves.shape[1]
    return lax.dynamic_slice_in_dim(
        jnp.concatenate(pieces * 2, axis=1), start, count * moves.shape[1], 1
    )


def to_band(strip, other):
    tiles, passes, cores = [lax.axis_size(a) for a in ("tile", "pass", "row")]

    def index(band, side):
        return (band // cores) * passes * cores + side * cores + band % cores

    bands = tiles * cores
    pairs = [(index(b, 0), index(b - 1, other)) for b in range(1, bands)]
    pairs += [(index(b, 1), index(b + 1, 1 - other)) for b in range(bands - 1)]
    return lax.ppermute(strip, ("tile", "pass", "row"), pairs)


def local(revisits, shifts, flags, *weights):
    params, (conv_first, conv_second) = weights[:10], weights[10:]
    passes = lax.axis_size("pass")
    bands = lax.axis_size(("tile", "row"))
    count, per_device, chans, nrows = revisits.shape
    assert per_device == 1 and passes % 2 == 0 and count <= 32
    ncols = bands
    width = ncols // passes
    band = nrows // bands
    slots = min(SLOTS, count)
    first, moves = pack(revisits, shifts.T, passes, bands, ncols, slots)
    first = send(first)
    every = all_moves(moves)
    arranged = arrange(params, conv_first, conv_second, every, flags.T, passes, ncols, band)
    plan = arranged[7]

    outs = conv_second.shape[3]
    w_first, w_second = arranged[5:7]

    def finish(parts):
        joined, strip = join(parts, plan, arranged, params[9].T, width)
        theirs = swap(joined, "pass", 0)
        if passes == 2:
            strip_a, strip_b = to_band(strip, 0), to_band(strip, 1)
            (products,) = frame(frame_pair_kernel, (joined, theirs, w_first))
        else:
            side = rem(lax.axis_index("pass"), 2)
            first = jnp.where(side == 0, joined[:2], joined[-2:]).astype(f32)
            second = jnp.where(side == 0, theirs[:2], theirs[-2:]).astype(f32)
            own = div(jnp.arange(band, dtype=jnp.int32), band // 2) == side
            edge = jnp.where(own, first, jnp.roll(second, band // 2, -1)).astype(half)
            far = swap(edge, "pass", 1)
            products, strip_a, strip_b = frame(frame_kernel, (joined, theirs, w_first, far))
            strip_a, strip_b = swap(strip_a, ("tile", "row"), 0), swap(strip_b, ("tile", "row"), 1)
        arrays = (products, strip_a, strip_b, w_first, w_second)
        return decode(passes == 2, arrays, outs, ncols, nrows)

    if count <= slots:
        return finish(first)
    needed = plan[plan.shape[0] - 1]

    def more():
        held = jnp.zeros((first.shape[0], count) + first.shape[2:], half)
        held = lax.dynamic_update_slice_in_dim(held, first, 0, 1)

        def step(i, held):
            sent = send(pack(revisits, moves, passes, bands, ncols, 1, i)[0])
            return lax.dynamic_update_slice_in_dim(held, sent, i, 1)

        return finish(lax.fori_loop(slots, needed, step, held))

    return lax.cond(needed > slots, more, lambda: finish(first))


def solution(mesh):
    return jax.shard_map(
        local,
        mesh=mesh,
        in_specs=(
            P(("groups", "pass"), ("tile", "row"), None, None),
            P(("groups", "pass"), None),
            P("groups", ("tile", "row")),
        )
        + (P(),) * 12,
        out_specs=P(("groups", "pass"), None, ("tile", "row")),
        check_vma=False,
    )
```

```python
import functools

import jax
import jax.numpy as jnp
from jax import lax
from jax.experimental import pallas as pl
from jax.experimental.pallas import tpu as pltpu
from jax.sharding import PartitionSpec as P

HEADS = 4
eps = 1e-05
SLOTS = 3
AT_ONCE = 4
AFTER = 2
LIMIT = 48 * 1024 * 1024
PACK_LIMIT = 63 * 1024 * 1024
f32 = jnp.float32
half = jnp.bfloat16
SMEM = pltpu.MemorySpace.SMEM
VMEM = pltpu.MemorySpace.VMEM
HBM = pltpu.MemorySpace.HBM


def pack_kernel(window, ncols, first_slot, moves, revisits, *rest):
    if first_slot is None:
        base, out, moves_out, table, held, staged, sems, out_sems, echo_sem = rest
        first_slot = base[0]
    else:
        out, moves_out, table, held, staged, sems, out_sems, echo_sem = rest
    count = held.shape[0]
    chans, rows = held.shape[1:]
    bands, slots, part, band = out.shape[1:]
    mine = here()[2]
    read = pltpu.make_async_copy(moves, table, echo_sem.at[0])
    read.start()
    loads = [
        pltpu.make_async_copy(revisits.at[r, 0], held.at[r], sems.at[r]) for r in range(count)
    ]
    for load in loads:
        load.start()
    read.wait()
    echo = pltpu.make_async_copy(table, moves_out, echo_sem.at[1])
    echo.start()
    places = []
    for r in range(count):
        place = mine - table[1, r]
        inside = (place >= 0) & (place < ncols)
        owner = jnp.where(inside, lax.div(jnp.maximum(place, 0), jnp.int32(window)), -1)
        slot = jnp.int32(0) - first_slot
        for other, _, _ in places:
            slot = slot + jnp.where(other == owner, 1, 0)
        places.append((owner, slot, inside & (slot >= 0) & (slot < slots)))

    def writes(r):
        owner, slot, _ = places[r]
        return [
            pltpu.make_async_copy(
                staged.at[r, side], out.at[2 * owner + side, :, slot], out_sems.at[r, side]
            )
            for side in range(2)
        ]

    for r in range(count):
        loads[r].wait()

        @pl.when(places[r][2])
        def _():
            offset = table[0, r]
            turn = jnp.where(offset > 0, band - offset, -offset)
            lane = iota((16, band), 1)
            stays = (lane + offset >= 0) & (lane + offset < band)
            later = jnp.broadcast_to(offset > 0, (16, band))
            first = lane < band // 2
            none = jnp.zeros((16, band), f32)
            for c in range(0, part, 16):
                halves = []
                for low in (c, part + c):
                    turned = [
                        pltpu.roll(
                            held[r, low : low + 16, b * band : (b + 1) * band].astype(f32), turn, 1
                        )
                        for b in range(bands)
                    ]
                    turned = [none] + turned + [none]
                    halves.append(
                        [
                            jnp.where(
                                stays, turned[b + 1], jnp.where(later, turned[b + 2], turned[b])
                            )
                            for b in range(bands)
                        ]
                    )
                for b in range(bands):
                    top, bottom = halves[0][b], halves[1][b]
                    staged[r, 0, b, c : c + 16, :] = jnp.where(
                        first, top, pltpu.roll(bottom, band // 2, 1)
                    ).astype(half)
                    staged[r, 1, b, c : c + 16, :] = jnp.where(
                        first, pltpu.roll(top, band // 2, 1), bottom
                    ).astype(half)
            for write in writes(r):
                write.start()

    for r in range(count):

        @pl.when(places[r][2])
        def _():
            for write in writes(r):
                write.wait()

    echo.wait()


def pack(revisits, moves, passes, bands, ncols, slots, base=None):
    count, _, chans, rows = revisits.shape
    part, band = chans // 2, rows // bands
    first_slot = 0 if base is None else None
    scalars = [] if base is None else [base.reshape(1)]
    return pl.pallas_call(
        functools.partial(pack_kernel, 2 * ncols // passes, ncols, first_slot),
        out_shape=[
            jax.ShapeDtypeStruct((passes, bands, slots, part, band), half),
            jax.ShapeDtypeStruct(moves.shape, jnp.int32),
        ],
        in_specs=[pl.BlockSpec(memory_space=HBM)] * 2
        + [pl.BlockSpec(memory_space=SMEM)] * len(scalars),
        out_specs=[pl.BlockSpec(memory_space=HBM)] * 2,
        scratch_shapes=[
            pltpu.SMEM(moves.shape, jnp.int32),
            pltpu.VMEM((count, chans, rows), half),
            pltpu.VMEM((count, 2, bands, part, band), half),
            pltpu.SemaphoreType.DMA((count,)),
            pltpu.SemaphoreType.DMA((count, 2)),
            pltpu.SemaphoreType.DMA((2,)),
        ],
        compiler_params=pltpu.CompilerParams(vmem_limit_bytes=PACK_LIMIT),
        name="pack",
    )(moves, revisits, *scalars)


def send(packed):
    passes, bands, slots, part, band = packed.shape
    packed = packed.reshape(passes * bands, slots * part, band)
    sent = lax.all_to_all(packed, ("pass", "tile", "row"), 0, 0, tiled=True)
    return sent.reshape(passes * bands, slots, part, band)


def here():
    index = lax.axis_index("pass")
    band = lax.axis_index("tile") * lax.axis_size("row") + lax.axis_index("row")
    return rem(index, 2), div(index, 2), band


def iota(shape, dim):
    return lax.broadcasted_iota(jnp.int32, shape, dim)


def div(values, by):
    return lax.div(values, jnp.int32(by))


def rem(values, by):
    return lax.rem(values, jnp.int32(by))


def dot(a, b, dims=((1,), (0,))):
    return lax.dot_general(a, b, (dims, ((), ())), preferred_element_type=f32)


def make_plan(width, ncols, windows, moves, flags, plan, seen, filled):
    window = 2 * width
    total = flags.shape[1]
    sources = seen.shape[0]
    per = total // (sources // ncols)
    listed = (total + AT_ONCE + AFTER) * window

    def fill(ref, count, value):
        def one(i, carry):
            ref[i] = value
            return carry

        lax.fori_loop(0, count, one, 0)

    fill(plan, listed, jnp.int32(-1))
    fill(filled, window, jnp.int32(0))
    pair = here()[1]
    most = jnp.int32(0)
    for w in range(windows):
        base = w * window
        fill(seen, sources, jnp.int32(0))

        def revisit(r, most):
            shift = moves[1, r]
            counts = (flags[0, r] != 0) & (pair == w)
            first_source = div(r, per) * ncols + shift + base

            def column(x, most):
                source = first_source + x
                slot = seen[source]
                seen[source] = slot + 1

                @pl.when(counts)
                def _():
                    place = filled[x]
                    filled[x] = place + 1
                    plan[place * window + x] = source * 32 + slot

                return jnp.maximum(most, slot + 1)

            low = jnp.maximum(0, -shift - base)
            return lax.fori_loop(low, jnp.minimum(window, ncols - shift - base), column, most)

        most = lax.fori_loop(0, total, revisit, most)
    longest = lax.fori_loop(0, window, lambda x, n: jnp.maximum(n, filled[x]), jnp.int32(0))
    counting = lax.fori_loop(
        0, total, lambda r, n: n + jnp.where(flags[0, r] != 0, 1, 0), jnp.int32(0)
    )
    plan[listed] = longest
    plan[listed + 1] = counting
    plan[listed + 2] = most


def weights_kernel(
    width,
    ncols,
    windows,
    moves,
    flags,
    norm1_gain,
    w_query,
    w_key,
    w_value,
    query_gain,
    key_gain,
    w_out,
    norm2_gain,
    w_in,
    conv_first,
    conv_second,
    w_qkv,
    w_mix,
    w_mlp,
    norm_gains,
    head_gains,
    w_first,
    w_second,
    plan,
    seen,
    filled,
):
    make_plan(width, ncols, windows, moves, flags, plan, seen, filled)
    chans, mlp = w_in.shape
    head = chans // HEADS
    pair = 8 // width
    rows = width * chans
    band = head_gains.shape[2]
    row = iota((rows, chans), 0)
    channel = (div(row, 8 * head) * pair + rem(div(row, width), pair)) * head + rem(div(row, 8), head)
    picked = channel == iota((rows, chans), 1)
    pick = jnp.where(picked, 1.0, 0.0).astype(half)
    spread = rem(iota((chans, rows), 1), chans) == iota((chans, rows), 0)
    spread = jnp.where(spread, 1.0, 0.0).astype(half)
    same = div(iota((rows, rows), 1), chans) == rem(iota((rows, rows), 0), width)
    for n, weight in enumerate((w_query, w_key, w_value)):
        chosen = dot(pick, weight[...], ((1,), (1,))).astype(half)
        w_qkv[n * rows : (n + 1) * rows, :] = jnp.where(same, dot(chosen, spread), 0.0).astype(half)
    mixing = dot(w_out[...], pick, ((0,), (1,)))
    mixing = jnp.concatenate([mixing] * width, axis=0)
    same = rem(iota((rows, rows), 1), width) == div(iota((rows, rows), 0), chans)
    w_mix[...] = jnp.where(same, mixing, 0.0).astype(half)
    wide = dot(w_in[...], spread, ((0,), (0,)))
    wide = jnp.concatenate([wide] * width, axis=0)
    same = div(iota((width * mlp, rows), 0), mlp) == div(iota((width * mlp, rows), 1), chans)
    w_mlp[...] = jnp.where(same, wide, 0.0).astype(half)
    plain = iota((chans, chans), 0) == iota((chans, chans), 1)
    for n, gain in enumerate((norm1_gain, norm2_gain)):
        column = jnp.sum(jnp.where(plain, gain[...], 0.0), axis=1, keepdims=True)
        norm_gains[n] = jnp.broadcast_to(column, (chans, band))
    for n, gain in enumerate((query_gain, key_gain)):
        column = jnp.sum(jnp.where(picked, gain[...], 0.0), axis=1, keepdims=True)
        head_gains[n] = jnp.broadcast_to(column, (rows, band))
    for kernel, result in ((conv_first, w_first), (conv_second, w_second)):
        outs = kernel.shape[3]
        for down in range(3):
            total = jnp.zeros((outs, 3 * chans), f32)
            for across in range(3):
                place = iota((chans, 3 * chans), 1) == iota((chans, 3 * chans), 0) + across * chans
                place = jnp.where(place, 1.0, 0.0).astype(half)
                total += dot(kernel[across, down], place, ((0,), (0,)))
            result[down * outs : (down + 1) * outs, :] = total.astype(half)


def arrange(params, conv_first, conv_second, moves, flags, passes, ncols, band):
    chans, mlp = params[8].shape
    width = ncols // passes
    rows = width * chans
    total = flags.shape[1]
    sources = passes * ncols
    outs = -(-conv_second.shape[3] // 16) * 16
    padding = ((0, 0), (0, 0), (0, 0), (0, outs - conv_second.shape[3]))
    conv_second = jnp.pad(conv_second, padding)
    arrays = [p.reshape(1, -1) if p.ndim == 1 else p for p in params[:9]]
    arrays += [conv_first, conv_second]
    return pl.pallas_call(
        functools.partial(weights_kernel, width, ncols, passes // 2),
        out_shape=[
            jax.ShapeDtypeStruct((3 * rows, rows), half),
            jax.ShapeDtypeStruct((rows, rows), half),
            jax.ShapeDtypeStruct((width * mlp, rows), half),
            jax.ShapeDtypeStruct((2, chans, band), f32),
            jax.ShapeDtypeStruct((2, rows, band), f32),
            jax.ShapeDtypeStruct((3 * conv_first.shape[3], 3 * chans), half),
            jax.ShapeDtypeStruct((3 * outs, 3 * chans), half),
            jax.ShapeDtypeStruct(((total + AT_ONCE + AFTER) * 2 * width + 3,), jnp.int32),
        ],
        in_specs=[pl.BlockSpec(memory_space=SMEM)] * 2
        + [pl.BlockSpec(memory_space=VMEM)] * len(arrays),
        out_specs=[pl.BlockSpec(memory_space=VMEM)] * 7 + [pl.BlockSpec(memory_space=SMEM)],
        scratch_shapes=[
            pltpu.SMEM((sources,), jnp.int32),
            pltpu.SMEM((2 * width,), jnp.int32),
        ],
        compiler_params=pltpu.CompilerParams(vmem_limit_bytes=LIMIT),
        name="weights",
    )(moves, flags, *arrays)


def join_kernel(
    plan,
    parts,
    w_qkv,
    w_mix,
    w_mlp,
    norm_gains,
    head_gains,
    w_back,
    out,
    strip,
    tokens,
    queries,
    keys,
    values,
    weights,
    sum_hidden,
    sum_inner,
):
    sources, slots, part, band = parts.shape
    width, chans = out.shape[:2]
    mlp = w_mlp.shape[0] // width
    head = chans // HEADS
    rows = width * chans
    groups = HEADS * width // 8
    window = 2 * width
    listed = plan.shape[0] - 3
    found, counting = plan[listed], plan[listed + 1]
    steps = div(jnp.maximum(found - AT_ONCE, 0) + AFTER - 1, AFTER)
    blank = (counting - found).astype(f32)
    first_lanes = iota((part, band), 1) < band // 2
    side = here()[0]
    tiles = (rows // 8, 8, band)

    def scale(tile, gain):
        lanes = tile.shape[1]
        tile = tile.reshape(width, chans, lanes)
        mean = jnp.mean(tile * tile, axis=1, keepdims=True)
        tile = tile * lax.rsqrt(mean + eps) * side_by_side([gain] * (lanes // band))
        return tile.astype(half).reshape(rows, lanes)

    def head_scale(tile, gain):
        square = jnp.sum(tile * tile, axis=0).reshape(8 // width, width, band)
        mean = jnp.sum(square, axis=0, keepdims=True) * (1.0 / chans)
        factor = jnp.broadcast_to(lax.rsqrt(mean + eps), (8 // width, width, band))
        scaled = tile * factor.reshape(1, 8, band) * gain.reshape(tiles)
        return scaled.astype(half).astype(f32)

    def side_by_side(pieces):
        return jnp.concatenate(pieces, axis=1)

    def project(start, count):
        loaded = []
        for t in range(count):
            i = start + t

            def piece(x):
                entry = plan[i * window + x]
                held = jnp.maximum(entry, 0)
                source, slot = lax.shift_right_logical(held, 5), held & 31
                return jnp.where(entry >= 0, parts[source, slot].astype(f32), 0.0)

            columns = []
            for x in range(width):
                left, right = piece(x), piece(x + width)
                columns.append(jnp.where(first_lanes, left, pltpu.roll(right, band // 2, 1)))
                columns.append(jnp.where(first_lanes, pltpu.roll(left, band // 2, 1), right))
            token = jnp.concatenate(columns, axis=0)
            tokens[i] = token
            loaded.append(token)
        qkv = dot(w_qkv[...], scale(side_by_side(loaded), norm_gains[0]))
        for t in range(count):
            i = start + t
            one = qkv[:, t * band : (t + 1) * band]
            query, key, value = [one[n * rows : (n + 1) * rows].reshape(tiles) for n in range(3)]
            queries[i] = head_scale(query, head_gains[0]) * (1.0 / float(head) ** 0.5)
            keys[i] = head_scale(key, head_gains[1])
            values[i] = value.astype(half).astype(f32)

    def finish(hidden):
        inner = dot(w_mlp[...], scale(hidden, norm_gains[1]))
        return jax.nn.gelu(inner, approximate=True).astype(half)

    def add_up(array, count):
        total = array[:, :band]
        for t in range(1, count):
            total = total + array[:, t * band : (t + 1) * band]
        return total

    def attend(start, count, with_blank, held=None):
        def loop(body, start):
            if held is None:
                return lax.fori_loop(0, found, body, start)
            for s in range(held):
                start = body(s, start)
            return start

        def score(s, norms):
            added = []
            for t in range(count):
                product = (queries[start + t] * keys[s]).reshape(groups, head, 8, band)
                weight = jnp.exp(jnp.sum(product, axis=1))
                weights[t, s] = weight
                added.append(norms[t] + weight)
            return tuple(added)

        others = blank if held is None else (counting - held).astype(f32)
        norms = loop(score, (jnp.zeros((groups, 8, band), f32) + others,) * count)
        inverses = [1.0 / norm for norm in norms]
        mixed = [[] for _ in range(count)]
        none = jnp.zeros((head, 8, band), f32)
        for g in range(groups):
            for t in range(0, count, 2):

                def mix(s, sums):
                    value = values[s, g * head : (g + 1) * head]
                    probs = [weights[t + k, s, g] * inverses[t + k][g] for k in range(2)]
                    probs = [prob.astype(half).astype(f32) for prob in probs]
                    return tuple(sums[k] + probs[k][None] * value for k in range(2))

                sums = loop(mix, (none, none))
                for k in range(2):
                    mixed[t + k].append(sums[k].reshape(head * 8, band).astype(half))
        mixed = [jnp.concatenate(m, axis=0) for m in mixed]
        if with_blank:

            def gather(s, total):
                return total + values[s]

            prob = jnp.broadcast_to(1.0 / counting.astype(f32), (8, band)).astype(half).astype(f32)
            total = loop(gather, jnp.zeros(tiles, f32))
            mixed.append((total * prob[None]).reshape(rows, band).astype(half))
        hidden = dot(w_mix[...], side_by_side(mixed))
        own = [
            hidden[:, t * band : (t + 1) * band] + tokens[start + t] for t in range(count)
        ] + ([hidden[:, count * band :]] if with_blank else [])
        hidden = side_by_side(own)
        return hidden, finish(hidden)

    def first_tokens(count, held, padding):
        hidden, inner = attend(0, count, True, held)
        rest = blank - padding.astype(f32)
        inner = inner.astype(f32)
        sum_hidden[...] = add_up(hidden, count) + hidden[:, count * band :] * rest
        sum_inner[...] = add_up(inner, count) + inner[:, count * band :] * rest

    few = [2, AT_ONCE]
    for n, count in enumerate(few):

        @pl.when((found <= count) & (found > (few[n - 1] if n else -1)))
        def _():
            project(0, count)
            first_tokens(count, count, count - found)

    @pl.when(found > AT_ONCE)
    def _():
        project(0, AT_ONCE)

        def project_more(n, carry):
            project(AT_ONCE + AFTER * n, AFTER)
            return carry

        lax.fori_loop(0, steps, project_more, 0)
        first_tokens(AT_ONCE, None, AT_ONCE + AFTER * steps - found)

        def attend_more(n, carry):
            hidden, inner = attend(AT_ONCE + AFTER * n, AFTER, False)
            sum_hidden[...] += add_up(hidden, AFTER)
            sum_inner[...] += add_up(inner.astype(f32), AFTER)
            return carry

        lax.fori_loop(0, steps, attend_more, 0)

    inverse = 1.0 / counting.astype(f32)
    lane = iota((chans, band), 1)
    edges = jnp.zeros((chans, band), f32)
    taken = jnp.where(side == 0, 0, band // 2 - 2)
    for x in range(width):
        inner = sum_inner[x * mlp : (x + 1) * mlp, :]
        high = inner.astype(half)
        low = (inner - high.astype(f32)).astype(half)
        back = dot(w_back[...], jnp.concatenate([high, low], axis=1))
        sums = sum_hidden[x * chans : (x + 1) * chans, :] + back[:, :band] + back[:, band:]
        joined = (sums * inverse).astype(half)
        out[x] = joined
        joined = joined.astype(f32)
        for column, start in ((x, 0), (x + width, band // 2)):
            turn = rem(2 * column - start - taken + 2 * band, band)
            edges = jnp.where(div(lane, 2) == column, pltpu.roll(joined, turn, 1), edges)
    strip[...] = edges.astype(half)


def join(parts, plan, arranged, w_back, width):
    part, band = parts.shape[2:]
    chans, mlp = w_back.shape
    spaces = (plan.shape[0] - 3) // (2 * width)
    rows = width * chans
    groups = HEADS * width // 8
    arrays = (parts, *arranged[:5], w_back)
    tiles = pltpu.VMEM((spaces, rows // 8, 8, band), f32)
    return pl.pallas_call(
        join_kernel,
        out_shape=[
            jax.ShapeDtypeStruct((width, chans, band), half),
            jax.ShapeDtypeStruct((chans, band), half),
        ],
        in_specs=[pl.BlockSpec(memory_space=SMEM)]
        + [pl.BlockSpec(memory_space=VMEM)] * len(arrays),
        out_specs=[pl.BlockSpec(memory_space=VMEM)] * 2,
        scratch_shapes=[
            pltpu.VMEM((spaces, rows, band), f32),
            tiles,
            tiles,
            tiles,
            pltpu.VMEM((AT_ONCE, spaces, groups, 8, band), f32),
            pltpu.VMEM((rows, band), f32),
            pltpu.VMEM((width * mlp, band), f32),
        ],
        compiler_params=pltpu.CompilerParams(vmem_limit_bytes=LIMIT),
        name="join",
    )(plan, *arrays)


def frame_columns(mine, theirs, far, w_first, wide, products):
    width, chans, band = mine.shape
    side = here()[0]
    own = div(iota((chans, band), 1), band // 2) == side

    def put(j, column):
        wide[j * chans : (j + 1) * chans, :] = column

    for j in range(width):
        first, second = mine[j].astype(f32), theirs[j].astype(f32)
        put(2 + j, jnp.where(own, first, pltpu.roll(second, band // 2, 1)).astype(half))

    def near(j):
        first, second = mine[j].astype(f32), theirs[j].astype(f32)
        return jnp.where(own, pltpu.roll(first, band // 2, 1), second).astype(half)

    @pl.when(side == 0)
    def _():
        for j in range(2):
            put(width + 2 + j, near(j))
            put(j, far(j))

    @pl.when(side == 1)
    def _():
        for j in range(2):
            put(j, near(width - 2 + j))
            put(width + 2 + j, far(j))

    for x in range(width + 2):
        products[x] = dot(w_first[...], wide[x * chans : (x + 3) * chans, :])


def frame_pair_kernel(mine, theirs, w_first, products, wide):
    none = jnp.zeros(mine.shape[1:], half)
    frame_columns(mine, theirs, lambda j: none, w_first, wide, products)


def frame_kernel(mine, theirs, w_first, far, products, strip_a, strip_b, wide):
    width, chans, band = mine.shape
    odd = rem(here()[2], 2)
    lane = iota((chans, band), 1)
    frame_columns(mine, theirs, lambda j: far[j], w_first, wide, products)
    low = jnp.zeros((chans, band), f32)
    high = low
    for j in range(width + 4):
        column = wide[j * chans : (j + 1) * chans, :].astype(f32)
        place = div(lane, 2) == j
        low = jnp.where(place, column if j == 0 else pltpu.roll(column, 2 * j, 1), low)
        high = jnp.where(place, pltpu.roll(column, 2 * j + 2, 1), high)
    strip_a[...] = jnp.where(odd == 0, high, low).astype(half)
    strip_b[...] = jnp.where(odd == 0, low, high).astype(half)


def frame(kernel, arrays):
    width, chans, band = arrays[0].shape
    strip = jax.ShapeDtypeStruct((chans, band), half)
    shapes = [jax.ShapeDtypeStruct((width + 2, 3 * chans, band), f32)]
    if kernel is frame_kernel:
        shapes += [strip, strip]
    return pl.pallas_call(
        kernel,
        out_shape=shapes,
        in_specs=[pl.BlockSpec(memory_space=VMEM)] * len(arrays),
        out_specs=[pl.BlockSpec(memory_space=VMEM)] * len(shapes),
        scratch_shapes=[pltpu.VMEM(((width + 4) * chans, band), half)],
        compiler_params=pltpu.CompilerParams(vmem_limit_bytes=LIMIT),
        name="frame",
    )(*arrays)


def decode_kernel(
    single, ncols, nrows, inner, strip_a, strip_b, w_first, w_second, out, wide, act
):
    chans, band = strip_a.shape
    outs, width = out.shape[:2]
    side, pair, index = here()
    odd = rem(index, 2)
    from_a, from_b = strip_a[...].astype(f32), strip_b[...].astype(f32)
    if single:
        turn = jnp.where(side == 0, 4, band + 4 - 2 * width)
        from_a, from_b = pltpu.roll(from_a, turn, 1), pltpu.roll(from_b, turn, 1)
    low_in_a = side == 1 if single else odd == 1
    low = jnp.where(low_in_a, from_a, from_b)
    high = jnp.where(low_in_a, from_b, from_a)
    lane = iota((chans, band), 1)
    for j in range(width + 4):
        after = high if j == 0 else pltpu.roll(high, band - 2 * j, 1)
        before = pltpu.roll(low, band - 2 - 2 * j, 1)
        edge = jnp.where(lane < 2, after, jnp.where(lane >= band - 2, before, 0.0))
        wide[j * chans : (j + 1) * chans, :] = edge.astype(half)

    def shifted(products, count):
        above, level, below = [products[n * count : (n + 1) * count] for n in range(3)]
        return pltpu.roll(above, 1, 1) + level + pltpu.roll(below, 2 * band - 1, 1)

    lane = iota((chans, 2 * band), 1)
    row = index * band + jnp.where(lane < band + band // 2, lane, lane - 2 * band)
    row_inside = (row >= 0) & (row < nrows)
    for x in range(width + 2):
        column = (2 * pair + side) * width + (x - 1)
        outer = dot(w_first[...], wide[x * chans : (x + 3) * chans, :])
        products = jnp.concatenate([inner[x], outer], axis=1)
        hidden = jax.nn.gelu(shifted(products, chans), approximate=True)
        inside = row_inside & (column >= 0) & (column < ncols)
        act[x * chans : (x + 1) * chans, :] = jnp.where(inside, hidden, 0.0).astype(half)
    for x in range(width):
        products = dot(w_second[...], act[x * chans : (x + 3) * chans, :])
        out[:, x, :] = shifted(products, products.shape[0] // 3)[:outs, :band]


def decode(single, arrays, outs, ncols, nrows):
    width = arrays[0].shape[0] - 2
    chans, band = arrays[1].shape
    out = pl.pallas_call(
        functools.partial(decode_kernel, single, ncols, nrows),
        out_shape=jax.ShapeDtypeStruct((outs, width, band), f32),
        in_specs=[pl.BlockSpec(memory_space=VMEM)] * len(arrays),
        out_specs=pl.BlockSpec(memory_space=VMEM),
        scratch_shapes=[
            pltpu.VMEM(((width + 4) * chans, band), half),
            pltpu.VMEM(((width + 2) * chans, 2 * band), half),
        ],
        compiler_params=pltpu.CompilerParams(vmem_limit_bytes=LIMIT),
        name="decode",
    )(*arrays)
    return jnp.transpose(out, (1, 0, 2))


def swap(values, axis, first):
    count = lax.axis_size(axis)
    pairs = [(i, i + 1) for i in range(first, count - 1, 2)]
    if not pairs:
        return jnp.zeros_like(values)
    return lax.ppermute(values, axis, pairs + [(b, a) for a, b in pairs])


def all_moves(moves):
    count = lax.axis_size("pass")
    me = lax.axis_index("pass")
    pieces = [moves]
    for step in range(1, count):
        pieces.append(lax.ppermute(moves, "pass", [(i, (i - step) % count) for i in range(count)]))
    start = rem(count - me, count) * moves.shape[1]
    return lax.dynamic_slice_in_dim(
        jnp.concatenate(pieces * 2, axis=1), start, count * moves.shape[1], 1
    )


def to_band(strip, other):
    tiles, passes, cores = [lax.axis_size(a) for a in ("tile", "pass", "row")]

    def index(band, side):
        return (band // cores) * passes * cores + side * cores + band % cores

    bands = tiles * cores
    pairs = [(index(b, 0), index(b - 1, other)) for b in range(1, bands)]
    pairs += [(index(b, 1), index(b + 1, 1 - other)) for b in range(bands - 1)]
    return lax.ppermute(strip, ("tile", "pass", "row"), pairs)


def local(revisits, shifts, flags, *weights):
    params, (conv_first, conv_second) = weights[:10], weights[10:]
    passes = lax.axis_size("pass")
    bands = lax.axis_size(("tile", "row"))
    count, per_device, chans, nrows = revisits.shape
    assert per_device == 1 and passes % 2 == 0 and count <= 32
    ncols = bands
    width = ncols // passes
    band = nrows // bands
    slots = min(SLOTS, count)
    first, moves = pack(revisits, shifts.T, passes, bands, ncols, slots)
    first = send(first)
    every = all_moves(moves)
    arranged = arrange(params, conv_first, conv_second, every, flags.T, passes, ncols, band)
    plan = arranged[7]

    outs = conv_second.shape[3]
    w_first, w_second = arranged[5:7]

    def finish(parts):
        joined, strip = join(parts, plan, arranged, params[9].T, width)
        theirs = swap(joined, "pass", 0)
        if passes == 2:
            strip_a, strip_b = to_band(strip, 0), to_band(strip, 1)
            (products,) = frame(frame_pair_kernel, (joined, theirs, w_first))
        else:
            side = rem(lax.axis_index("pass"), 2)
            first = jnp.where(side == 0, joined[:2], joined[-2:]).astype(f32)
            second = jnp.where(side == 0, theirs[:2], theirs[-2:]).astype(f32)
            own = div(jnp.arange(band, dtype=jnp.int32), band // 2) == side
            edge = jnp.where(own, first, jnp.roll(second, band // 2, -1)).astype(half)
            far = swap(edge, "pass", 1)
            products, strip_a, strip_b = frame(frame_kernel, (joined, theirs, w_first, far))
            strip_a, strip_b = swap(strip_a, ("tile", "row"), 0), swap(strip_b, ("tile", "row"), 1)
        arrays = (products, strip_a, strip_b, w_first, w_second)
        return decode(passes == 2, arrays, outs, ncols, nrows)

    if count <= slots:
        return finish(first)
    needed = plan[plan.shape[0] - 1]

    def more():
        held = jnp.zeros((first.shape[0], count) + first.shape[2:], half)
        held = lax.dynamic_update_slice_in_dim(held, first, 0, 1)

        def step(i, held):
            sent = send(pack(revisits, moves, passes, bands, ncols, 1, i)[0])
            return lax.dynamic_update_slice_in_dim(held, sent, i, 1)

        return finish(lax.fori_loop(slots, needed, step, held))

    return lax.cond(needed > slots, more, lambda: finish(first))


def solution(mesh):
    return jax.shard_map(
        local,
        mesh=mesh,
        in_specs=(
            P(("groups", "pass"), ("tile", "row"), None, None),
            P(("groups", "pass"), None),
            P("groups", ("tile", "row")),
        )
        + (P(),) * 12,
        out_specs=P(("groups", "pass"), None, ("tile", "row")),
        check_vma=False,
    )
```

```python
import functools

import jax
import jax.numpy as jnp
from jax import lax
from jax.experimental import pallas as pl
from jax.experimental.pallas import tpu as pltpu
from jax.sharding import PartitionSpec as P

HEADS = 4
eps = 1e-05
SLOTS = 3
FEW = (2, 4, 6)
AFTER = 2
LIMIT = 48 * 1024 * 1024
PACK_LIMIT = 63 * 1024 * 1024
f32 = jnp.float32
half = jnp.bfloat16
SMEM = pltpu.MemorySpace.SMEM
VMEM = pltpu.MemorySpace.VMEM
HBM = pltpu.MemorySpace.HBM


def pack_kernel(window, ncols, first_slot, moves, revisits, *rest):
    if first_slot is None:
        base, out, moves_out, table, held, staged, sems, out_sems, echo_sem = rest
        first_slot = base[0]
    else:
        out, moves_out, table, held, staged, sems, out_sems, echo_sem = rest
    count = held.shape[0]
    chans, rows = held.shape[1:]
    bands, slots, part, band = out.shape[1:]
    mine = here()[2]
    read = pltpu.make_async_copy(moves, table, echo_sem.at[0])
    read.start()
    loads = [
        pltpu.make_async_copy(revisits.at[r, 0], held.at[r], sems.at[r]) for r in range(count)
    ]
    for load in loads:
        load.start()
    read.wait()
    echo = pltpu.make_async_copy(table, moves_out, echo_sem.at[1])
    echo.start()
    places = []
    for r in range(count):
        place = mine - table[1, r]
        inside = (place >= 0) & (place < ncols)
        owner = jnp.where(inside, lax.div(jnp.maximum(place, 0), jnp.int32(window)), -1)
        slot = jnp.int32(0) - first_slot
        for other, _, _ in places:
            slot = slot + jnp.where(other == owner, 1, 0)
        places.append((owner, slot, inside & (slot >= 0) & (slot < slots)))

    def writes(r):
        owner, slot, _ = places[r]
        return [
            pltpu.make_async_copy(
                staged.at[r, side], out.at[2 * owner + side, :, slot], out_sems.at[r, side]
            )
            for side in range(2)
        ]

    for r in range(count):
        loads[r].wait()

        @pl.when(places[r][2])
        def _():
            offset = table[0, r]
            turn = jnp.where(offset > 0, band - offset, -offset)
            lane = iota((16, band), 1)
            stays = (lane + offset >= 0) & (lane + offset < band)
            later = jnp.broadcast_to(offset > 0, (16, band))
            first = lane < band // 2
            none = jnp.zeros((16, band), f32)
            for c in range(0, part, 16):
                halves = []
                for low in (c, part + c):
                    turned = [
                        pltpu.roll(
                            held[r, low : low + 16, b * band : (b + 1) * band].astype(f32), turn, 1
                        )
                        for b in range(bands)
                    ]
                    turned = [none] + turned + [none]
                    halves.append(
                        [
                            jnp.where(
                                stays, turned[b + 1], jnp.where(later, turned[b + 2], turned[b])
                            )
                            for b in range(bands)
                        ]
                    )
                for b in range(bands):
                    top, bottom = halves[0][b], halves[1][b]
                    staged[r, 0, b, c : c + 16, :] = jnp.where(
                        first, top, pltpu.roll(bottom, band // 2, 1)
                    ).astype(half)
                    staged[r, 1, b, c : c + 16, :] = jnp.where(
                        first, pltpu.roll(top, band // 2, 1), bottom
                    ).astype(half)
            for write in writes(r):
                write.start()

    for r in range(count):

        @pl.when(places[r][2])
        def _():
            for write in writes(r):
                write.wait()

    echo.wait()


def pack(revisits, moves, passes, bands, ncols, slots, base=None):
    count, _, chans, rows = revisits.shape
    part, band = chans // 2, rows // bands
    first_slot = 0 if base is None else None
    scalars = [] if base is None else [base.reshape(1)]
    return pl.pallas_call(
        functools.partial(pack_kernel, 2 * ncols // passes, ncols, first_slot),
        out_shape=[
            jax.ShapeDtypeStruct((passes, bands, slots, part, band), half),
            jax.ShapeDtypeStruct(moves.shape, jnp.int32),
        ],
        in_specs=[pl.BlockSpec(memory_space=HBM)] * 2
        + [pl.BlockSpec(memory_space=SMEM)] * len(scalars),
        out_specs=[pl.BlockSpec(memory_space=HBM)] * 2,
        scratch_shapes=[
            pltpu.SMEM(moves.shape, jnp.int32),
            pltpu.VMEM((count, chans, rows), half),
            pltpu.VMEM((count, 2, bands, part, band), half),
            pltpu.SemaphoreType.DMA((count,)),
            pltpu.SemaphoreType.DMA((count, 2)),
            pltpu.SemaphoreType.DMA((2,)),
        ],
        compiler_params=pltpu.CompilerParams(vmem_limit_bytes=PACK_LIMIT),
        name="pack",
    )(moves, revisits, *scalars)


def send(packed):
    passes, bands, slots, part, band = packed.shape
    packed = packed.reshape(passes * bands, slots * part, band)
    sent = lax.all_to_all(packed, ("pass", "tile", "row"), 0, 0, tiled=True)
    return sent.reshape(passes * bands, slots, part, band)


def here():
    index = lax.axis_index("pass")
    band = lax.axis_index("tile") * lax.axis_size("row") + lax.axis_index("row")
    return rem(index, 2), div(index, 2), band


def iota(shape, dim):
    return lax.broadcasted_iota(jnp.int32, shape, dim)


def div(values, by):
    return lax.div(values, jnp.int32(by))


def rem(values, by):
    return lax.rem(values, jnp.int32(by))


def dot(a, b, dims=((1,), (0,))):
    return lax.dot_general(a, b, (dims, ((), ())), preferred_element_type=f32)


def plan_kernel(width, ncols, windows, moves, flags, plan, needed, seen, filled):
    window = 2 * width
    total = flags.shape[1]
    sources = seen.shape[0]
    per = total // (sources // ncols)
    listed = (total + FEW[-1] + AFTER) * window

    def fill(ref, count, value):
        def one(i, carry):
            for x in range(window):
                ref[i * window + x] = value
            return carry

        lax.fori_loop(0, count // window, one, 0)

    fill(plan, listed, jnp.int32(-1))
    fill(filled, window, jnp.int32(0))
    pair = here()[1]
    most = jnp.int32(0)
    for w in range(windows):
        base = w * window
        fill(seen, sources, jnp.int32(0))

        def revisit(r, most):
            shift = moves[1, r]
            counts = (flags[0, r] != 0) & (pair == w)
            first_source = div(r, per) * ncols + shift + base

            def column(x, most):
                source = first_source + x
                slot = seen[source]
                seen[source] = slot + 1

                @pl.when(counts)
                def _():
                    place = filled[x]
                    filled[x] = place + 1
                    plan[place * window + x] = source * 32 + slot

                return jnp.maximum(most, slot + 1)

            low = jnp.maximum(0, -shift - base)
            return lax.fori_loop(low, jnp.minimum(window, ncols - shift - base), column, most)

        most = lax.fori_loop(0, total, revisit, most)
    longest = lax.fori_loop(0, window, lambda x, n: jnp.maximum(n, filled[x]), jnp.int32(0))
    counting = lax.fori_loop(
        0, total, lambda r, n: n + jnp.where(flags[0, r] != 0, 1, 0), jnp.int32(0)
    )
    plan[listed] = longest
    plan[listed + 1] = counting
    needed[0] = most


def weights_kernel(
    width,
    norm1_gain,
    w_query,
    w_key,
    w_value,
    query_gain,
    key_gain,
    w_out,
    norm2_gain,
    w_in,
    conv_first,
    conv_second,
    w_qkv,
    w_mix,
    w_mlp,
    norm_gains,
    head_gains,
    w_first,
    w_second,
):
    chans, mlp = w_in.shape
    head = chans // HEADS
    pair = 8 // width
    rows = width * chans
    band = head_gains.shape[2]
    row = iota((rows, chans), 0)
    channel = (div(row, 8 * head) * pair + rem(div(row, width), pair)) * head + rem(div(row, 8), head)
    picked = channel == iota((rows, chans), 1)
    pick = jnp.where(picked, 1.0, 0.0).astype(half)
    spread = rem(iota((chans, rows), 1), chans) == iota((chans, rows), 0)
    spread = jnp.where(spread, 1.0, 0.0).astype(half)
    same = div(iota((rows, rows), 1), chans) == rem(iota((rows, rows), 0), width)
    for n, weight in enumerate((w_query, w_key, w_value)):
        chosen = dot(pick, weight[...], ((1,), (1,))).astype(half)
        w_qkv[n * rows : (n + 1) * rows, :] = jnp.where(same, dot(chosen, spread), 0.0).astype(half)
    mixing = dot(w_out[...], pick, ((0,), (1,)))
    mixing = jnp.concatenate([mixing] * width, axis=0)
    same = rem(iota((rows, rows), 1), width) == div(iota((rows, rows), 0), chans)
    w_mix[...] = jnp.where(same, mixing, 0.0).astype(half)
    wide = dot(w_in[...], spread, ((0,), (0,)))
    wide = jnp.concatenate([wide] * width, axis=0)
    same = div(iota((width * mlp, rows), 0), mlp) == div(iota((width * mlp, rows), 1), chans)
    w_mlp[...] = jnp.where(same, wide, 0.0).astype(half)
    plain = iota((chans, chans), 0) == iota((chans, chans), 1)
    for n, gain in enumerate((norm1_gain, norm2_gain)):
        column = jnp.sum(jnp.where(plain, gain[...], 0.0), axis=1, keepdims=True)
        norm_gains[n] = jnp.broadcast_to(column, (chans, band))
    for n, gain in enumerate((query_gain, key_gain)):
        column = jnp.sum(jnp.where(picked, gain[...], 0.0), axis=1, keepdims=True)
        head_gains[n] = jnp.broadcast_to(column, (rows, band))
    for kernel, result in ((conv_first, w_first), (conv_second, w_second)):
        outs = kernel.shape[3]
        for down in range(3):
            total = jnp.zeros((outs, 3 * chans), f32)
            for across in range(3):
                place = iota((chans, 3 * chans), 1) == iota((chans, 3 * chans), 0) + across * chans
                place = jnp.where(place, 1.0, 0.0).astype(half)
                total += dot(kernel[across, down], place, ((0,), (0,)))
            result[down * outs : (down + 1) * outs, :] = total.astype(half)


def arrange(params, conv_first, conv_second, width, band):
    chans, mlp = params[8].shape
    rows = width * chans
    outs = -(-conv_second.shape[3] // 16) * 16
    padding = ((0, 0), (0, 0), (0, 0), (0, outs - conv_second.shape[3]))
    conv_second = jnp.pad(conv_second, padding)
    arrays = [p.reshape(1, -1) if p.ndim == 1 else p for p in params[:9]]
    arrays += [conv_first, conv_second]
    return pl.pallas_call(
        functools.partial(weights_kernel, width),
        out_shape=[
            jax.ShapeDtypeStruct((3 * rows, rows), half),
            jax.ShapeDtypeStruct((rows, rows), half),
            jax.ShapeDtypeStruct((width * mlp, rows), half),
            jax.ShapeDtypeStruct((2, chans, band), f32),
            jax.ShapeDtypeStruct((2, rows, band), f32),
            jax.ShapeDtypeStruct((3 * conv_first.shape[3], 3 * chans), half),
            jax.ShapeDtypeStruct((3 * outs, 3 * chans), half),
        ],
        in_specs=[pl.BlockSpec(memory_space=VMEM)] * len(arrays),
        out_specs=[pl.BlockSpec(memory_space=VMEM)] * 7,
        compiler_params=pltpu.CompilerParams(vmem_limit_bytes=LIMIT),
        name="weights",
    )(*arrays)


def make_plan(moves, flags, passes, ncols):
    width = ncols // passes
    sources = passes * ncols
    spaces = flags.shape[1] + FEW[-1] + AFTER
    return pl.pallas_call(
        functools.partial(plan_kernel, width, ncols, passes // 2),
        out_shape=[
            jax.ShapeDtypeStruct((spaces * 2 * width + 2,), jnp.int32),
            jax.ShapeDtypeStruct((1,), jnp.int32),
        ],
        in_specs=[pl.BlockSpec(memory_space=SMEM)] * 2,
        out_specs=[pl.BlockSpec(memory_space=SMEM)] * 2,
        scratch_shapes=[
            pltpu.SMEM((sources,), jnp.int32),
            pltpu.SMEM((2 * width,), jnp.int32),
        ],
        name="plan",
    )(moves, flags)


def join_kernel(
    plan,
    parts,
    w_qkv,
    w_mix,
    w_mlp,
    norm_gains,
    head_gains,
    w_back,
    out,
    strip,
    tokens,
    queries,
    keys,
    values,
    weights,
    sum_hidden,
    sum_inner,
):
    sources, slots, part, band = parts.shape
    width, chans = out.shape[:2]
    mlp = w_mlp.shape[0] // width
    head = chans // HEADS
    rows = width * chans
    groups = HEADS * width // 8
    window = 2 * width
    listed = plan.shape[0] - 2
    found, counting = plan[listed], plan[listed + 1]
    steps = div(jnp.maximum(found - FEW[-1], 0) + AFTER - 1, AFTER)
    blank = (counting - found).astype(f32)
    first_lanes = iota((part, band), 1) < band // 2
    side = here()[0]
    tiles = (rows // 8, 8, band)

    def scale(tile, gain):
        lanes = tile.shape[1]
        tile = tile.reshape(width, chans, lanes)
        mean = jnp.mean(tile * tile, axis=1, keepdims=True)
        tile = tile * lax.rsqrt(mean + eps) * side_by_side([gain] * (lanes // band))
        return tile.astype(half).reshape(rows, lanes)

    def head_scale(tile, gain):
        square = jnp.sum(tile * tile, axis=0).reshape(8 // width, width, band)
        mean = jnp.sum(square, axis=0, keepdims=True) * (1.0 / chans)
        factor = jnp.broadcast_to(lax.rsqrt(mean + eps), (8 // width, width, band))
        scaled = tile * factor.reshape(1, 8, band) * gain.reshape(tiles)
        return scaled.astype(half).astype(f32)

    def side_by_side(pieces):
        return jnp.concatenate(pieces, axis=1)

    def project(start, count):
        loaded = []
        for t in range(count):
            i = start + t

            def piece(x):
                entry = plan[i * window + x]
                held = jnp.maximum(entry, 0)
                source, slot = lax.shift_right_logical(held, 5), held & 31
                return jnp.where(entry >= 0, parts[source, slot].astype(f32), 0.0)

            columns = []
            for x in range(width):
                left, right = piece(x), piece(x + width)
                columns.append(jnp.where(first_lanes, left, pltpu.roll(right, band // 2, 1)))
                columns.append(jnp.where(first_lanes, pltpu.roll(left, band // 2, 1), right))
            token = jnp.concatenate(columns, axis=0)
            tokens[i] = token
            loaded.append(token)
        qkv = dot(w_qkv[...], scale(side_by_side(loaded), norm_gains[0]))
        for t in range(count):
            i = start + t
            one = qkv[:, t * band : (t + 1) * band]
            query, key, value = [one[n * rows : (n + 1) * rows].reshape(tiles) for n in range(3)]
            queries[i] = head_scale(query, head_gains[0]) * (1.0 / float(head) ** 0.5)
            keys[i] = head_scale(key, head_gains[1])
            values[i] = value.astype(half).astype(f32)

    def finish(hidden):
        inner = dot(w_mlp[...], scale(hidden, norm_gains[1]))
        return jax.nn.gelu(inner, approximate=True).astype(half)

    def add_up(array, count):
        total = array[:, :band]
        for t in range(1, count):
            total = total + array[:, t * band : (t + 1) * band]
        return total

    def attend(start, count, with_blank, held=None):
        def loop(body, start):
            if held is None:
                return lax.fori_loop(0, found, body, start)
            for s in range(held):
                start = body(s, start)
            return start

        def score(s, norms):
            added = []
            for t in range(count):
                product = (queries[start + t] * keys[s]).reshape(groups, head, 8, band)
                weight = jnp.exp(jnp.sum(product, axis=1))
                weights[t, s] = weight
                added.append(norms[t] + weight)
            return tuple(added)

        others = blank if held is None else (counting - held).astype(f32)
        norms = loop(score, (jnp.zeros((groups, 8, band), f32) + others,) * count)
        inverses = [1.0 / norm for norm in norms]
        mixed = [[] for _ in range(count)]
        none = jnp.zeros((head, 8, band), f32)
        for g in range(groups):
            for t in range(0, count, 2):

                def mix(s, sums):
                    value = values[s, g * head : (g + 1) * head]
                    probs = [weights[t + k, s, g] * inverses[t + k][g] for k in range(2)]
                    probs = [prob.astype(half).astype(f32) for prob in probs]
                    return tuple(sums[k] + probs[k][None] * value for k in range(2))

                sums = loop(mix, (none, none))
                for k in range(2):
                    mixed[t + k].append(sums[k].reshape(head * 8, band).astype(half))
        mixed = [jnp.concatenate(m, axis=0) for m in mixed]
        if with_blank:

            def gather(s, total):
                return total + values[s]

            prob = jnp.broadcast_to(1.0 / counting.astype(f32), (8, band)).astype(half).astype(f32)
            total = loop(gather, jnp.zeros(tiles, f32))
            mixed.append((total * prob[None]).reshape(rows, band).astype(half))
        hidden = dot(w_mix[...], side_by_side(mixed))
        own = [
            hidden[:, t * band : (t + 1) * band] + tokens[start + t] for t in range(count)
        ] + ([hidden[:, count * band :]] if with_blank else [])
        hidden = side_by_side(own)
        return hidden, finish(hidden)

    def first_tokens(count, held, padding):
        hidden, inner = attend(0, count, True, held)
        rest = blank - padding.astype(f32)
        inner = inner.astype(f32)
        sum_hidden[...] = add_up(hidden, count) + hidden[:, count * band :] * rest
        sum_inner[...] = add_up(inner, count) + inner[:, count * band :] * rest

    for n, count in enumerate(FEW):

        @pl.when((found <= count) & (found > (FEW[n - 1] if n else -1)))
        def _():
            project(0, count)
            first_tokens(count, count, count - found)

    @pl.when(found > FEW[-1])
    def _():
        project(0, FEW[-1])

        def project_more(n, carry):
            project(FEW[-1] + AFTER * n, AFTER)
            return carry

        lax.fori_loop(0, steps, project_more, 0)
        first_tokens(FEW[-1], None, FEW[-1] + AFTER * steps - found)

        def attend_more(n, carry):
            hidden, inner = attend(FEW[-1] + AFTER * n, AFTER, False)
            sum_hidden[...] += add_up(hidden, AFTER)
            sum_inner[...] += add_up(inner.astype(f32), AFTER)
            return carry

        lax.fori_loop(0, steps, attend_more, 0)

    inverse = 1.0 / counting.astype(f32)
    lane = iota((chans, band), 1)
    edges = jnp.zeros((chans, band), f32)
    taken = jnp.where(side == 0, 0, band // 2 - 2)
    for x in range(width):
        inner = sum_inner[x * mlp : (x + 1) * mlp, :]
        high = inner.astype(half)
        low = (inner - high.astype(f32)).astype(half)
        back = dot(w_back[...], jnp.concatenate([high, low], axis=1))
        sums = sum_hidden[x * chans : (x + 1) * chans, :] + back[:, :band] + back[:, band:]
        joined = (sums * inverse).astype(half)
        out[x] = joined
        joined = joined.astype(f32)
        for column, start in ((x, 0), (x + width, band // 2)):
            turn = rem(2 * column - start - taken + 2 * band, band)
            edges = jnp.where(div(lane, 2) == column, pltpu.roll(joined, turn, 1), edges)
    strip[...] = edges.astype(half)


def join(parts, plan, arranged, w_back, width):
    part, band = parts.shape[2:]
    chans, mlp = w_back.shape
    spaces = (plan.shape[0] - 2) // (2 * width)
    rows = width * chans
    groups = HEADS * width // 8
    arrays = (parts, *arranged[:5], w_back)
    tiles = pltpu.VMEM((spaces, rows // 8, 8, band), f32)
    return pl.pallas_call(
        join_kernel,
        out_shape=[
            jax.ShapeDtypeStruct((width, chans, band), half),
            jax.ShapeDtypeStruct((chans, band), half),
        ],
        in_specs=[pl.BlockSpec(memory_space=SMEM)]
        + [pl.BlockSpec(memory_space=VMEM)] * len(arrays),
        out_specs=[pl.BlockSpec(memory_space=VMEM)] * 2,
        scratch_shapes=[
            pltpu.VMEM((spaces, rows, band), f32),
            tiles,
            tiles,
            tiles,
            pltpu.VMEM((FEW[-1], spaces, groups, 8, band), f32),
            pltpu.VMEM((rows, band), f32),
            pltpu.VMEM((width * mlp, band), f32),
        ],
        compiler_params=pltpu.CompilerParams(vmem_limit_bytes=LIMIT),
        name="join",
    )(plan, *arrays)


def frame_columns(mine, theirs, far, w_first, wide, products):
    width, chans, band = mine.shape
    side = here()[0]
    own = div(iota((chans, band), 1), band // 2) == side

    def put(j, column):
        wide[j * chans : (j + 1) * chans, :] = column

    for j in range(width):
        first, second = mine[j].astype(f32), theirs[j].astype(f32)
        put(2 + j, jnp.where(own, first, pltpu.roll(second, band // 2, 1)).astype(half))

    def near(j):
        first, second = mine[j].astype(f32), theirs[j].astype(f32)
        return jnp.where(own, pltpu.roll(first, band // 2, 1), second).astype(half)

    @pl.when(side == 0)
    def _():
        for j in range(2):
            put(width + 2 + j, near(j))
            put(j, far(j))

    @pl.when(side == 1)
    def _():
        for j in range(2):
            put(j, near(width - 2 + j))
            put(width + 2 + j, far(j))

    for x in range(width + 2):
        products[x] = dot(w_first[...], wide[x * chans : (x + 3) * chans, :])


def frame_pair_kernel(mine, theirs, w_first, products, wide):
    none = jnp.zeros(mine.shape[1:], half)
    frame_columns(mine, theirs, lambda j: none, w_first, wide, products)


def frame_kernel(mine, theirs, w_first, far, products, strip_a, strip_b, wide):
    width, chans, band = mine.shape
    odd = rem(here()[2], 2)
    lane = iota((chans, band), 1)
    frame_columns(mine, theirs, lambda j: far[j], w_first, wide, products)
    low = jnp.zeros((chans, band), f32)
    high = low
    for j in range(width + 4):
        column = wide[j * chans : (j + 1) * chans, :].astype(f32)
        place = div(lane, 2) == j
        low = jnp.where(place, column if j == 0 else pltpu.roll(column, 2 * j, 1), low)
        high = jnp.where(place, pltpu.roll(column, 2 * j + 2, 1), high)
    strip_a[...] = jnp.where(odd == 0, high, low).astype(half)
    strip_b[...] = jnp.where(odd == 0, low, high).astype(half)


def frame(kernel, arrays):
    width, chans, band = arrays[0].shape
    strip = jax.ShapeDtypeStruct((chans, band), half)
    shapes = [jax.ShapeDtypeStruct((width + 2, 3 * chans, band), f32)]
    if kernel is frame_kernel:
        shapes += [strip, strip]
    return pl.pallas_call(
        kernel,
        out_shape=shapes,
        in_specs=[pl.BlockSpec(memory_space=VMEM)] * len(arrays),
        out_specs=[pl.BlockSpec(memory_space=VMEM)] * len(shapes),
        scratch_shapes=[pltpu.VMEM(((width + 4) * chans, band), half)],
        compiler_params=pltpu.CompilerParams(vmem_limit_bytes=LIMIT),
        name="frame",
    )(*arrays)


def decode_kernel(
    single, ncols, nrows, inner, strip_a, strip_b, w_first, w_second, out, wide, act
):
    chans, band = strip_a.shape
    outs, width = out.shape[:2]
    side, pair, index = here()
    odd = rem(index, 2)
    from_a, from_b = strip_a[...].astype(f32), strip_b[...].astype(f32)
    if single:
        turn = jnp.where(side == 0, 4, band + 4 - 2 * width)
        from_a, from_b = pltpu.roll(from_a, turn, 1), pltpu.roll(from_b, turn, 1)
    low_in_a = side == 1 if single else odd == 1
    low = jnp.where(low_in_a, from_a, from_b)
    high = jnp.where(low_in_a, from_b, from_a)
    lane = iota((chans, band), 1)
    for j in range(width + 4):
        after = high if j == 0 else pltpu.roll(high, band - 2 * j, 1)
        before = pltpu.roll(low, band - 2 - 2 * j, 1)
        edge = jnp.where(lane < 2, after, jnp.where(lane >= band - 2, before, 0.0))
        wide[j * chans : (j + 1) * chans, :] = edge.astype(half)

    def shifted(products, count):
        above, level, below = [products[n * count : (n + 1) * count] for n in range(3)]
        return pltpu.roll(above, 1, 1) + level + pltpu.roll(below, 2 * band - 1, 1)

    lane = iota((chans, 2 * band), 1)
    row = index * band + jnp.where(lane < band + band // 2, lane, lane - 2 * band)
    row_inside = (row >= 0) & (row < nrows)
    for x in range(width + 2):
        column = (2 * pair + side) * width + (x - 1)
        outer = dot(w_first[...], wide[x * chans : (x + 3) * chans, :])
        products = jnp.concatenate([inner[x], outer], axis=1)
        hidden = jax.nn.gelu(shifted(products, chans), approximate=True)
        inside = row_inside & (column >= 0) & (column < ncols)
        act[x * chans : (x + 1) * chans, :] = jnp.where(inside, hidden, 0.0).astype(half)
    for x in range(width):
        products = dot(w_second[...], act[x * chans : (x + 3) * chans, :])
        out[:, x, :] = shifted(products, products.shape[0] // 3)[:outs, :band]


def decode(single, arrays, outs, ncols, nrows):
    width = arrays[0].shape[0] - 2
    chans, band = arrays[1].shape
    out = pl.pallas_call(
        functools.partial(decode_kernel, single, ncols, nrows),
        out_shape=jax.ShapeDtypeStruct((outs, width, band), f32),
        in_specs=[pl.BlockSpec(memory_space=VMEM)] * len(arrays),
        out_specs=pl.BlockSpec(memory_space=VMEM),
        scratch_shapes=[
            pltpu.VMEM(((width + 4) * chans, band), half),
            pltpu.VMEM(((width + 2) * chans, 2 * band), half),
        ],
        compiler_params=pltpu.CompilerParams(vmem_limit_bytes=LIMIT),
        name="decode",
    )(*arrays)
    return jnp.transpose(out, (1, 0, 2))


def swap(values, axis, first):
    count = lax.axis_size(axis)
    pairs = [(i, i + 1) for i in range(first, count - 1, 2)]
    if not pairs:
        return jnp.zeros_like(values)
    return lax.ppermute(values, axis, pairs + [(b, a) for a, b in pairs])


def all_moves(moves):
    count = lax.axis_size("pass")
    me = lax.axis_index("pass")
    pieces = [moves]
    for step in range(1, count):
        pieces.append(lax.ppermute(moves, "pass", [(i, (i - step) % count) for i in range(count)]))
    start = rem(count - me, count) * moves.shape[1]
    return lax.dynamic_slice_in_dim(
        jnp.concatenate(pieces * 2, axis=1), start, count * moves.shape[1], 1
    )


def to_band(strip, other):
    tiles, passes, cores = [lax.axis_size(a) for a in ("tile", "pass", "row")]

    def index(band, side):
        return (band // cores) * passes * cores + side * cores + band % cores

    bands = tiles * cores
    pairs = [(index(b, 0), index(b - 1, other)) for b in range(1, bands)]
    pairs += [(index(b, 1), index(b + 1, 1 - other)) for b in range(bands - 1)]
    return lax.ppermute(strip, ("tile", "pass", "row"), pairs)


def local(revisits, shifts, flags, *weights):
    params, (conv_first, conv_second) = weights[:10], weights[10:]
    passes = lax.axis_size("pass")
    bands = lax.axis_size(("tile", "row"))
    count, per_device, chans, nrows = revisits.shape
    assert per_device == 1 and passes % 2 == 0 and count <= 32
    ncols = bands
    width = ncols // passes
    band = nrows // bands
    slots = min(SLOTS, count)
    first, moves = pack(revisits, shifts.T, passes, bands, ncols, slots)
    first = send(first)
    every = all_moves(moves)
    arranged = arrange(params, conv_first, conv_second, width, band)
    plan, needed = make_plan(every, flags.T, passes, ncols)
    needed = needed[0]

    outs = conv_second.shape[3]
    w_first, w_second = arranged[5:7]

    def finish(parts):
        joined, strip = join(parts, plan, arranged, params[9].T, width)
        side = rem(lax.axis_index("pass"), 2)
        theirs = swap(joined, "pass", 0)
        if passes == 2:
            strip_a, strip_b = to_band(strip, 0), to_band(strip, 1)
            (products,) = frame(frame_pair_kernel, (joined, theirs, w_first))
        else:
            first = jnp.where(side == 0, joined[:2], joined[-2:]).astype(f32)
            second = jnp.where(side == 0, theirs[:2], theirs[-2:]).astype(f32)
            own = div(jnp.arange(band, dtype=jnp.int32), band // 2) == side
            edge = jnp.where(own, first, jnp.roll(second, band // 2, -1)).astype(half)
            far = swap(edge, "pass", 1)
            products, strip_a, strip_b = frame(frame_kernel, (joined, theirs, w_first, far))
            strip_a, strip_b = swap(strip_a, ("tile", "row"), 0), swap(strip_b, ("tile", "row"), 1)
        arrays = (products, strip_a, strip_b, w_first, w_second)
        return decode(passes == 2, arrays, outs, ncols, nrows)

    if count <= slots:
        return finish(first)

    def more():
        held = jnp.zeros((first.shape[0], count) + first.shape[2:], half)
        held = lax.dynamic_update_slice_in_dim(held, first, 0, 1)

        def step(i, held):
            sent = send(pack(revisits, moves, passes, bands, ncols, 1, i)[0])
            return lax.dynamic_update_slice_in_dim(held, sent, i, 1)

        return finish(lax.fori_loop(slots, needed, step, held))

    return lax.cond(needed > slots, more, lambda: finish(first))


def solution(mesh):
    return jax.shard_map(
        local,
        mesh=mesh,
        in_specs=(
            P(("groups", "pass"), ("tile", "row"), None, None),
            P(("groups", "pass"), None),
            P("groups", ("tile", "row")),
        )
        + (P(),) * 12,
        out_specs=P(("groups", "pass"), None, ("tile", "row")),
        check_vma=False,
    )
```

```python
import functools

import jax
import jax.numpy as jnp
from jax import lax
from jax.experimental import pallas as pl
from jax.experimental.pallas import tpu as pltpu
from jax.sharding import PartitionSpec as P

HEADS = 4
eps = 1e-05
SLOTS = 3
FEW = (2, 4, 6)
AFTER = 2
LIMIT = 48 * 1024 * 1024
PACK_LIMIT = 63 * 1024 * 1024
f32 = jnp.float32
half = jnp.bfloat16
SMEM = pltpu.MemorySpace.SMEM
VMEM = pltpu.MemorySpace.VMEM
HBM = pltpu.MemorySpace.HBM


def pack_kernel(window, ncols, first_slot, moves, revisits, *rest):
    if first_slot is None:
        base, out, moves_out, table, held, staged, sems, out_sems, echo_sem = rest
        first_slot = base[0]
    else:
        out, moves_out, table, held, staged, sems, out_sems, echo_sem = rest
    count = held.shape[0]
    chans, rows = held.shape[1:]
    bands, slots, part, band = out.shape[1:]
    mine = here()[2]
    read = pltpu.make_async_copy(moves, table, echo_sem.at[0])
    read.start()
    loads = [
        pltpu.make_async_copy(revisits.at[r, 0], held.at[r], sems.at[r]) for r in range(count)
    ]
    for load in loads:
        load.start()
    read.wait()
    echo = pltpu.make_async_copy(table, moves_out, echo_sem.at[1])
    echo.start()
    places = []
    for r in range(count):
        place = mine - table[1, r]
        inside = (place >= 0) & (place < ncols)
        owner = jnp.where(inside, lax.div(jnp.maximum(place, 0), jnp.int32(window)), -1)
        slot = jnp.int32(0) - first_slot
        for other, _, _ in places:
            slot = slot + jnp.where(other == owner, 1, 0)
        places.append((owner, slot, inside & (slot >= 0) & (slot < slots)))

    def writes(r):
        owner, slot, _ = places[r]
        return [
            pltpu.make_async_copy(
                staged.at[r, side], out.at[2 * owner + side, :, slot], out_sems.at[r, side]
            )
            for side in range(2)
        ]

    for r in range(count):
        loads[r].wait()

        @pl.when(places[r][2])
        def _():
            offset = table[0, r]
            turn = jnp.where(offset > 0, band - offset, -offset)
            lane = iota((16, band), 1)
            stays = (lane + offset >= 0) & (lane + offset < band)
            later = jnp.broadcast_to(offset > 0, (16, band))
            first = lane < band // 2
            none = jnp.zeros((16, band), f32)
            for c in range(0, part, 16):
                halves = []
                for low in (c, part + c):
                    turned = [
                        pltpu.roll(
                            held[r, low : low + 16, b * band : (b + 1) * band].astype(f32), turn, 1
                        )
                        for b in range(bands)
                    ]
                    turned = [none] + turned + [none]
                    halves.append(
                        [
                            jnp.where(
                                stays, turned[b + 1], jnp.where(later, turned[b + 2], turned[b])
                            )
                            for b in range(bands)
                        ]
                    )
                for b in range(bands):
                    top, bottom = halves[0][b], halves[1][b]
                    staged[r, 0, b, c : c + 16, :] = jnp.where(
                        first, top, pltpu.roll(bottom, band // 2, 1)
                    ).astype(half)
                    staged[r, 1, b, c : c + 16, :] = jnp.where(
                        first, pltpu.roll(top, band // 2, 1), bottom
                    ).astype(half)
            for write in writes(r):
                write.start()

    for r in range(count):

        @pl.when(places[r][2])
        def _():
            for write in writes(r):
                write.wait()

    echo.wait()


def pack(revisits, moves, passes, bands, ncols, slots, base=None):
    count, _, chans, rows = revisits.shape
    part, band = chans // 2, rows // bands
    first_slot = 0 if base is None else None
    scalars = [] if base is None else [base.reshape(1)]
    return pl.pallas_call(
        functools.partial(pack_kernel, 2 * ncols // passes, ncols, first_slot),
        out_shape=[
            jax.ShapeDtypeStruct((passes, bands, slots, part, band), half),
            jax.ShapeDtypeStruct(moves.shape, jnp.int32),
        ],
        in_specs=[pl.BlockSpec(memory_space=HBM)] * 2
        + [pl.BlockSpec(memory_space=SMEM)] * len(scalars),
        out_specs=[pl.BlockSpec(memory_space=HBM)] * 2,
        scratch_shapes=[
            pltpu.SMEM(moves.shape, jnp.int32),
            pltpu.VMEM((count, chans, rows), half),
            pltpu.VMEM((count, 2, bands, part, band), half),
            pltpu.SemaphoreType.DMA((count,)),
            pltpu.SemaphoreType.DMA((count, 2)),
            pltpu.SemaphoreType.DMA((2,)),
        ],
        compiler_params=pltpu.CompilerParams(vmem_limit_bytes=PACK_LIMIT),
        name="pack",
    )(moves, revisits, *scalars)


def send(packed):
    passes, bands, slots, part, band = packed.shape
    packed = packed.reshape(passes * bands, slots * part, band)
    sent = lax.all_to_all(packed, ("pass", "tile", "row"), 0, 0, tiled=True)
    return sent.reshape(passes * bands, slots, part, band)


def here():
    index = lax.axis_index("pass")
    band = lax.axis_index("tile") * lax.axis_size("row") + lax.axis_index("row")
    return rem(index, 2), div(index, 2), band


def iota(shape, dim):
    return lax.broadcasted_iota(jnp.int32, shape, dim)


def div(values, by):
    return lax.div(values, jnp.int32(by))


def rem(values, by):
    return lax.rem(values, jnp.int32(by))


def dot(a, b, dims=((1,), (0,))):
    return lax.dot_general(a, b, (dims, ((), ())), preferred_element_type=f32)


def plan_kernel(width, ncols, windows, moves, flags, plan, needed, seen, filled):
    window = 2 * width
    total = flags.shape[1]
    sources = seen.shape[0]
    per = total // (sources // ncols)
    listed = (total + FEW[-1] + AFTER) * window

    def fill(ref, count, value):
        def one(i, carry):
            for x in range(window):
                ref[i * window + x] = value
            return carry

        lax.fori_loop(0, count // window, one, 0)

    fill(plan, listed, jnp.int32(-1))
    fill(filled, window, jnp.int32(0))
    pair = here()[1]
    most = jnp.int32(0)
    for w in range(windows):
        base = w * window
        fill(seen, sources, jnp.int32(0))

        def revisit(r, most):
            shift = moves[1, r]
            counts = (flags[0, r] != 0) & (pair == w)
            first_source = div(r, per) * ncols + shift + base

            def column(x, most):
                source = first_source + x
                slot = seen[source]
                seen[source] = slot + 1

                @pl.when(counts)
                def _():
                    place = filled[x]
                    filled[x] = place + 1
                    plan[place * window + x] = source * 32 + slot

                return jnp.maximum(most, slot + 1)

            low = jnp.maximum(0, -shift - base)
            return lax.fori_loop(low, jnp.minimum(window, ncols - shift - base), column, most)

        most = lax.fori_loop(0, total, revisit, most)
    longest = lax.fori_loop(0, window, lambda x, n: jnp.maximum(n, filled[x]), jnp.int32(0))
    counting = lax.fori_loop(
        0, total, lambda r, n: n + jnp.where(flags[0, r] != 0, 1, 0), jnp.int32(0)
    )
    plan[listed] = longest
    plan[listed + 1] = counting
    needed[0] = most


def weights_kernel(
    width,
    norm1_gain,
    w_query,
    w_key,
    w_value,
    query_gain,
    key_gain,
    w_out,
    norm2_gain,
    w_in,
    conv_first,
    conv_second,
    w_qkv,
    w_mix,
    w_mlp,
    norm_gains,
    head_gains,
    w_first,
    w_second,
):
    chans, mlp = w_in.shape
    head = chans // HEADS
    pair = 8 // width
    rows = width * chans
    band = head_gains.shape[2]
    row = iota((rows, chans), 0)
    channel = (div(row, 8 * head) * pair + rem(div(row, width), pair)) * head + rem(div(row, 8), head)
    picked = channel == iota((rows, chans), 1)
    pick = jnp.where(picked, 1.0, 0.0).astype(half)
    spread = rem(iota((chans, rows), 1), chans) == iota((chans, rows), 0)
    spread = jnp.where(spread, 1.0, 0.0).astype(half)
    same = div(iota((rows, rows), 1), chans) == rem(iota((rows, rows), 0), width)
    for n, weight in enumerate((w_query, w_key, w_value)):
        chosen = dot(pick, weight[...], ((1,), (1,))).astype(half)
        w_qkv[n * rows : (n + 1) * rows, :] = jnp.where(same, dot(chosen, spread), 0.0).astype(half)
    mixing = dot(w_out[...], pick, ((0,), (1,)))
    mixing = jnp.concatenate([mixing] * width, axis=0)
    same = rem(iota((rows, rows), 1), width) == div(iota((rows, rows), 0), chans)
    w_mix[...] = jnp.where(same, mixing, 0.0).astype(half)
    wide = dot(w_in[...], spread, ((0,), (0,)))
    wide = jnp.concatenate([wide] * width, axis=0)
    same = div(iota((width * mlp, rows), 0), mlp) == div(iota((width * mlp, rows), 1), chans)
    w_mlp[...] = jnp.where(same, wide, 0.0).astype(half)
    plain = iota((chans, chans), 0) == iota((chans, chans), 1)
    for n, gain in enumerate((norm1_gain, norm2_gain)):
        column = jnp.sum(jnp.where(plain, gain[...], 0.0), axis=1, keepdims=True)
        norm_gains[n] = jnp.broadcast_to(column, (chans, band))
    for n, gain in enumerate((query_gain, key_gain)):
        column = jnp.sum(jnp.where(picked, gain[...], 0.0), axis=1, keepdims=True)
        head_gains[n] = jnp.broadcast_to(column, (rows, band))
    for kernel, result in ((conv_first, w_first), (conv_second, w_second)):
        outs = kernel.shape[3]
        for down in range(3):
            total = jnp.zeros((outs, 3 * chans), f32)
            for across in range(3):
                place = iota((chans, 3 * chans), 1) == iota((chans, 3 * chans), 0) + across * chans
                place = jnp.where(place, 1.0, 0.0).astype(half)
                total += dot(kernel[across, down], place, ((0,), (0,)))
            result[down * outs : (down + 1) * outs, :] = total.astype(half)


def arrange(params, conv_first, conv_second, width, band):
    chans, mlp = params[8].shape
    rows = width * chans
    outs = -(-conv_second.shape[3] // 16) * 16
    padding = ((0, 0), (0, 0), (0, 0), (0, outs - conv_second.shape[3]))
    conv_second = jnp.pad(conv_second, padding)
    arrays = [p.reshape(1, -1) if p.ndim == 1 else p for p in params[:9]]
    arrays += [conv_first, conv_second]
    return pl.pallas_call(
        functools.partial(weights_kernel, width),
        out_shape=[
            jax.ShapeDtypeStruct((3 * rows, rows), half),
            jax.ShapeDtypeStruct((rows, rows), half),
            jax.ShapeDtypeStruct((width * mlp, rows), half),
            jax.ShapeDtypeStruct((2, chans, band), f32),
            jax.ShapeDtypeStruct((2, rows, band), f32),
            jax.ShapeDtypeStruct((3 * conv_first.shape[3], 3 * chans), half),
            jax.ShapeDtypeStruct((3 * outs, 3 * chans), half),
        ],
        in_specs=[pl.BlockSpec(memory_space=VMEM)] * len(arrays),
        out_specs=[pl.BlockSpec(memory_space=VMEM)] * 7,
        compiler_params=pltpu.CompilerParams(vmem_limit_bytes=LIMIT),
        name="weights",
    )(*arrays)


def make_plan(moves, flags, passes, ncols):
    width = ncols // passes
    sources = passes * ncols
    spaces = flags.shape[1] + FEW[-1] + AFTER
    return pl.pallas_call(
        functools.partial(plan_kernel, width, ncols, passes // 2),
        out_shape=[
            jax.ShapeDtypeStruct((spaces * 2 * width + 2,), jnp.int32),
            jax.ShapeDtypeStruct((1,), jnp.int32),
        ],
        in_specs=[pl.BlockSpec(memory_space=SMEM)] * 2,
        out_specs=[pl.BlockSpec(memory_space=SMEM)] * 2,
        scratch_shapes=[
            pltpu.SMEM((sources,), jnp.int32),
            pltpu.SMEM((2 * width,), jnp.int32),
        ],
        name="plan",
    )(moves, flags)


def join_kernel(
    lists,
    parts,
    w_qkv,
    w_mix,
    w_mlp,
    norm_gains,
    head_gains,
    w_back,
    out,
    strip,
    plan,
    plan_sem,
    tokens,
    queries,
    keys,
    values,
    weights,
    sum_hidden,
    sum_inner,
):
    sources, slots, part, band = parts.shape
    width, chans = out.shape[:2]
    mlp = w_mlp.shape[0] // width
    head = chans // HEADS
    rows = width * chans
    groups = HEADS * width // 8
    window = 2 * width
    listed = lists.shape[1] - 2
    seen = lists[...]
    found, counting = seen[0, listed], seen[0, listed + 1]
    steps = div(jnp.maximum(found - FEW[-1], 0) + AFTER - 1, AFTER)
    blank = (counting - found).astype(f32)
    first_lanes = iota((part, band), 1) < band // 2
    side = here()[0]
    tiles = (rows // 8, 8, band)

    def scale(tile, gain):
        lanes = tile.shape[1]
        tile = tile.reshape(width, chans, lanes)
        mean = jnp.mean(tile * tile, axis=1, keepdims=True)
        tile = tile * lax.rsqrt(mean + eps) * side_by_side([gain] * (lanes // band))
        return tile.astype(half).reshape(rows, lanes)

    def head_scale(tile, gain):
        square = jnp.sum(tile * tile, axis=0).reshape(8 // width, width, band)
        mean = jnp.sum(square, axis=0, keepdims=True) * (1.0 / chans)
        factor = jnp.broadcast_to(lax.rsqrt(mean + eps), (8 // width, width, band))
        scaled = tile * factor.reshape(1, 8, band) * gain.reshape(tiles)
        return scaled.astype(half).astype(f32)

    def side_by_side(pieces):
        return jnp.concatenate(pieces, axis=1)

    def project(start, count, entry_of):
        loaded = []
        for t in range(count):
            i = start + t

            def piece(x):
                entry = entry_of(i * window + x)
                held = jnp.maximum(entry, 0)
                source, slot = lax.shift_right_logical(held, 5), held & 31
                return jnp.where(entry >= 0, parts[source, slot].astype(f32), 0.0)

            columns = []
            for x in range(width):
                left, right = piece(x), piece(x + width)
                columns.append(jnp.where(first_lanes, left, pltpu.roll(right, band // 2, 1)))
                columns.append(jnp.where(first_lanes, pltpu.roll(left, band // 2, 1), right))
            token = jnp.concatenate(columns, axis=0)
            tokens[i] = token
            loaded.append(token)
        qkv = dot(w_qkv[...], scale(side_by_side(loaded), norm_gains[0]))
        for t in range(count):
            i = start + t
            one = qkv[:, t * band : (t + 1) * band]
            query, key, value = [one[n * rows : (n + 1) * rows].reshape(tiles) for n in range(3)]
            queries[i] = head_scale(query, head_gains[0]) * (1.0 / float(head) ** 0.5)
            keys[i] = head_scale(key, head_gains[1])
            values[i] = value.astype(half).astype(f32)

    def finish(hidden):
        inner = dot(w_mlp[...], scale(hidden, norm_gains[1]))
        return jax.nn.gelu(inner, approximate=True).astype(half)

    def add_up(array, count):
        total = array[:, :band]
        for t in range(1, count):
            total = total + array[:, t * band : (t + 1) * band]
        return total

    def attend(start, count, with_blank, held=None):
        def loop(body, start):
            if held is None:
                return lax.fori_loop(0, found, body, start)
            for s in range(held):
                start = body(s, start)
            return start

        def score(s, norms):
            added = []
            for t in range(count):
                product = (queries[start + t] * keys[s]).reshape(groups, head, 8, band)
                weight = jnp.exp(jnp.sum(product, axis=1))
                weights[t, s] = weight
                added.append(norms[t] + weight)
            return tuple(added)

        others = blank if held is None else (counting - held).astype(f32)
        norms = loop(score, (jnp.zeros((groups, 8, band), f32) + others,) * count)
        inverses = [1.0 / norm for norm in norms]
        mixed = [[] for _ in range(count)]
        none = jnp.zeros((head, 8, band), f32)
        for g in range(groups):
            for t in range(0, count, 2):

                def mix(s, sums):
                    value = values[s, g * head : (g + 1) * head]
                    probs = [weights[t + k, s, g] * inverses[t + k][g] for k in range(2)]
                    probs = [prob.astype(half).astype(f32) for prob in probs]
                    return tuple(sums[k] + probs[k][None] * value for k in range(2))

                sums = loop(mix, (none, none))
                for k in range(2):
                    mixed[t + k].append(sums[k].reshape(head * 8, band).astype(half))
        mixed = [jnp.concatenate(m, axis=0) for m in mixed]
        if with_blank:

            def gather(s, total):
                return total + values[s]

            prob = jnp.broadcast_to(1.0 / counting.astype(f32), (8, band)).astype(half).astype(f32)
            total = loop(gather, jnp.zeros(tiles, f32))
            mixed.append((total * prob[None]).reshape(rows, band).astype(half))
        hidden = dot(w_mix[...], side_by_side(mixed))
        own = [
            hidden[:, t * band : (t + 1) * band] + tokens[start + t] for t in range(count)
        ] + ([hidden[:, count * band :]] if with_blank else [])
        hidden = side_by_side(own)
        return hidden, finish(hidden)

    def first_tokens(count, held, padding):
        hidden, inner = attend(0, count, True, held)
        rest = blank - padding.astype(f32)
        inner = inner.astype(f32)
        sum_hidden[...] = add_up(hidden, count) + hidden[:, count * band :] * rest
        sum_inner[...] = add_up(inner, count) + inner[:, count * band :] * rest

    for n, count in enumerate(FEW):

        @pl.when((found <= count) & (found > (FEW[n - 1] if n else -1)))
        def _():
            project(0, count, lambda place: seen[0, place])
            first_tokens(count, count, count - found)

    @pl.when(found > FEW[-1])
    def _():
        read = pltpu.make_async_copy(lists, plan, plan_sem)
        read.start()
        read.wait()

        def entry_of(place):
            return plan[0, place]

        project(0, FEW[-1], entry_of)

        def project_more(n, carry):
            project(FEW[-1] + AFTER * n, AFTER, entry_of)
            return carry

        lax.fori_loop(0, steps, project_more, 0)
        first_tokens(FEW[-1], None, FEW[-1] + AFTER * steps - found)

        def attend_more(n, carry):
            hidden, inner = attend(FEW[-1] + AFTER * n, AFTER, False)
            sum_hidden[...] += add_up(hidden, AFTER)
            sum_inner[...] += add_up(inner.astype(f32), AFTER)
            return carry

        lax.fori_loop(0, steps, attend_more, 0)

    inverse = 1.0 / counting.astype(f32)
    lane = iota((chans, band), 1)
    edges = jnp.zeros((chans, band), f32)
    taken = jnp.where(side == 0, 0, band // 2 - 2)
    for x in range(width):
        inner = sum_inner[x * mlp : (x + 1) * mlp, :]
        high = inner.astype(half)
        low = (inner - high.astype(f32)).astype(half)
        back = dot(w_back[...], jnp.concatenate([high, low], axis=1))
        sums = sum_hidden[x * chans : (x + 1) * chans, :] + back[:, :band] + back[:, band:]
        joined = (sums * inverse).astype(half)
        out[x] = joined
        joined = joined.astype(f32)
        for column, start in ((x, 0), (x + width, band // 2)):
            turn = rem(2 * column - start - taken + 2 * band, band)
            edges = jnp.where(div(lane, 2) == column, pltpu.roll(joined, turn, 1), edges)
    strip[...] = edges.astype(half)


def join(parts, plan, arranged, w_back, width):
    part, band = parts.shape[2:]
    chans, mlp = w_back.shape
    lists = plan.reshape(1, -1)
    spaces = (plan.shape[0] - 2) // (2 * width)
    rows = width * chans
    groups = HEADS * width // 8
    arrays = (parts, *arranged[:5], w_back)
    tiles = pltpu.VMEM((spaces, rows // 8, 8, band), f32)
    return pl.pallas_call(
        join_kernel,
        out_shape=[
            jax.ShapeDtypeStruct((width, chans, band), half),
            jax.ShapeDtypeStruct((chans, band), half),
        ],
        in_specs=[pl.BlockSpec(memory_space=VMEM)] * (1 + len(arrays)),
        out_specs=[pl.BlockSpec(memory_space=VMEM)] * 2,
        scratch_shapes=[
            pltpu.SMEM(lists.shape, jnp.int32),
            pltpu.SemaphoreType.DMA,
            pltpu.VMEM((spaces, rows, band), f32),
            tiles,
            tiles,
            tiles,
            pltpu.VMEM((FEW[-1], spaces, groups, 8, band), f32),
            pltpu.VMEM((rows, band), f32),
            pltpu.VMEM((width * mlp, band), f32),
        ],
        compiler_params=pltpu.CompilerParams(vmem_limit_bytes=LIMIT),
        name="join",
    )(lists, *arrays)


def frame_columns(mine, theirs, far, w_first, wide, products):
    width, chans, band = mine.shape
    side = here()[0]
    own = div(iota((chans, band), 1), band // 2) == side

    def put(j, column):
        wide[j * chans : (j + 1) * chans, :] = column

    for j in range(width):
        first, second = mine[j].astype(f32), theirs[j].astype(f32)
        put(2 + j, jnp.where(own, first, pltpu.roll(second, band // 2, 1)).astype(half))

    def near(j):
        first, second = mine[j].astype(f32), theirs[j].astype(f32)
        return jnp.where(own, pltpu.roll(first, band // 2, 1), second).astype(half)

    @pl.when(side == 0)
    def _():
        for j in range(2):
            put(width + 2 + j, near(j))
            put(j, far(j))

    @pl.when(side == 1)
    def _():
        for j in range(2):
            put(j, near(width - 2 + j))
            put(width + 2 + j, far(j))

    for x in range(width + 2):
        products[x] = dot(w_first[...], wide[x * chans : (x + 3) * chans, :])


def frame_pair_kernel(mine, theirs, w_first, products, wide):
    none = jnp.zeros(mine.shape[1:], half)
    frame_columns(mine, theirs, lambda j: none, w_first, wide, products)


def frame_kernel(mine, theirs, w_first, far, products, strip_a, strip_b, wide):
    width, chans, band = mine.shape
    odd = rem(here()[2], 2)
    lane = iota((chans, band), 1)
    frame_columns(mine, theirs, lambda j: far[j], w_first, wide, products)
    low = jnp.zeros((chans, band), f32)
    high = low
    for j in range(width + 4):
        column = wide[j * chans : (j + 1) * chans, :].astype(f32)
        place = div(lane, 2) == j
        low = jnp.where(place, column if j == 0 else pltpu.roll(column, 2 * j, 1), low)
        high = jnp.where(place, pltpu.roll(column, 2 * j + 2, 1), high)
    strip_a[...] = jnp.where(odd == 0, high, low).astype(half)
    strip_b[...] = jnp.where(odd == 0, low, high).astype(half)


def frame(kernel, arrays):
    width, chans, band = arrays[0].shape
    strip = jax.ShapeDtypeStruct((chans, band), half)
    shapes = [jax.ShapeDtypeStruct((width + 2, 3 * chans, band), f32)]
    if kernel is frame_kernel:
        shapes += [strip, strip]
    return pl.pallas_call(
        kernel,
        out_shape=shapes,
        in_specs=[pl.BlockSpec(memory_space=VMEM)] * len(arrays),
        out_specs=[pl.BlockSpec(memory_space=VMEM)] * len(shapes),
        scratch_shapes=[pltpu.VMEM(((width + 4) * chans, band), half)],
        compiler_params=pltpu.CompilerParams(vmem_limit_bytes=LIMIT),
        name="frame",
    )(*arrays)


def decode_kernel(
    single, ncols, nrows, inner, strip_a, strip_b, w_first, w_second, out, wide, act
):
    chans, band = strip_a.shape
    outs, width = out.shape[:2]
    side, pair, index = here()
    odd = rem(index, 2)
    from_a, from_b = strip_a[...].astype(f32), strip_b[...].astype(f32)
    if single:
        turn = jnp.where(side == 0, 4, band + 4 - 2 * width)
        from_a, from_b = pltpu.roll(from_a, turn, 1), pltpu.roll(from_b, turn, 1)
    low_in_a = side == 1 if single else odd == 1
    low = jnp.where(low_in_a, from_a, from_b)
    high = jnp.where(low_in_a, from_b, from_a)
    lane = iota((chans, band), 1)
    for j in range(width + 4):
        after = high if j == 0 else pltpu.roll(high, band - 2 * j, 1)
        before = pltpu.roll(low, band - 2 - 2 * j, 1)
        edge = jnp.where(lane < 2, after, jnp.where(lane >= band - 2, before, 0.0))
        wide[j * chans : (j + 1) * chans, :] = edge.astype(half)

    def shifted(products, count):
        above, level, below = [products[n * count : (n + 1) * count] for n in range(3)]
        return pltpu.roll(above, 1, 1) + level + pltpu.roll(below, 2 * band - 1, 1)

    lane = iota((chans, 2 * band), 1)
    row = index * band + jnp.where(lane < band + band // 2, lane, lane - 2 * band)
    row_inside = (row >= 0) & (row < nrows)
    for x in range(width + 2):
        column = (2 * pair + side) * width + (x - 1)
        outer = dot(w_first[...], wide[x * chans : (x + 3) * chans, :])
        products = jnp.concatenate([inner[x], outer], axis=1)
        hidden = jax.nn.gelu(shifted(products, chans), approximate=True)
        inside = row_inside & (column >= 0) & (column < ncols)
        act[x * chans : (x + 1) * chans, :] = jnp.where(inside, hidden, 0.0).astype(half)
    for x in range(width):
        products = dot(w_second[...], act[x * chans : (x + 3) * chans, :])
        out[:, x, :] = shifted(products, products.shape[0] // 3)[:outs, :band]


def decode(single, arrays, outs, ncols, nrows):
    width = arrays[0].shape[0] - 2
    chans, band = arrays[1].shape
    out = pl.pallas_call(
        functools.partial(decode_kernel, single, ncols, nrows),
        out_shape=jax.ShapeDtypeStruct((outs, width, band), f32),
        in_specs=[pl.BlockSpec(memory_space=VMEM)] * len(arrays),
        out_specs=pl.BlockSpec(memory_space=VMEM),
        scratch_shapes=[
            pltpu.VMEM(((width + 4) * chans, band), half),
            pltpu.VMEM(((width + 2) * chans, 2 * band), half),
        ],
        compiler_params=pltpu.CompilerParams(vmem_limit_bytes=LIMIT),
        name="decode",
    )(*arrays)
    return jnp.transpose(out, (1, 0, 2))


def swap(values, axis, first):
    count = lax.axis_size(axis)
    pairs = [(i, i + 1) for i in range(first, count - 1, 2)]
    if not pairs:
        return jnp.zeros_like(values)
    return lax.ppermute(values, axis, pairs + [(b, a) for a, b in pairs])


def all_moves(moves):
    count = lax.axis_size("pass")
    me = lax.axis_index("pass")
    pieces = [moves]
    for step in range(1, count):
        pieces.append(lax.ppermute(moves, "pass", [(i, (i - step) % count) for i in range(count)]))
    start = rem(count - me, count) * moves.shape[1]
    return lax.dynamic_slice_in_dim(
        jnp.concatenate(pieces * 2, axis=1), start, count * moves.shape[1], 1
    )


def to_band(strip, other):
    tiles, passes, cores = [lax.axis_size(a) for a in ("tile", "pass", "row")]

    def index(band, side):
        return (band // cores) * passes * cores + side * cores + band % cores

    bands = tiles * cores
    pairs = [(index(b, 0), index(b - 1, other)) for b in range(1, bands)]
    pairs += [(index(b, 1), index(b + 1, 1 - other)) for b in range(bands - 1)]
    return lax.ppermute(strip, ("tile", "pass", "row"), pairs)


def local(revisits, shifts, flags, *weights):
    params, (conv_first, conv_second) = weights[:10], weights[10:]
    passes = lax.axis_size("pass")
    bands = lax.axis_size(("tile", "row"))
    count, per_device, chans, nrows = revisits.shape
    assert per_device == 1 and passes % 2 == 0 and count <= 32
    ncols = bands
    width = ncols // passes
    band = nrows // bands
    slots = min(SLOTS, count)
    first, moves = pack(revisits, shifts.T, passes, bands, ncols, slots)
    first = send(first)
    every = all_moves(moves)
    arranged = arrange(params, conv_first, conv_second, width, band)
    plan, needed = make_plan(every, flags.T, passes, ncols)
    needed = needed[0]

    outs = conv_second.shape[3]
    w_first, w_second = arranged[5:7]

    def finish(parts):
        joined, strip = join(parts, plan, arranged, params[9].T, width)
        side = rem(lax.axis_index("pass"), 2)
        theirs = swap(joined, "pass", 0)
        if passes == 2:
            strip_a, strip_b = to_band(strip, 0), to_band(strip, 1)
            (products,) = frame(frame_pair_kernel, (joined, theirs, w_first))
        else:
            first = jnp.where(side == 0, joined[:2], joined[-2:]).astype(f32)
            second = jnp.where(side == 0, theirs[:2], theirs[-2:]).astype(f32)
            own = div(jnp.arange(band, dtype=jnp.int32), band // 2) == side
            edge = jnp.where(own, first, jnp.roll(second, band // 2, -1)).astype(half)
            far = swap(edge, "pass", 1)
            products, strip_a, strip_b = frame(frame_kernel, (joined, theirs, w_first, far))
            strip_a, strip_b = swap(strip_a, ("tile", "row"), 0), swap(strip_b, ("tile", "row"), 1)
        arrays = (products, strip_a, strip_b, w_first, w_second)
        return decode(passes == 2, arrays, outs, ncols, nrows)

    if count <= slots:
        return finish(first)

    def more():
        held = jnp.zeros((first.shape[0], count) + first.shape[2:], half)
        held = lax.dynamic_update_slice_in_dim(held, first, 0, 1)

        def step(i, held):
            sent = send(pack(revisits, moves, passes, bands, ncols, 1, i)[0])
            return lax.dynamic_update_slice_in_dim(held, sent, i, 1)

        return finish(lax.fori_loop(slots, needed, step, held))

    return lax.cond(needed > slots, more, lambda: finish(first))


def solution(mesh):
    return jax.shard_map(
        local,
        mesh=mesh,
        in_specs=(
            P(("groups", "pass"), ("tile", "row"), None, None),
            P(("groups", "pass"), None),
            P("groups", ("tile", "row")),
        )
        + (P(),) * 12,
        out_specs=P(("groups", "pass"), None, ("tile", "row")),
        check_vma=False,
    )
```

```python
import functools

import jax
import jax.numpy as jnp
from jax import lax
from jax.experimental import pallas as pl
from jax.experimental.pallas import tpu as pltpu
from jax.sharding import PartitionSpec as P

HEADS = 4
eps = 1e-05
SLOTS = 3
FEW = (2, 3, 4, 6)
AFTER = 2
LIMIT = 48 * 1024 * 1024
PACK_LIMIT = 63 * 1024 * 1024
f32 = jnp.float32
half = jnp.bfloat16
SMEM = pltpu.MemorySpace.SMEM
VMEM = pltpu.MemorySpace.VMEM
HBM = pltpu.MemorySpace.HBM


def pack_kernel(window, ncols, first_slot, moves, revisits, *rest):
    if first_slot is None:
        base, out, moves_out, table, held, staged, sems, out_sems, echo_sem = rest
        first_slot = base[0]
    else:
        out, moves_out, table, held, staged, sems, out_sems, echo_sem = rest
    count = held.shape[0]
    chans, rows = held.shape[1:]
    bands, slots, part, band = out.shape[1:]
    mine = here()[2]
    read = pltpu.make_async_copy(moves, table, echo_sem.at[0])
    read.start()
    loads = [
        pltpu.make_async_copy(revisits.at[r, 0], held.at[r], sems.at[r]) for r in range(count)
    ]
    for load in loads:
        load.start()
    read.wait()
    echo = pltpu.make_async_copy(table, moves_out, echo_sem.at[1])
    echo.start()
    places = []
    for r in range(count):
        place = mine - table[1, r]
        inside = (place >= 0) & (place < ncols)
        owner = jnp.where(inside, lax.div(jnp.maximum(place, 0), jnp.int32(window)), -1)
        slot = jnp.int32(0) - first_slot
        for other, _, _ in places:
            slot = slot + jnp.where(other == owner, 1, 0)
        places.append((owner, slot, inside & (slot >= 0) & (slot < slots)))

    def writes(r):
        owner, slot, _ = places[r]
        return [
            pltpu.make_async_copy(
                staged.at[r, side], out.at[2 * owner + side, :, slot], out_sems.at[r, side]
            )
            for side in range(2)
        ]

    for r in range(count):
        loads[r].wait()

        @pl.when(places[r][2])
        def _():
            offset = table[0, r]
            turn = jnp.where(offset > 0, band - offset, -offset)
            lane = iota((16, band), 1)
            stays = (lane + offset >= 0) & (lane + offset < band)
            later = jnp.broadcast_to(offset > 0, (16, band))
            first = lane < band // 2
            none = jnp.zeros((16, band), f32)
            for c in range(0, part, 16):
                halves = []
                for low in (c, part + c):
                    turned = [
                        pltpu.roll(
                            held[r, low : low + 16, b * band : (b + 1) * band].astype(f32), turn, 1
                        )
                        for b in range(bands)
                    ]
                    turned = [none] + turned + [none]
                    halves.append(
                        [
                            jnp.where(
                                stays, turned[b + 1], jnp.where(later, turned[b + 2], turned[b])
                            )
                            for b in range(bands)
                        ]
                    )
                for b in range(bands):
                    top, bottom = halves[0][b], halves[1][b]
                    staged[r, 0, b, c : c + 16, :] = jnp.where(
                        first, top, pltpu.roll(bottom, band // 2, 1)
                    ).astype(half)
                    staged[r, 1, b, c : c + 16, :] = jnp.where(
                        first, pltpu.roll(top, band // 2, 1), bottom
                    ).astype(half)
            for write in writes(r):
                write.start()

    for r in range(count):

        @pl.when(places[r][2])
        def _():
            for write in writes(r):
                write.wait()

    echo.wait()


def pack(revisits, moves, passes, bands, ncols, slots, base=None):
    count, _, chans, rows = revisits.shape
    part, band = chans // 2, rows // bands
    first_slot = 0 if base is None else None
    scalars = [] if base is None else [base.reshape(1)]
    return pl.pallas_call(
        functools.partial(pack_kernel, 2 * ncols // passes, ncols, first_slot),
        out_shape=[
            jax.ShapeDtypeStruct((passes, bands, slots, part, band), half),
            jax.ShapeDtypeStruct(moves.shape, jnp.int32),
        ],
        in_specs=[pl.BlockSpec(memory_space=HBM)] * 2
        + [pl.BlockSpec(memory_space=SMEM)] * len(scalars),
        out_specs=[pl.BlockSpec(memory_space=HBM)] * 2,
        scratch_shapes=[
            pltpu.SMEM(moves.shape, jnp.int32),
            pltpu.VMEM((count, chans, rows), half),
            pltpu.VMEM((count, 2, bands, part, band), half),
            pltpu.SemaphoreType.DMA((count,)),
            pltpu.SemaphoreType.DMA((count, 2)),
            pltpu.SemaphoreType.DMA((2,)),
        ],
        compiler_params=pltpu.CompilerParams(vmem_limit_bytes=PACK_LIMIT),
        name="pack",
    )(moves, revisits, *scalars)


def send(packed):
    passes, bands, slots, part, band = packed.shape
    packed = packed.reshape(passes * bands, slots * part, band)
    sent = lax.all_to_all(packed, ("pass", "tile", "row"), 0, 0, tiled=True)
    return sent.reshape(passes * bands, slots, part, band)


def here():
    index = lax.axis_index("pass")
    band = lax.axis_index("tile") * lax.axis_size("row") + lax.axis_index("row")
    return rem(index, 2), div(index, 2), band


def iota(shape, dim):
    return lax.broadcasted_iota(jnp.int32, shape, dim)


def div(values, by):
    return lax.div(values, jnp.int32(by))


def rem(values, by):
    return lax.rem(values, jnp.int32(by))


def dot(a, b, dims=((1,), (0,))):
    return lax.dot_general(a, b, (dims, ((), ())), preferred_element_type=f32)


def plan_kernel(width, ncols, windows, moves, flags, plan, needed, seen, filled):
    window = 2 * width
    total = flags.shape[1]
    sources = seen.shape[0]
    per = total // (sources // ncols)
    listed = (total + FEW[-1] + AFTER) * window

    def fill(ref, count, value):
        def one(i, carry):
            for x in range(window):
                ref[i * window + x] = value
            return carry

        lax.fori_loop(0, count // window, one, 0)

    fill(plan, listed, jnp.int32(-1))
    fill(filled, window, jnp.int32(0))
    pair = here()[1]
    most = jnp.int32(0)
    for w in range(windows):
        base = w * window
        fill(seen, sources, jnp.int32(0))

        def revisit(r, most):
            shift = moves[1, r]
            counts = (flags[0, r] != 0) & (pair == w)
            first_source = div(r, per) * ncols + shift + base

            def column(x, most):
                source = first_source + x
                slot = seen[source]
                seen[source] = slot + 1

                @pl.when(counts)
                def _():
                    place = filled[x]
                    filled[x] = place + 1
                    plan[place * window + x] = source * 32 + slot

                return jnp.maximum(most, slot + 1)

            low = jnp.maximum(0, -shift - base)
            return lax.fori_loop(low, jnp.minimum(window, ncols - shift - base), column, most)

        most = lax.fori_loop(0, total, revisit, most)
    longest = lax.fori_loop(0, window, lambda x, n: jnp.maximum(n, filled[x]), jnp.int32(0))
    counting = lax.fori_loop(
        0, total, lambda r, n: n + jnp.where(flags[0, r] != 0, 1, 0), jnp.int32(0)
    )
    plan[listed] = longest
    plan[listed + 1] = counting
    needed[0] = most


def weights_kernel(
    width,
    norm1_gain,
    w_query,
    w_key,
    w_value,
    query_gain,
    key_gain,
    w_out,
    norm2_gain,
    w_in,
    conv_first,
    conv_second,
    w_qkv,
    w_mix,
    w_mlp,
    norm_gains,
    head_gains,
    w_first,
    w_second,
):
    chans, mlp = w_in.shape
    head = chans // HEADS
    pair = 8 // width
    rows = width * chans
    band = head_gains.shape[2]
    row = iota((rows, chans), 0)
    channel = (div(row, 8 * head) * pair + rem(div(row, width), pair)) * head + rem(div(row, 8), head)
    picked = channel == iota((rows, chans), 1)
    pick = jnp.where(picked, 1.0, 0.0).astype(half)
    spread = rem(iota((chans, rows), 1), chans) == iota((chans, rows), 0)
    spread = jnp.where(spread, 1.0, 0.0).astype(half)
    same = div(iota((rows, rows), 1), chans) == rem(iota((rows, rows), 0), width)
    for n, weight in enumerate((w_query, w_key, w_value)):
        chosen = dot(pick, weight[...], ((1,), (1,))).astype(half)
        w_qkv[n * rows : (n + 1) * rows, :] = jnp.where(same, dot(chosen, spread), 0.0).astype(half)
    mixing = dot(w_out[...], pick, ((0,), (1,)))
    mixing = jnp.concatenate([mixing] * width, axis=0)
    same = rem(iota((rows, rows), 1), width) == div(iota((rows, rows), 0), chans)
    w_mix[...] = jnp.where(same, mixing, 0.0).astype(half)
    wide = dot(w_in[...], spread, ((0,), (0,)))
    wide = jnp.concatenate([wide] * width, axis=0)
    same = div(iota((width * mlp, rows), 0), mlp) == div(iota((width * mlp, rows), 1), chans)
    w_mlp[...] = jnp.where(same, wide, 0.0).astype(half)
    plain = iota((chans, chans), 0) == iota((chans, chans), 1)
    for n, gain in enumerate((norm1_gain, norm2_gain)):
        column = jnp.sum(jnp.where(plain, gain[...], 0.0), axis=1, keepdims=True)
        norm_gains[n] = jnp.broadcast_to(column, (chans, band))
    for n, gain in enumerate((query_gain, key_gain)):
        column = jnp.sum(jnp.where(picked, gain[...], 0.0), axis=1, keepdims=True)
        head_gains[n] = jnp.broadcast_to(column, (rows, band))
    for kernel, result in ((conv_first, w_first), (conv_second, w_second)):
        outs = kernel.shape[3]
        for down in range(3):
            total = jnp.zeros((outs, 3 * chans), f32)
            for across in range(3):
                place = iota((chans, 3 * chans), 1) == iota((chans, 3 * chans), 0) + across * chans
                place = jnp.where(place, 1.0, 0.0).astype(half)
                total += dot(kernel[across, down], place, ((0,), (0,)))
            result[down * outs : (down + 1) * outs, :] = total.astype(half)


def arrange(params, conv_first, conv_second, width, band):
    chans, mlp = params[8].shape
    rows = width * chans
    outs = -(-conv_second.shape[3] // 16) * 16
    padding = ((0, 0), (0, 0), (0, 0), (0, outs - conv_second.shape[3]))
    conv_second = jnp.pad(conv_second, padding)
    arrays = [p.reshape(1, -1) if p.ndim == 1 else p for p in params[:9]]
    arrays += [conv_first, conv_second]
    return pl.pallas_call(
        functools.partial(weights_kernel, width),
        out_shape=[
            jax.ShapeDtypeStruct((3 * rows, rows), half),
            jax.ShapeDtypeStruct((rows, rows), half),
            jax.ShapeDtypeStruct((width * mlp, rows), half),
            jax.ShapeDtypeStruct((2, chans, band), f32),
            jax.ShapeDtypeStruct((2, rows, band), f32),
            jax.ShapeDtypeStruct((3 * conv_first.shape[3], 3 * chans), half),
            jax.ShapeDtypeStruct((3 * outs, 3 * chans), half),
        ],
        in_specs=[pl.BlockSpec(memory_space=VMEM)] * len(arrays),
        out_specs=[pl.BlockSpec(memory_space=VMEM)] * 7,
        compiler_params=pltpu.CompilerParams(vmem_limit_bytes=LIMIT),
        name="weights",
    )(*arrays)


def make_plan(moves, flags, passes, ncols):
    width = ncols // passes
    sources = passes * ncols
    spaces = flags.shape[1] + FEW[-1] + AFTER
    return pl.pallas_call(
        functools.partial(plan_kernel, width, ncols, passes // 2),
        out_shape=[
            jax.ShapeDtypeStruct((spaces * 2 * width + 2,), jnp.int32),
            jax.ShapeDtypeStruct((1,), jnp.int32),
        ],
        in_specs=[pl.BlockSpec(memory_space=SMEM)] * 2,
        out_specs=[pl.BlockSpec(memory_space=SMEM)] * 2,
        scratch_shapes=[
            pltpu.SMEM((sources,), jnp.int32),
            pltpu.SMEM((2 * width,), jnp.int32),
        ],
        name="plan",
    )(moves, flags)


def join_kernel(
    lists,
    parts,
    w_qkv,
    w_mix,
    w_mlp,
    norm_gains,
    head_gains,
    w_back,
    out,
    strip,
    plan,
    plan_sem,
    tokens,
    queries,
    keys,
    values,
    weights,
    sum_hidden,
    sum_inner,
):
    sources, slots, part, band = parts.shape
    width, chans = out.shape[:2]
    mlp = w_mlp.shape[0] // width
    head = chans // HEADS
    rows = width * chans
    groups = HEADS * width // 8
    window = 2 * width
    listed = lists.shape[1] - 2
    seen = lists[...]
    found, counting = seen[0, listed], seen[0, listed + 1]
    steps = div(jnp.maximum(found - FEW[-1], 0) + AFTER - 1, AFTER)
    blank = (counting - found).astype(f32)
    first_lanes = iota((part, band), 1) < band // 2
    side = here()[0]
    tiles = (rows // 8, 8, band)

    def scale(tile, gain):
        lanes = tile.shape[1]
        tile = tile.reshape(width, chans, lanes)
        mean = jnp.mean(tile * tile, axis=1, keepdims=True)
        tile = tile * lax.rsqrt(mean + eps) * side_by_side([gain] * (lanes // band))
        return tile.astype(half).reshape(rows, lanes)

    def head_scale(tile, gain):
        square = jnp.sum(tile * tile, axis=0).reshape(8 // width, width, band)
        mean = jnp.sum(square, axis=0, keepdims=True) * (1.0 / chans)
        factor = jnp.broadcast_to(lax.rsqrt(mean + eps), (8 // width, width, band))
        scaled = tile * factor.reshape(1, 8, band) * gain.reshape(tiles)
        return scaled.astype(half).astype(f32)

    def side_by_side(pieces):
        return jnp.concatenate(pieces, axis=1)

    def project(start, count, entry_of):
        loaded = []
        for t in range(count):
            i = start + t

            def piece(x):
                entry = entry_of(i * window + x)
                held = jnp.maximum(entry, 0)
                source, slot = lax.shift_right_logical(held, 5), held & 31
                return jnp.where(entry >= 0, parts[source, slot].astype(f32), 0.0)

            columns = []
            for x in range(width):
                left, right = piece(x), piece(x + width)
                columns.append(jnp.where(first_lanes, left, pltpu.roll(right, band // 2, 1)))
                columns.append(jnp.where(first_lanes, pltpu.roll(left, band // 2, 1), right))
            token = jnp.concatenate(columns, axis=0)
            tokens[i] = token
            loaded.append(token)
        qkv = dot(w_qkv[...], scale(side_by_side(loaded), norm_gains[0]))
        for t in range(count):
            i = start + t
            one = qkv[:, t * band : (t + 1) * band]
            query, key, value = [one[n * rows : (n + 1) * rows].reshape(tiles) for n in range(3)]
            queries[i] = head_scale(query, head_gains[0]) * (1.0 / float(head) ** 0.5)
            keys[i] = head_scale(key, head_gains[1])
            values[i] = value.astype(half).astype(f32)

    def finish(hidden):
        inner = dot(w_mlp[...], scale(hidden, norm_gains[1]))
        return jax.nn.gelu(inner, approximate=True).astype(half)

    def add_up(array, count):
        total = array[:, :band]
        for t in range(1, count):
            total = total + array[:, t * band : (t + 1) * band]
        return total

    def attend(start, count, with_blank, held=None):
        def loop(body, start):
            if held is None:
                return lax.fori_loop(0, found, body, start)
            for s in range(held):
                start = body(s, start)
            return start

        def score(s, norms):
            added = []
            for t in range(count):
                product = (queries[start + t] * keys[s]).reshape(groups, head, 8, band)
                weight = jnp.exp(jnp.sum(product, axis=1))
                weights[t, s] = weight
                added.append(norms[t] + weight)
            return tuple(added)

        others = blank if held is None else (counting - held).astype(f32)
        norms = loop(score, (jnp.zeros((groups, 8, band), f32) + others,) * count)
        inverses = [1.0 / norm for norm in norms]
        mixed = [[] for _ in range(count)]
        none = jnp.zeros((head, 8, band), f32)
        for g in range(groups):
            for t in range(0, count, 2):

                both = range(min(2, count - t))

                def mix(s, sums):
                    value = values[s, g * head : (g + 1) * head]
                    probs = [weights[t + k, s, g] * inverses[t + k][g] for k in both]
                    probs = [prob.astype(half).astype(f32) for prob in probs]
                    return tuple(sums[k] + probs[k][None] * value for k in both)

                sums = loop(mix, (none,) * len(both))
                for k in both:
                    mixed[t + k].append(sums[k].reshape(head * 8, band).astype(half))
        mixed = [jnp.concatenate(m, axis=0) for m in mixed]
        if with_blank:

            def gather(s, total):
                return total + values[s]

            prob = jnp.broadcast_to(1.0 / counting.astype(f32), (8, band)).astype(half).astype(f32)
            total = loop(gather, jnp.zeros(tiles, f32))
            mixed.append((total * prob[None]).reshape(rows, band).astype(half))
        hidden = dot(w_mix[...], side_by_side(mixed))
        own = [
            hidden[:, t * band : (t + 1) * band] + tokens[start + t] for t in range(count)
        ] + ([hidden[:, count * band :]] if with_blank else [])
        hidden = side_by_side(own)
        return hidden, finish(hidden)

    def first_tokens(count, held, padding):
        hidden, inner = attend(0, count, True, held)
        rest = blank - padding.astype(f32)
        inner = inner.astype(f32)
        sum_hidden[...] = add_up(hidden, count) + hidden[:, count * band :] * rest
        sum_inner[...] = add_up(inner, count) + inner[:, count * band :] * rest

    for n, count in enumerate(FEW):

        @pl.when((found <= count) & (found > (FEW[n - 1] if n else -1)))
        def _():
            project(0, count, lambda place: seen[0, place])
            first_tokens(count, count, count - found)

    @pl.when(found > FEW[-1])
    def _():
        read = pltpu.make_async_copy(lists, plan, plan_sem)
        read.start()
        read.wait()

        def entry_of(place):
            return plan[0, place]

        project(0, FEW[-1], entry_of)

        def project_more(n, carry):
            project(FEW[-1] + AFTER * n, AFTER, entry_of)
            return carry

        lax.fori_loop(0, steps, project_more, 0)
        first_tokens(FEW[-1], None, FEW[-1] + AFTER * steps - found)

        def attend_more(n, carry):
            hidden, inner = attend(FEW[-1] + AFTER * n, AFTER, False)
            sum_hidden[...] += add_up(hidden, AFTER)
            sum_inner[...] += add_up(inner.astype(f32), AFTER)
            return carry

        lax.fori_loop(0, steps, attend_more, 0)

    inverse = 1.0 / counting.astype(f32)
    lane = iota((chans, band), 1)
    edges = jnp.zeros((chans, band), f32)
    taken = jnp.where(side == 0, 0, band // 2 - 2)
    for x in range(width):
        inner = sum_inner[x * mlp : (x + 1) * mlp, :]
        high = inner.astype(half)
        low = (inner - high.astype(f32)).astype(half)
        back = dot(w_back[...], jnp.concatenate([high, low], axis=1))
        sums = sum_hidden[x * chans : (x + 1) * chans, :] + back[:, :band] + back[:, band:]
        joined = (sums * inverse).astype(half)
        out[x] = joined
        joined = joined.astype(f32)
        for column, start in ((x, 0), (x + width, band // 2)):
            turn = rem(2 * column - start - taken + 2 * band, band)
            edges = jnp.where(div(lane, 2) == column, pltpu.roll(joined, turn, 1), edges)
    strip[...] = edges.astype(half)


def join(parts, plan, arranged, w_back, width):
    part, band = parts.shape[2:]
    chans, mlp = w_back.shape
    lists = plan.reshape(1, -1)
    spaces = (plan.shape[0] - 2) // (2 * width)
    rows = width * chans
    groups = HEADS * width // 8
    arrays = (parts, *arranged[:5], w_back)
    tiles = pltpu.VMEM((spaces, rows // 8, 8, band), f32)
    return pl.pallas_call(
        join_kernel,
        out_shape=[
            jax.ShapeDtypeStruct((width, chans, band), half),
            jax.ShapeDtypeStruct((chans, band), half),
        ],
        in_specs=[pl.BlockSpec(memory_space=VMEM)] * (1 + len(arrays)),
        out_specs=[pl.BlockSpec(memory_space=VMEM)] * 2,
        scratch_shapes=[
            pltpu.SMEM(lists.shape, jnp.int32),
            pltpu.SemaphoreType.DMA,
            pltpu.VMEM((spaces, rows, band), f32),
            tiles,
            tiles,
            tiles,
            pltpu.VMEM((FEW[-1], spaces, groups, 8, band), f32),
            pltpu.VMEM((rows, band), f32),
            pltpu.VMEM((width * mlp, band), f32),
        ],
        compiler_params=pltpu.CompilerParams(vmem_limit_bytes=LIMIT),
        name="join",
    )(lists, *arrays)


def frame_columns(mine, theirs, far, w_first, wide, products):
    width, chans, band = mine.shape
    side = here()[0]
    own = div(iota((chans, band), 1), band // 2) == side

    def put(j, column):
        wide[j * chans : (j + 1) * chans, :] = column

    for j in range(width):
        first, second = mine[j].astype(f32), theirs[j].astype(f32)
        put(2 + j, jnp.where(own, first, pltpu.roll(second, band // 2, 1)).astype(half))

    def near(j):
        first, second = mine[j].astype(f32), theirs[j].astype(f32)
        return jnp.where(own, pltpu.roll(first, band // 2, 1), second).astype(half)

    @pl.when(side == 0)
    def _():
        for j in range(2):
            put(width + 2 + j, near(j))
            put(j, far(j))

    @pl.when(side == 1)
    def _():
        for j in range(2):
            put(j, near(width - 2 + j))
            put(width + 2 + j, far(j))

    for x in range(width + 2):
        products[x] = dot(w_first[...], wide[x * chans : (x + 3) * chans, :])


def frame_pair_kernel(mine, theirs, w_first, products, wide):
    none = jnp.zeros(mine.shape[1:], half)
    frame_columns(mine, theirs, lambda j: none, w_first, wide, products)


def frame_kernel(mine, theirs, w_first, far, products, strip_a, strip_b, wide):
    width, chans, band = mine.shape
    odd = rem(here()[2], 2)
    lane = iota((chans, band), 1)
    frame_columns(mine, theirs, lambda j: far[j], w_first, wide, products)
    low = jnp.zeros((chans, band), f32)
    high = low
    for j in range(width + 4):
        column = wide[j * chans : (j + 1) * chans, :].astype(f32)
        place = div(lane, 2) == j
        low = jnp.where(place, column if j == 0 else pltpu.roll(column, 2 * j, 1), low)
        high = jnp.where(place, pltpu.roll(column, 2 * j + 2, 1), high)
    strip_a[...] = jnp.where(odd == 0, high, low).astype(half)
    strip_b[...] = jnp.where(odd == 0, low, high).astype(half)


def frame(kernel, arrays):
    width, chans, band = arrays[0].shape
    strip = jax.ShapeDtypeStruct((chans, band), half)
    shapes = [jax.ShapeDtypeStruct((width + 2, 3 * chans, band), f32)]
    if kernel is frame_kernel:
        shapes += [strip, strip]
    return pl.pallas_call(
        kernel,
        out_shape=shapes,
        in_specs=[pl.BlockSpec(memory_space=VMEM)] * len(arrays),
        out_specs=[pl.BlockSpec(memory_space=VMEM)] * len(shapes),
        scratch_shapes=[pltpu.VMEM(((width + 4) * chans, band), half)],
        compiler_params=pltpu.CompilerParams(vmem_limit_bytes=LIMIT),
        name="frame",
    )(*arrays)


def decode_kernel(
    single, ncols, nrows, inner, strip_a, strip_b, w_first, w_second, out, wide, act
):
    chans, band = strip_a.shape
    outs, width = out.shape[:2]
    side, pair, index = here()
    odd = rem(index, 2)
    from_a, from_b = strip_a[...].astype(f32), strip_b[...].astype(f32)
    if single:
        turn = jnp.where(side == 0, 4, band + 4 - 2 * width)
        from_a, from_b = pltpu.roll(from_a, turn, 1), pltpu.roll(from_b, turn, 1)
    low_in_a = side == 1 if single else odd == 1
    low = jnp.where(low_in_a, from_a, from_b)
    high = jnp.where(low_in_a, from_b, from_a)
    lane = iota((chans, band), 1)
    for j in range(width + 4):
        after = high if j == 0 else pltpu.roll(high, band - 2 * j, 1)
        before = pltpu.roll(low, band - 2 - 2 * j, 1)
        edge = jnp.where(lane < 2, after, jnp.where(lane >= band - 2, before, 0.0))
        wide[j * chans : (j + 1) * chans, :] = edge.astype(half)

    def shifted(products, count):
        above, level, below = [products[n * count : (n + 1) * count] for n in range(3)]
        return pltpu.roll(above, 1, 1) + level + pltpu.roll(below, 2 * band - 1, 1)

    lane = iota((chans, 2 * band), 1)
    row = index * band + jnp.where(lane < band + band // 2, lane, lane - 2 * band)
    row_inside = (row >= 0) & (row < nrows)
    for x in range(width + 2):
        column = (2 * pair + side) * width + (x - 1)
        outer = dot(w_first[...], wide[x * chans : (x + 3) * chans, :])
        products = jnp.concatenate([inner[x], outer], axis=1)
        hidden = jax.nn.gelu(shifted(products, chans), approximate=True)
        inside = row_inside & (column >= 0) & (column < ncols)
        act[x * chans : (x + 1) * chans, :] = jnp.where(inside, hidden, 0.0).astype(half)
    for x in range(width):
        products = dot(w_second[...], act[x * chans : (x + 3) * chans, :])
        out[:, x, :] = shifted(products, products.shape[0] // 3)[:outs, :band]


def decode(single, arrays, outs, ncols, nrows):
    width = arrays[0].shape[0] - 2
    chans, band = arrays[1].shape
    out = pl.pallas_call(
        functools.partial(decode_kernel, single, ncols, nrows),
        out_shape=jax.ShapeDtypeStruct((outs, width, band), f32),
        in_specs=[pl.BlockSpec(memory_space=VMEM)] * len(arrays),
        out_specs=pl.BlockSpec(memory_space=VMEM),
        scratch_shapes=[
            pltpu.VMEM(((width + 4) * chans, band), half),
            pltpu.VMEM(((width + 2) * chans, 2 * band), half),
        ],
        compiler_params=pltpu.CompilerParams(vmem_limit_bytes=LIMIT),
        name="decode",
    )(*arrays)
    return jnp.transpose(out, (1, 0, 2))


def swap(values, axis, first):
    count = lax.axis_size(axis)
    pairs = [(i, i + 1) for i in range(first, count - 1, 2)]
    if not pairs:
        return jnp.zeros_like(values)
    return lax.ppermute(values, axis, pairs + [(b, a) for a, b in pairs])


def all_moves(moves):
    count = lax.axis_size("pass")
    me = lax.axis_index("pass")
    pieces = [moves]
    for step in range(1, count):
        pieces.append(lax.ppermute(moves, "pass", [(i, (i - step) % count) for i in range(count)]))
    start = rem(count - me, count) * moves.shape[1]
    return lax.dynamic_slice_in_dim(
        jnp.concatenate(pieces * 2, axis=1), start, count * moves.shape[1], 1
    )


def to_band(strip, other):
    tiles, passes, cores = [lax.axis_size(a) for a in ("tile", "pass", "row")]

    def index(band, side):
        return (band // cores) * passes * cores + side * cores + band % cores

    bands = tiles * cores
    pairs = [(index(b, 0), index(b - 1, other)) for b in range(1, bands)]
    pairs += [(index(b, 1), index(b + 1, 1 - other)) for b in range(bands - 1)]
    return lax.ppermute(strip, ("tile", "pass", "row"), pairs)


def local(revisits, shifts, flags, *weights):
    params, (conv_first, conv_second) = weights[:10], weights[10:]
    passes = lax.axis_size("pass")
    bands = lax.axis_size(("tile", "row"))
    count, per_device, chans, nrows = revisits.shape
    assert per_device == 1 and passes % 2 == 0 and count <= 32
    ncols = bands
    width = ncols // passes
    band = nrows // bands
    slots = min(SLOTS, count)
    first, moves = pack(revisits, shifts.T, passes, bands, ncols, slots)
    first = send(first)
    every = all_moves(moves)
    arranged = arrange(params, conv_first, conv_second, width, band)
    plan, needed = make_plan(every, flags.T, passes, ncols)
    needed = needed[0]

    outs = conv_second.shape[3]
    w_first, w_second = arranged[5:7]

    def finish(parts):
        joined, strip = join(parts, plan, arranged, params[9].T, width)
        side = rem(lax.axis_index("pass"), 2)
        theirs = swap(joined, "pass", 0)
        if passes == 2:
            strip_a, strip_b = to_band(strip, 0), to_band(strip, 1)
            (products,) = frame(frame_pair_kernel, (joined, theirs, w_first))
        else:
            first = jnp.where(side == 0, joined[:2], joined[-2:]).astype(f32)
            second = jnp.where(side == 0, theirs[:2], theirs[-2:]).astype(f32)
            own = div(jnp.arange(band, dtype=jnp.int32), band // 2) == side
            edge = jnp.where(own, first, jnp.roll(second, band // 2, -1)).astype(half)
            far = swap(edge, "pass", 1)
            products, strip_a, strip_b = frame(frame_kernel, (joined, theirs, w_first, far))
            strip_a, strip_b = swap(strip_a, ("tile", "row"), 0), swap(strip_b, ("tile", "row"), 1)
        arrays = (products, strip_a, strip_b, w_first, w_second)
        return decode(passes == 2, arrays, outs, ncols, nrows)

    if count <= slots:
        return finish(first)

    def more():
        held = jnp.zeros((first.shape[0], count) + first.shape[2:], half)
        held = lax.dynamic_update_slice_in_dim(held, first, 0, 1)

        def step(i, held):
            sent = send(pack(revisits, moves, passes, bands, ncols, 1, i)[0])
            return lax.dynamic_update_slice_in_dim(held, sent, i, 1)

        return finish(lax.fori_loop(slots, needed, step, held))

    return lax.cond(needed > slots, more, lambda: finish(first))


def solution(mesh):
    return jax.shard_map(
        local,
        mesh=mesh,
        in_specs=(
            P(("groups", "pass"), ("tile", "row"), None, None),
            P(("groups", "pass"), None),
            P("groups", ("tile", "row")),
        )
        + (P(),) * 12,
        out_specs=P(("groups", "pass"), None, ("tile", "row")),
        check_vma=False,
    )
```

```python
import functools

import jax
import jax.numpy as jnp
from jax import lax
from jax.experimental import pallas as pl
from jax.experimental.pallas import tpu as pltpu
from jax.sharding import PartitionSpec as P

HEADS = 4
eps = 1e-05
SLOTS = 3
FEW = (2, 3, 4, 6)
AFTER = 2
LIMIT = 48 * 1024 * 1024
PACK_LIMIT = 63 * 1024 * 1024
f32 = jnp.float32
half = jnp.bfloat16
SMEM = pltpu.MemorySpace.SMEM
VMEM = pltpu.MemorySpace.VMEM
HBM = pltpu.MemorySpace.HBM


def pack_kernel(window, ncols, first_slot, moves, revisits, *rest):
    if first_slot is None:
        base, out, moves_out, table, held, staged, sems, out_sems, echo_sem = rest
        first_slot = base[0]
    else:
        out, moves_out, table, held, staged, sems, out_sems, echo_sem = rest
    count = held.shape[0]
    chans, rows = held.shape[1:]
    bands, slots, part, band = out.shape[1:]
    mine = here()[2]
    read = pltpu.make_async_copy(moves, table, echo_sem.at[0])
    read.start()
    loads = [
        pltpu.make_async_copy(revisits.at[r, 0], held.at[r], sems.at[r]) for r in range(count)
    ]
    for load in loads:
        load.start()
    read.wait()
    echo = pltpu.make_async_copy(table, moves_out, echo_sem.at[1])
    echo.start()
    places = []
    for r in range(count):
        place = mine - table[1, r]
        inside = (place >= 0) & (place < ncols)
        owner = jnp.where(inside, lax.div(jnp.maximum(place, 0), jnp.int32(window)), -1)
        slot = jnp.int32(0) - first_slot
        for other, _, _ in places:
            slot = slot + jnp.where(other == owner, 1, 0)
        places.append((owner, slot, inside & (slot >= 0) & (slot < slots)))

    def writes(r):
        owner, slot, _ = places[r]
        return [
            pltpu.make_async_copy(
                staged.at[r, side], out.at[2 * owner + side, :, slot], out_sems.at[r, side]
            )
            for side in range(2)
        ]

    for r in range(count):
        loads[r].wait()

        @pl.when(places[r][2])
        def _():
            offset = table[0, r]
            turn = jnp.where(offset > 0, band - offset, -offset)
            lane = iota((16, band), 1)
            stays = (lane + offset >= 0) & (lane + offset < band)
            later = jnp.broadcast_to(offset > 0, (16, band))
            first = lane < band // 2
            none = jnp.zeros((16, band), f32)
            for c in range(0, part, 16):
                halves = []
                for low in (c, part + c):
                    turned = [
                        pltpu.roll(
                            held[r, low : low + 16, b * band : (b + 1) * band].astype(f32), turn, 1
                        )
                        for b in range(bands)
                    ]
                    turned = [none] + turned + [none]
                    halves.append(
                        [
                            jnp.where(
                                stays, turned[b + 1], jnp.where(later, turned[b + 2], turned[b])
                            )
                            for b in range(bands)
                        ]
                    )
                for b in range(bands):
                    top, bottom = halves[0][b], halves[1][b]
                    staged[r, 0, b, c : c + 16, :] = jnp.where(
                        first, top, pltpu.roll(bottom, band // 2, 1)
                    ).astype(half)
                    staged[r, 1, b, c : c + 16, :] = jnp.where(
                        first, pltpu.roll(top, band // 2, 1), bottom
                    ).astype(half)
            for write in writes(r):
                write.start()

    for r in range(count):

        @pl.when(places[r][2])
        def _():
            for write in writes(r):
                write.wait()

    echo.wait()


def pack(revisits, moves, passes, bands, ncols, slots, base=None):
    count, _, chans, rows = revisits.shape
    part, band = chans // 2, rows // bands
    first_slot = 0 if base is None else None
    scalars = [] if base is None else [base.reshape(1)]
    return pl.pallas_call(
        functools.partial(pack_kernel, 2 * ncols // passes, ncols, first_slot),
        out_shape=[
            jax.ShapeDtypeStruct((passes, bands, slots, part, band), half),
            jax.ShapeDtypeStruct(moves.shape, jnp.int32),
        ],
        in_specs=[pl.BlockSpec(memory_space=HBM)] * 2
        + [pl.BlockSpec(memory_space=SMEM)] * len(scalars),
        out_specs=[pl.BlockSpec(memory_space=HBM)] * 2,
        scratch_shapes=[
            pltpu.SMEM(moves.shape, jnp.int32),
            pltpu.VMEM((count, chans, rows), half),
            pltpu.VMEM((count, 2, bands, part, band), half),
            pltpu.SemaphoreType.DMA((count,)),
            pltpu.SemaphoreType.DMA((count, 2)),
            pltpu.SemaphoreType.DMA((2,)),
        ],
        compiler_params=pltpu.CompilerParams(vmem_limit_bytes=PACK_LIMIT),
        name="pack",
    )(moves, revisits, *scalars)


def send(packed):
    passes, bands, slots, part, band = packed.shape
    packed = packed.reshape(passes * bands, slots * part, band)
    sent = lax.all_to_all(packed, ("pass", "tile", "row"), 0, 0, tiled=True)
    return sent.reshape(passes * bands, slots, part, band)


def here():
    index = lax.axis_index("pass")
    band = lax.axis_index("tile") * lax.axis_size("row") + lax.axis_index("row")
    return rem(index, 2), div(index, 2), band


def iota(shape, dim):
    return lax.broadcasted_iota(jnp.int32, shape, dim)


def gelu(x):
    root = (2.0 / 3.141592653589793) ** 0.5
    low = 0.5 * x
    return low + low * jnp.tanh(x * (root + (0.044715 * root) * (x * x)))


def div(values, by):
    return lax.div(values, jnp.int32(by))


def rem(values, by):
    return lax.rem(values, jnp.int32(by))


def dot(a, b, dims=((1,), (0,))):
    return lax.dot_general(a, b, (dims, ((), ())), preferred_element_type=f32)


def plan_kernel(width, ncols, windows, moves, flags, plan, needed, seen, filled):
    window = 2 * width
    total = flags.shape[1]
    sources = seen.shape[0]
    per = total // (sources // ncols)
    listed = (total + FEW[-1] + AFTER) * window

    def fill(ref, count, value):
        def one(i, carry):
            for x in range(window):
                ref[i * window + x] = value
            return carry

        lax.fori_loop(0, count // window, one, 0)

    fill(plan, listed, jnp.int32(-1))
    fill(filled, window, jnp.int32(0))
    pair = here()[1]
    most = jnp.int32(0)
    for w in range(windows):
        base = w * window
        fill(seen, sources, jnp.int32(0))

        def revisit(r, most):
            shift = moves[1, r]
            counts = (flags[0, r] != 0) & (pair == w)
            first_source = div(r, per) * ncols + shift + base

            def column(x, most):
                source = first_source + x
                slot = seen[source]
                seen[source] = slot + 1

                @pl.when(counts)
                def _():
                    place = filled[x]
                    filled[x] = place + 1
                    plan[place * window + x] = source * 32 + slot

                return jnp.maximum(most, slot + 1)

            low = jnp.maximum(0, -shift - base)
            return lax.fori_loop(low, jnp.minimum(window, ncols - shift - base), column, most)

        most = lax.fori_loop(0, total, revisit, most)
    longest = lax.fori_loop(0, window, lambda x, n: jnp.maximum(n, filled[x]), jnp.int32(0))
    counting = lax.fori_loop(
        0, total, lambda r, n: n + jnp.where(flags[0, r] != 0, 1, 0), jnp.int32(0)
    )
    plan[listed] = longest
    plan[listed + 1] = counting
    needed[0] = most


def weights_kernel(
    width,
    norm1_gain,
    w_query,
    w_key,
    w_value,
    query_gain,
    key_gain,
    w_out,
    norm2_gain,
    w_in,
    conv_first,
    conv_second,
    w_qkv,
    w_mix,
    w_mlp,
    norm_gains,
    head_gains,
    w_first,
    w_second,
):
    chans, mlp = w_in.shape
    head = chans // HEADS
    pair = 8 // width
    rows = width * chans
    band = head_gains.shape[2]
    row = iota((rows, chans), 0)
    channel = (div(row, 8 * head) * pair + rem(div(row, width), pair)) * head + rem(div(row, 8), head)
    picked = channel == iota((rows, chans), 1)
    pick = jnp.where(picked, 1.0, 0.0).astype(half)
    spread = rem(iota((chans, rows), 1), chans) == iota((chans, rows), 0)
    spread = jnp.where(spread, 1.0, 0.0).astype(half)
    same = div(iota((rows, rows), 1), chans) == rem(iota((rows, rows), 0), width)
    for n, weight in enumerate((w_query, w_key, w_value)):
        chosen = dot(pick, weight[...], ((1,), (1,))).astype(half)
        w_qkv[n * rows : (n + 1) * rows, :] = jnp.where(same, dot(chosen, spread), 0.0).astype(half)
    mixing = dot(w_out[...], pick, ((0,), (1,)))
    mixing = jnp.concatenate([mixing] * width, axis=0)
    same = rem(iota((rows, rows), 1), width) == div(iota((rows, rows), 0), chans)
    w_mix[...] = jnp.where(same, mixing, 0.0).astype(half)
    wide = dot(w_in[...], spread, ((0,), (0,)))
    wide = jnp.concatenate([wide] * width, axis=0)
    same = div(iota((width * mlp, rows), 0), mlp) == div(iota((width * mlp, rows), 1), chans)
    w_mlp[...] = jnp.where(same, wide, 0.0).astype(half)
    plain = iota((chans, chans), 0) == iota((chans, chans), 1)
    for n, gain in enumerate((norm1_gain, norm2_gain)):
        column = jnp.sum(jnp.where(plain, gain[...], 0.0), axis=1, keepdims=True)
        norm_gains[n] = jnp.broadcast_to(column, (chans, band))
    for n, gain in enumerate((query_gain, key_gain)):
        column = jnp.sum(jnp.where(picked, gain[...], 0.0), axis=1, keepdims=True)
        head_gains[n] = jnp.broadcast_to(column, (rows, band))
    for kernel, result in ((conv_first, w_first), (conv_second, w_second)):
        outs = kernel.shape[3]
        for down in range(3):
            total = jnp.zeros((outs, 3 * chans), f32)
            for across in range(3):
                place = iota((chans, 3 * chans), 1) == iota((chans, 3 * chans), 0) + across * chans
                place = jnp.where(place, 1.0, 0.0).astype(half)
                total += dot(kernel[across, down], place, ((0,), (0,)))
            result[down * outs : (down + 1) * outs, :] = total.astype(half)


def arrange(params, conv_first, conv_second, width, band):
    chans, mlp = params[8].shape
    rows = width * chans
    outs = -(-conv_second.shape[3] // 16) * 16
    padding = ((0, 0), (0, 0), (0, 0), (0, outs - conv_second.shape[3]))
    conv_second = jnp.pad(conv_second, padding)
    arrays = [p.reshape(1, -1) if p.ndim == 1 else p for p in params[:9]]
    arrays += [conv_first, conv_second]
    return pl.pallas_call(
        functools.partial(weights_kernel, width),
        out_shape=[
            jax.ShapeDtypeStruct((3 * rows, rows), half),
            jax.ShapeDtypeStruct((rows, rows), half),
            jax.ShapeDtypeStruct((width * mlp, rows), half),
            jax.ShapeDtypeStruct((2, chans, band), f32),
            jax.ShapeDtypeStruct((2, rows, band), f32),
            jax.ShapeDtypeStruct((3 * conv_first.shape[3], 3 * chans), half),
            jax.ShapeDtypeStruct((3 * outs, 3 * chans), half),
        ],
        in_specs=[pl.BlockSpec(memory_space=VMEM)] * len(arrays),
        out_specs=[pl.BlockSpec(memory_space=VMEM)] * 7,
        compiler_params=pltpu.CompilerParams(vmem_limit_bytes=LIMIT),
        name="weights",
    )(*arrays)


def make_plan(moves, flags, passes, ncols):
    width = ncols // passes
    sources = passes * ncols
    spaces = flags.shape[1] + FEW[-1] + AFTER
    return pl.pallas_call(
        functools.partial(plan_kernel, width, ncols, passes // 2),
        out_shape=[
            jax.ShapeDtypeStruct((spaces * 2 * width + 2,), jnp.int32),
            jax.ShapeDtypeStruct((1,), jnp.int32),
        ],
        in_specs=[pl.BlockSpec(memory_space=SMEM)] * 2,
        out_specs=[pl.BlockSpec(memory_space=SMEM)] * 2,
        scratch_shapes=[
            pltpu.SMEM((sources,), jnp.int32),
            pltpu.SMEM((2 * width,), jnp.int32),
        ],
        name="plan",
    )(moves, flags)


def join_kernel(
    lists,
    parts,
    w_qkv,
    w_mix,
    w_mlp,
    norm_gains,
    head_gains,
    w_back,
    out,
    strip,
    plan,
    plan_sem,
    tokens,
    queries,
    keys,
    values,
    weights,
    sum_hidden,
    sum_inner,
):
    sources, slots, part, band = parts.shape
    width, chans = out.shape[:2]
    mlp = w_mlp.shape[0] // width
    head = chans // HEADS
    rows = width * chans
    groups = HEADS * width // 8
    window = 2 * width
    listed = lists.shape[1] - 2
    seen = lists[...]
    found, counting = seen[0, listed], seen[0, listed + 1]
    steps = div(jnp.maximum(found - FEW[-1], 0) + AFTER - 1, AFTER)
    blank = (counting - found).astype(f32)
    first_lanes = iota((part, band), 1) < band // 2
    side = here()[0]
    tiles = (rows // 8, 8, band)

    def scale(tile, gain):
        lanes = tile.shape[1]
        tile = tile.reshape(width, chans, lanes)
        mean = jnp.mean(tile * tile, axis=1, keepdims=True)
        tile = tile * lax.rsqrt(mean + eps) * side_by_side([gain] * (lanes // band))
        return tile.astype(half).reshape(rows, lanes)

    def head_scale(tile, gain):
        square = jnp.sum(tile * tile, axis=0).reshape(8 // width, width, band)
        mean = jnp.sum(square, axis=0, keepdims=True) * (1.0 / chans)
        factor = jnp.broadcast_to(lax.rsqrt(mean + eps), (8 // width, width, band))
        scaled = tile * factor.reshape(1, 8, band) * gain.reshape(tiles)
        return scaled.astype(half).astype(f32)

    def side_by_side(pieces):
        return jnp.concatenate(pieces, axis=1)

    def project(start, count, entry_of):
        loaded = []
        for t in range(count):
            i = start + t

            def piece(x):
                entry = entry_of(i * window + x)
                held = jnp.maximum(entry, 0)
                source, slot = lax.shift_right_logical(held, 5), held & 31
                return jnp.where(entry >= 0, parts[source, slot].astype(f32), 0.0)

            columns = []
            for x in range(width):
                left, right = piece(x), piece(x + width)
                columns.append(jnp.where(first_lanes, left, pltpu.roll(right, band // 2, 1)))
                columns.append(jnp.where(first_lanes, pltpu.roll(left, band // 2, 1), right))
            token = jnp.concatenate(columns, axis=0)
            tokens[i] = token
            loaded.append(token)
        qkv = dot(w_qkv[...], scale(side_by_side(loaded), norm_gains[0]))
        for t in range(count):
            i = start + t
            one = qkv[:, t * band : (t + 1) * band]
            query, key, value = [one[n * rows : (n + 1) * rows].reshape(tiles) for n in range(3)]
            queries[i] = head_scale(query, head_gains[0]) * (1.0 / float(head) ** 0.5)
            keys[i] = head_scale(key, head_gains[1])
            values[i] = value.astype(half).astype(f32)

    def finish(hidden):
        inner = dot(w_mlp[...], scale(hidden, norm_gains[1]))
        return gelu(inner).astype(half)

    def add_up(array, count):
        total = array[:, :band]
        for t in range(1, count):
            total = total + array[:, t * band : (t + 1) * band]
        return total

    def attend(start, count, with_blank, held=None):
        def loop(body, start):
            if held is None:
                return lax.fori_loop(0, found, body, start)
            for s in range(held):
                start = body(s, start)
            return start

        def score(s, norms):
            added = []
            for t in range(count):
                product = (queries[start + t] * keys[s]).reshape(groups, head, 8, band)
                weight = jnp.exp(jnp.sum(product, axis=1))
                weights[t, s] = weight
                added.append(norms[t] + weight)
            return tuple(added)

        others = blank if held is None else (counting - held).astype(f32)
        norms = loop(score, (jnp.zeros((groups, 8, band), f32) + others,) * count)
        inverses = [1.0 / norm for norm in norms]
        mixed = [[] for _ in range(count)]
        none = jnp.zeros((head, 8, band), f32)
        for g in range(groups):
            for t in range(0, count, 2):

                both = range(min(2, count - t))

                def mix(s, sums):
                    value = values[s, g * head : (g + 1) * head]
                    probs = [weights[t + k, s, g] * inverses[t + k][g] for k in both]
                    probs = [prob.astype(half).astype(f32) for prob in probs]
                    return tuple(sums[k] + probs[k][None] * value for k in both)

                sums = loop(mix, (none,) * len(both))
                for k in both:
                    mixed[t + k].append(sums[k].reshape(head * 8, band).astype(half))
        mixed = [jnp.concatenate(m, axis=0) for m in mixed]
        if with_blank:

            def gather(s, total):
                return total + values[s]

            prob = jnp.broadcast_to(1.0 / counting.astype(f32), (8, band)).astype(half).astype(f32)
            total = loop(gather, jnp.zeros(tiles, f32))
            mixed.append((total * prob[None]).reshape(rows, band).astype(half))
        hidden = dot(w_mix[...], side_by_side(mixed))
        own = [
            hidden[:, t * band : (t + 1) * band] + tokens[start + t] for t in range(count)
        ] + ([hidden[:, count * band :]] if with_blank else [])
        hidden = side_by_side(own)
        return hidden, finish(hidden)

    def first_tokens(count, held, padding):
        hidden, inner = attend(0, count, True, held)
        rest = blank - padding.astype(f32)
        inner = inner.astype(f32)
        sum_hidden[...] = add_up(hidden, count) + hidden[:, count * band :] * rest
        sum_inner[...] = add_up(inner, count) + inner[:, count * band :] * rest

    for n, count in enumerate(FEW):

        @pl.when((found <= count) & (found > (FEW[n - 1] if n else -1)))
        def _():
            project(0, count, lambda place: seen[0, place])
            first_tokens(count, count, count - found)

    @pl.when(found > FEW[-1])
    def _():
        read = pltpu.make_async_copy(lists, plan, plan_sem)
        read.start()
        read.wait()

        def entry_of(place):
            return plan[0, place]

        project(0, FEW[-1], entry_of)

        def project_more(n, carry):
            project(FEW[-1] + AFTER * n, AFTER, entry_of)
            return carry

        lax.fori_loop(0, steps, project_more, 0)
        first_tokens(FEW[-1], None, FEW[-1] + AFTER * steps - found)

        def attend_more(n, carry):
            hidden, inner = attend(FEW[-1] + AFTER * n, AFTER, False)
            sum_hidden[...] += add_up(hidden, AFTER)
            sum_inner[...] += add_up(inner.astype(f32), AFTER)
            return carry

        lax.fori_loop(0, steps, attend_more, 0)

    inverse = 1.0 / counting.astype(f32)
    lane = iota((chans, band), 1)
    edges = jnp.zeros((chans, band), f32)
    taken = jnp.where(side == 0, 0, band // 2 - 2)
    for x in range(width):
        inner = sum_inner[x * mlp : (x + 1) * mlp, :]
        high = inner.astype(half)
        low = (inner - high.astype(f32)).astype(half)
        back = dot(w_back[...], jnp.concatenate([high, low], axis=1))
        sums = sum_hidden[x * chans : (x + 1) * chans, :] + back[:, :band] + back[:, band:]
        joined = (sums * inverse).astype(half)
        out[x] = joined
        joined = joined.astype(f32)
        for column, start in ((x, 0), (x + width, band // 2)):
            turn = rem(2 * column - start - taken + 2 * band, band)
            edges = jnp.where(div(lane, 2) == column, pltpu.roll(joined, turn, 1), edges)
    strip[...] = edges.astype(half)


def join(parts, plan, arranged, w_back, width):
    part, band = parts.shape[2:]
    chans, mlp = w_back.shape
    lists = plan.reshape(1, -1)
    spaces = (plan.shape[0] - 2) // (2 * width)
    rows = width * chans
    groups = HEADS * width // 8
    arrays = (parts, *arranged[:5], w_back)
    tiles = pltpu.VMEM((spaces, rows // 8, 8, band), f32)
    return pl.pallas_call(
        join_kernel,
        out_shape=[
            jax.ShapeDtypeStruct((width, chans, band), half),
            jax.ShapeDtypeStruct((chans, band), half),
        ],
        in_specs=[pl.BlockSpec(memory_space=VMEM)] * (1 + len(arrays)),
        out_specs=[pl.BlockSpec(memory_space=VMEM)] * 2,
        scratch_shapes=[
            pltpu.SMEM(lists.shape, jnp.int32),
            pltpu.SemaphoreType.DMA,
            pltpu.VMEM((spaces, rows, band), f32),
            tiles,
            tiles,
            tiles,
            pltpu.VMEM((FEW[-1], spaces, groups, 8, band), f32),
            pltpu.VMEM((rows, band), f32),
            pltpu.VMEM((width * mlp, band), f32),
        ],
        compiler_params=pltpu.CompilerParams(vmem_limit_bytes=LIMIT),
        name="join",
    )(lists, *arrays)


def frame_columns(mine, theirs, far, w_first, wide, products):
    width, chans, band = mine.shape
    side = here()[0]
    own = div(iota((chans, band), 1), band // 2) == side

    def put(j, column):
        wide[j * chans : (j + 1) * chans, :] = column

    for j in range(width):
        first, second = mine[j].astype(f32), theirs[j].astype(f32)
        put(2 + j, jnp.where(own, first, pltpu.roll(second, band // 2, 1)).astype(half))

    def near(j):
        first, second = mine[j].astype(f32), theirs[j].astype(f32)
        return jnp.where(own, pltpu.roll(first, band // 2, 1), second).astype(half)

    @pl.when(side == 0)
    def _():
        for j in range(2):
            put(width + 2 + j, near(j))
            put(j, far(j))

    @pl.when(side == 1)
    def _():
        for j in range(2):
            put(j, near(width - 2 + j))
            put(width + 2 + j, far(j))

    for x in range(width + 2):
        products[x] = dot(w_first[...], wide[x * chans : (x + 3) * chans, :])


def frame_pair_kernel(mine, theirs, w_first, products, wide):
    none = jnp.zeros(mine.shape[1:], half)
    frame_columns(mine, theirs, lambda j: none, w_first, wide, products)


def frame_kernel(mine, theirs, w_first, far, products, strip_a, strip_b, wide):
    width, chans, band = mine.shape
    odd = rem(here()[2], 2)
    lane = iota((chans, band), 1)
    frame_columns(mine, theirs, lambda j: far[j], w_first, wide, products)
    low = jnp.zeros((chans, band), f32)
    high = low
    for j in range(width + 4):
        column = wide[j * chans : (j + 1) * chans, :].astype(f32)
        place = div(lane, 2) == j
        low = jnp.where(place, column if j == 0 else pltpu.roll(column, 2 * j, 1), low)
        high = jnp.where(place, pltpu.roll(column, 2 * j + 2, 1), high)
    strip_a[...] = jnp.where(odd == 0, high, low).astype(half)
    strip_b[...] = jnp.where(odd == 0, low, high).astype(half)


def frame(kernel, arrays):
    width, chans, band = arrays[0].shape
    strip = jax.ShapeDtypeStruct((chans, band), half)
    shapes = [jax.ShapeDtypeStruct((width + 2, 3 * chans, band), f32)]
    if kernel is frame_kernel:
        shapes += [strip, strip]
    return pl.pallas_call(
        kernel,
        out_shape=shapes,
        in_specs=[pl.BlockSpec(memory_space=VMEM)] * len(arrays),
        out_specs=[pl.BlockSpec(memory_space=VMEM)] * len(shapes),
        scratch_shapes=[pltpu.VMEM(((width + 4) * chans, band), half)],
        compiler_params=pltpu.CompilerParams(vmem_limit_bytes=LIMIT),
        name="frame",
    )(*arrays)


def decode_kernel(
    single, ncols, nrows, inner, strip_a, strip_b, w_first, w_second, out, wide, act
):
    chans, band = strip_a.shape
    outs, width = out.shape[:2]
    side, pair, index = here()
    odd = rem(index, 2)
    from_a, from_b = strip_a[...].astype(f32), strip_b[...].astype(f32)
    if single:
        turn = jnp.where(side == 0, 4, band + 4 - 2 * width)
        from_a, from_b = pltpu.roll(from_a, turn, 1), pltpu.roll(from_b, turn, 1)
    low_in_a = side == 1 if single else odd == 1
    low = jnp.where(low_in_a, from_a, from_b)
    high = jnp.where(low_in_a, from_b, from_a)
    lane = iota((chans, band), 1)
    for j in range(width + 4):
        after = high if j == 0 else pltpu.roll(high, band - 2 * j, 1)
        before = pltpu.roll(low, band - 2 - 2 * j, 1)
        edge = jnp.where(lane < 2, after, jnp.where(lane >= band - 2, before, 0.0))
        wide[j * chans : (j + 1) * chans, :] = edge.astype(half)

    def shifted(products, count):
        above, level, below = [products[n * count : (n + 1) * count] for n in range(3)]
        return pltpu.roll(above, 1, 1) + level + pltpu.roll(below, 2 * band - 1, 1)

    lane = iota((chans, 2 * band), 1)
    row = index * band + jnp.where(lane < band + band // 2, lane, lane - 2 * band)
    row_inside = (row >= 0) & (row < nrows)
    for x in range(width + 2):
        column = (2 * pair + side) * width + (x - 1)
        outer = dot(w_first[...], wide[x * chans : (x + 3) * chans, :])
        products = jnp.concatenate([inner[x], outer], axis=1)
        hidden = gelu(shifted(products, chans))
        inside = row_inside & (column >= 0) & (column < ncols)
        act[x * chans : (x + 1) * chans, :] = jnp.where(inside, hidden, 0.0).astype(half)
    for x in range(width):
        products = dot(w_second[...], act[x * chans : (x + 3) * chans, :])
        out[:, x, :] = shifted(products, products.shape[0] // 3)[:outs, :band]


def decode(single, arrays, outs, ncols, nrows):
    width = arrays[0].shape[0] - 2
    chans, band = arrays[1].shape
    out = pl.pallas_call(
        functools.partial(decode_kernel, single, ncols, nrows),
        out_shape=jax.ShapeDtypeStruct((outs, width, band), f32),
        in_specs=[pl.BlockSpec(memory_space=VMEM)] * len(arrays),
        out_specs=pl.BlockSpec(memory_space=VMEM),
        scratch_shapes=[
            pltpu.VMEM(((width + 4) * chans, band), half),
            pltpu.VMEM(((width + 2) * chans, 2 * band), half),
        ],
        compiler_params=pltpu.CompilerParams(vmem_limit_bytes=LIMIT),
        name="decode",
    )(*arrays)
    return jnp.transpose(out, (1, 0, 2))


def swap(values, axis, first):
    count = lax.axis_size(axis)
    pairs = [(i, i + 1) for i in range(first, count - 1, 2)]
    if not pairs:
        return jnp.zeros_like(values)
    return lax.ppermute(values, axis, pairs + [(b, a) for a, b in pairs])


def all_moves(moves):
    count = lax.axis_size("pass")
    me = lax.axis_index("pass")
    pieces = [moves]
    for step in range(1, count):
        pieces.append(lax.ppermute(moves, "pass", [(i, (i - step) % count) for i in range(count)]))
    start = rem(count - me, count) * moves.shape[1]
    return lax.dynamic_slice_in_dim(
        jnp.concatenate(pieces * 2, axis=1), start, count * moves.shape[1], 1
    )


def to_band(strip, other):
    tiles, passes, cores = [lax.axis_size(a) for a in ("tile", "pass", "row")]

    def index(band, side):
        return (band // cores) * passes * cores + side * cores + band % cores

    bands = tiles * cores
    pairs = [(index(b, 0), index(b - 1, other)) for b in range(1, bands)]
    pairs += [(index(b, 1), index(b + 1, 1 - other)) for b in range(bands - 1)]
    return lax.ppermute(strip, ("tile", "pass", "row"), pairs)


def local(revisits, shifts, flags, *weights):
    params, (conv_first, conv_second) = weights[:10], weights[10:]
    passes = lax.axis_size("pass")
    bands = lax.axis_size(("tile", "row"))
    count, per_device, chans, nrows = revisits.shape
    assert per_device == 1 and passes % 2 == 0 and count <= 32
    ncols = bands
    width = ncols // passes
    band = nrows // bands
    slots = min(SLOTS, count)
    first, moves = pack(revisits, shifts.T, passes, bands, ncols, slots)
    first = send(first)
    every = all_moves(moves)
    arranged = arrange(params, conv_first, conv_second, width, band)
    plan, needed = make_plan(every, flags.T, passes, ncols)
    needed = needed[0]

    outs = conv_second.shape[3]
    w_first, w_second = arranged[5:7]

    def finish(parts):
        joined, strip = join(parts, plan, arranged, params[9].T, width)
        side = rem(lax.axis_index("pass"), 2)
        theirs = swap(joined, "pass", 0)
        if passes == 2:
            strip_a, strip_b = to_band(strip, 0), to_band(strip, 1)
            (products,) = frame(frame_pair_kernel, (joined, theirs, w_first))
        else:
            first = jnp.where(side == 0, joined[:2], joined[-2:]).astype(f32)
            second = jnp.where(side == 0, theirs[:2], theirs[-2:]).astype(f32)
            own = div(jnp.arange(band, dtype=jnp.int32), band // 2) == side
            edge = jnp.where(own, first, jnp.roll(second, band // 2, -1)).astype(half)
            far = swap(edge, "pass", 1)
            products, strip_a, strip_b = frame(frame_kernel, (joined, theirs, w_first, far))
            strip_a, strip_b = swap(strip_a, ("tile", "row"), 0), swap(strip_b, ("tile", "row"), 1)
        arrays = (products, strip_a, strip_b, w_first, w_second)
        return decode(passes == 2, arrays, outs, ncols, nrows)

    if count <= slots:
        return finish(first)

    def more():
        held = jnp.zeros((first.shape[0], count) + first.shape[2:], half)
        held = lax.dynamic_update_slice_in_dim(held, first, 0, 1)

        def step(i, held):
            sent = send(pack(revisits, moves, passes, bands, ncols, 1, i)[0])
            return lax.dynamic_update_slice_in_dim(held, sent, i, 1)

        return finish(lax.fori_loop(slots, needed, step, held))

    return lax.cond(needed > slots, more, lambda: finish(first))


def solution(mesh):
    return jax.shard_map(
        local,
        mesh=mesh,
        in_specs=(
            P(("groups", "pass"), ("tile", "row"), None, None),
            P(("groups", "pass"), None),
            P("groups", ("tile", "row")),
        )
        + (P(),) * 12,
        out_specs=P(("groups", "pass"), None, ("tile", "row")),
        check_vma=False,
    )
```
